256 devices in a mesh: ctx: 128 (over z, y_lo, x, core), dp: 2 (over y_hi).
Axes of the slice: x: 4, y: 4 (y_hi: 2, y_lo: 2; y = y_hi * 2 + y_lo), z: 8, core: 2. Of those that a mesh axis runs over, the one named last changes fastest.
Arguments:
- hidden_in: bfloat16 [65536, 8192], P(('dp', 'ctx')), parts along dimension 0, may hold values from -32 to 32
- segment_ids: int32 [65536], P('dp'), parts along dimension 0, may hold values from 1023 to 32767, as said below
- w_query: bfloat16 [8192, 512], P('ctx'), may hold values from -0.0625 to 0.0625
- w_key: bfloat16 [8192, 128], P('ctx'), may hold values from -0.0625 to 0.0625
- w_value: bfloat16 [8192, 128], P('ctx'), may hold values from -0.0625 to 0.0625
- w_out: bfloat16 [512, 8192], P(None, 'ctx'), may hold values from -0.25 to 0.25
Outputs:
- attended: bfloat16 [65536, 8192], P(('dp', 'ctx')), parts along dimension 0
The draws below stay inside these ranges and needn't reach their ends.
There are 2 independent parts, one for each index of `dp`. The reference program is written for one: setup_inputs(seed, part) draws one part's arguments, and reference() takes and returns one part's arrays. A program takes and returns all parts, laid end to end along the dimension named above; an argument that names none is the same for every part. Nothing has to cross between parts.
Inputs may be any that keep to these rules, and one draw needn't show every extreme that they name: `segment_ids`: A token's id is the position in sequence order of the last token of its document, so ids never fall along the sequence and tokens share an id exactly when they share a document; every document holds 1 to 1024 tokens, and the first one exactly 1024. Stored in the same block order as hidden_in.
All inputs are finite; a program needn't handle non-finite values.
Results may differ from the reference program's by a relative error of at most 0.034.
Values may be sent and summed in bfloat16 or wider, within the bound.
A program may use at most 128 MiB of HBM per device.

```python
import math
import jax
import jax.numpy as jnp
from jax import lax

D = 8192
HD = 128
HQ = 4
REACH = 8
BLOCK = 128
TOKENS = 32768
N_CTX = 128


def draw_hidden_in(key, part):
    key = jax.random.fold_in(key, 5)
    first_key = jax.random.fold_in(key, 0)
    drawn = jnp.clip(jax.random.normal(first_key, (TOKENS, D), jnp.float32), -6.0, 6.0)
    return drawn.astype(jnp.bfloat16)


def draw_segment_ids(key, part):
    key = jax.random.fold_in(key, 9)
    first_key = jax.random.fold_in(key, 0)
    longest = REACH * BLOCK
    lengths = jax.random.randint(first_key, (TOKENS,), 1, longest + 1, dtype=jnp.int32)
    lengths = jnp.where(jnp.arange(TOKENS, dtype=jnp.int32) == 0, longest, lengths)
    bounds = jnp.cumsum(lengths).astype(jnp.int32)
    doc_index = jnp.searchsorted(bounds, jnp.arange(TOKENS, dtype=jnp.int32), side='right').astype(jnp.int32)
    last_pos = jnp.minimum(bounds[doc_index] - 1, TOKENS - 1).astype(jnp.int32)
    stored = jnp.arange(2 * N_CTX, dtype=jnp.int32)
    sequence_of = jnp.where(stored % 2 == 0, stored // 2, 2 * N_CTX - 1 - stored // 2)
    return last_pos.reshape(2 * N_CTX, BLOCK)[sequence_of].reshape(TOKENS).astype(jnp.int32)


def shard_levels(rng, extent, shards, least, high):
    loudness = 1.0
    for dim, blocks in shards:
        heights = jax.random.uniform(jax.random.fold_in(jax.random.fold_in(rng, 6), dim), (blocks,), jnp.float32, least / len(shards), high / len(shards))
        loudness = loudness * jnp.repeat(jnp.exp(heights), extent[dim] // blocks).reshape((-1,) + (1,) * (len(extent) - 1 - dim))
    return loudness


def gaussian(own_key, dims, scale, bound, pieces=(), kind=jnp.bfloat16):
    level = shard_levels(own_key, dims, pieces, -0.22, 0.18) if pieces else 1.0
    values = jax.random.normal(own_key, dims, jnp.float32) * scale * level
    return jnp.minimum(jnp.maximum(values, -bound), bound).astype(kind)


def setup_inputs(seed: int = 0, part: int = 0) -> dict:
    arg_keys = jax.random.split(jax.random.key(seed), 7)
    own_keys = jax.random.split(jax.random.fold_in(arg_keys[6], part), 7)
    return {
        "hidden_in": draw_hidden_in(jax.random.fold_in(jax.random.fold_in(arg_keys[6], part), 71), part),
        "segment_ids": draw_segment_ids(jax.random.fold_in(jax.random.fold_in(arg_keys[6], part), 71), part),
        "w_query": gaussian(arg_keys[2], (D, HQ * HD), D ** -0.5, 0.0625, ((0, 128),)),
        "w_key": gaussian(arg_keys[3], (D, HD), D ** -0.5, 0.0625, ((0, 128),)),
        "w_value": gaussian(arg_keys[4], (D, HD), D ** -0.5, 0.0625, ((0, 128),)),
        "w_out": gaussian(arg_keys[5], (HQ * HD, D), (HQ * HD) ** -0.5, 0.25, ((1, 128),)),
    }


ROPE_BASE = 500000.0

def rotate(rows_in, positions):
    half_dim = rows_in.shape[-1] // 2
    frequency = ROPE_BASE ** (-(jnp.arange(half_dim, dtype=jnp.float32) * 2.0) / rows_in.shape[-1])
    angles = positions.astype(jnp.float32)[:, None] * frequency[None, :]
    cosine = jnp.cos(angles)[:, None, :]
    sine_part = jnp.sin(angles)[:, None, :]
    front_part = rows_in[..., :half_dim]
    back_part = rows_in[..., half_dim:]
    return jnp.concatenate([front_part * cosine - back_part * sine_part, back_part * cosine + front_part * sine_part], axis=-1)

def block_order():
    seq_blocks = jnp.arange(2 * N_CTX, dtype=jnp.int32)
    storage_of = jnp.where(seq_blocks < N_CTX, 2 * seq_blocks, 2 * (2 * N_CTX - 1 - seq_blocks) + 1)
    stored = jnp.arange(2 * N_CTX, dtype=jnp.int32)
    sequence_of = jnp.where(stored % 2 == 0, stored // 2, 2 * N_CTX - 1 - stored // 2)
    return (storage_of, sequence_of)

def reference(hidden_in, segment_ids, w_query, w_key, w_value, w_out):
    storage_of, sequence_of = block_order()
    tokens_seq = hidden_in.reshape(2 * N_CTX, BLOCK, D)[storage_of].reshape(TOKENS, D)
    seg_seq = segment_ids.reshape(2 * N_CTX, BLOCK)[storage_of].reshape(TOKENS)
    positions = jnp.arange(TOKENS, dtype=jnp.int32)
    query_sum = jnp.dot(tokens_seq, w_query, preferred_element_type=jnp.float32)
    queries = rotate(query_sum.reshape(TOKENS, HQ, HD), positions).astype(jnp.bfloat16)
    key_sum = jnp.dot(tokens_seq, w_key, preferred_element_type=jnp.float32)
    key_rows = rotate(key_sum.reshape(TOKENS, 1, HD), positions).reshape(TOKENS, HD).astype(jnp.bfloat16)
    value_rows = jnp.dot(tokens_seq, w_value, preferred_element_type=jnp.float32).astype(jnp.bfloat16)
    margin = REACH * BLOCK
    key_padded = jnp.concatenate([jnp.zeros((margin, HD), jnp.bfloat16), key_rows], axis=0)
    value_padded = jnp.concatenate([jnp.zeros((margin, HD), jnp.bfloat16), value_rows], axis=0)
    seg_padded = jnp.concatenate([jnp.full((margin,), -1, jnp.int32), seg_seq], axis=0)
    span_len = (REACH + 1) * BLOCK

    def one_block(block_id):
        begin = (block_id * BLOCK).astype(jnp.int32)
        query_part = lax.dynamic_slice_in_dim(queries, begin, BLOCK, 0).astype(jnp.float32)
        key_part = lax.dynamic_slice_in_dim(key_padded, begin, span_len, 0).astype(jnp.float32)
        value_part = lax.dynamic_slice_in_dim(value_padded, begin, span_len, 0).astype(jnp.float32)
        key_seg = lax.dynamic_slice_in_dim(seg_padded, begin, span_len, 0)
        query_seg = lax.dynamic_slice_in_dim(seg_seq, begin, BLOCK, 0)
        query_pos = begin + jnp.arange(BLOCK, dtype=jnp.int32)
        key_pos = begin - margin + jnp.arange(span_len, dtype=jnp.int32)
        scores = jnp.einsum('qhd,kd->hqk', query_part, key_part) / math.sqrt(HD)
        allowed = (query_seg[:, None] == key_seg[None, :]) & (key_pos[None, :] <= query_pos[:, None])
        scores = jnp.where(allowed[None], scores, -1e+30)
        row_peak = lax.optimization_barrier(jnp.max(scores, axis=-1, keepdims=True))
        exp_terms = jnp.exp(scores - row_peak)
        weights = (exp_terms / lax.optimization_barrier(jnp.sum(exp_terms, axis=-1, keepdims=True))).astype(jnp.bfloat16)
        mixed_part = jnp.einsum('hqk,kd->qhd', weights.astype(jnp.float32), value_part)
        return mixed_part.reshape(BLOCK, HQ * HD).astype(jnp.bfloat16)
    mixed_rows = lax.map(one_block, jnp.arange(2 * N_CTX, dtype=jnp.int32)).reshape(TOKENS, HQ * HD)
    attended_seq = jnp.dot(mixed_rows, w_out, preferred_element_type=jnp.float32).astype(jnp.bfloat16)
    return attended_seq.reshape(2 * N_CTX, BLOCK, D)[sequence_of].reshape(TOKENS, D)
```

```python
import functools
import math

import jax
import jax.numpy as jnp
import numpy as np
from jax import lax
from jax.experimental import pallas as pl
from jax.experimental.pallas import tpu as pltpu
from jax.sharding import PartitionSpec as P

MESH = pl.DeviceIdType.MESH
REACH = 8
ROPE_BASE = 500000.0
NZ, NY, NX = 8, 2, 4
CHIPS = NZ * NY * NX
BLOCK = 128
HD = 128
HQ = 4
D = 8192
QW = HQ * HD
QKV = QW + 2 * HD
SHARD = 64
ORDER = (0, 1, -1, 2, -2, 3, -3, 4)
FAR = -1e30
W_ROWS = ((0, 384), (384, 128))


class Gather:
    def __init__(self, place, ssem, rsem, sib_s, sib_r, slot, plane):
        self.place, self.ssem, self.rsem = place, ssem, rsem
        self.sib_s, self.sib_r = sib_s, sib_r
        self.slot, self.plane = slot, plane
        self.keys = ({}, {})
        self.sent = ([], [])

    def sem(self, core, key):
        table = self.keys[core]
        return table.setdefault(key, len(table))

    def send(self, core, where, key, move):
        index = self.sem(core, key)

        def make():
            ref = self.slot(core, *where)
            return pltpu.make_async_remote_copy(
                src_ref=ref, dst_ref=ref, send_sem=self.ssem.at[index], recv_sem=self.rsem.at[index],
                device_id=self.place.at(*move), device_id_type=MESH)

        make().start()
        self.sent[core].append(make)

    def recv(self, core, where, key):
        index = self.sem(core, key)
        ref = self.slot(core, *where)
        pltpu.make_async_remote_copy(
            src_ref=ref, dst_ref=ref, send_sem=self.ssem.at[index], recv_sem=self.rsem.at[index],
            device_id=self.place.sibling(), device_id_type=MESH).wait_recv()

    def sib_copy(self, core, zr):
        ref = self.plane(core, zr)
        index = (zr + NZ) % NZ
        return pltpu.make_async_remote_copy(
            src_ref=ref, dst_ref=ref, send_sem=self.sib_s.at[index], recv_sem=self.sib_r.at[index],
            device_id=self.place.sibling(), device_id_type=MESH)

    def sib(self, core, *planes):
        for zr in planes:
            self.sib_copy(core, zr).start()

    def drain(self, core):
        for make in self.sent[core]:
            make().wait_send()
        for zr in ORDER:
            self.sib_copy(core, zr).wait_send()

    def a_start(self):
        for step in (1, -1, 2):
            self.send(0, (0, 0, 0, None), ("X", step), (0, 0, step))

    def a_stream(self, j):
        xr = (0, -1, 1, 2)[j]
        if j:
            self.recv(0, (0, 0, xr, None), ("X", -xr if j < 3 else 2))
        for way in (1, -1):
            self.send(0, (0, 0, xr, None), ("Z", j, way, 1), (way, 0, 0))

    def a_y(self, *planes):
        for zr in planes:
            for way in (1, -1):
                self.send(0, (zr, 0, None, (1 - way) // 2), ("Y", zr, way), (0, way, 0))

    def a_step(self, s):
        for j in range(4):
            xr = (0, -1, 1, 2)[j]
            for way in (1, -1):
                half = (1 - way) // 2
                if s < 4:
                    self.recv(0, (-way * s, 0, xr, None), ("Z", j, way, s))
                    onward = half if s == 3 else None
                    self.send(0, (-way * s, 0, xr, onward), ("Z", j, way, s + 1), (way, 0, 0))
                else:
                    self.recv(0, (4, 0, xr, half), ("Z", j, way, 4))
        self.a_y(*((4,) if s == 4 else (-s, s)))

    def a_done(self, *planes):
        for zr in planes:
            for way in (1, -1):
                self.recv(0, (zr, 1, None, (1 - way) // 2), ("Y", zr, way))
        self.sib(0, *planes)

    def b_x(self, zr, yr):
        for way in (1, -1):
            self.send(1, (zr, yr, 0, None), ("X", zr, yr, way), (0, 0, way))

    def b_y(self, zr):
        for way in (1, -1):
            self.send(1, (zr, 0, 0, (1 - way) // 2), ("Y", zr, way), (0, way, 0))

    def b_start_z(self):
        for far in (1, 2, 3):
            for way in (1, -1):
                self.send(1, (0, 0, 0, None), ("Z", way, far), (way * far, 0, 0))

    def b_z(self, *planes, x=True):
        for zr in planes:
            if zr == 4:
                for way in (1, -1):
                    self.recv(1, (4, 0, 0, (1 - way) // 2), ("Z", way, 4))
            else:
                way = -1 if zr > 0 else 1
                self.recv(1, (zr, 0, 0, None), ("Z", way, abs(zr)))
                if abs(zr) == 3:
                    self.send(1, (zr, 0, 0, (1 - way) // 2), ("Z", way, 4), (way, 0, 0))
            if x:
                self.b_x(zr, 0)
            self.b_y(zr)

    def b_ywait(self, *planes, x=True):
        for zr in planes:
            for way in (1, -1):
                self.recv(1, (zr, 1, 0, (1 - way) // 2), ("Y", zr, way))
            if x:
                self.b_x(zr, 1)

    def b_relay(self, yr, *planes):
        for zr in planes:
            for way in (1, -1):
                self.recv(1, (zr, yr, -way, None), ("X", zr, yr, way))
                self.send(1, (zr, yr, -way, (1 - way) // 2), ("XR", zr, yr, way), (0, 0, way))

    def b_done(self, *planes):
        for zr in planes:
            for yr in (0, 1):
                for way in (1, -1):
                    self.recv(1, (zr, yr, 2, (1 - way) // 2), ("XR", zr, yr, way))
        self.sib(1, *planes)


class Place:
    def __init__(self):
        ctx, dp = lax.axis_index("ctx"), lax.axis_index("dp")
        self.ctx, self.dp = ctx, dp
        self.c = ctx % 2
        self.k = ctx // 2
        self.x = self.k % NX
        self.yl = (self.k // NX) % NY
        self.z = self.k // (NX * NY)
        self.y = dp * 2 + self.yl

    def zi(self, zr):
        return (self.z + (zr + NZ)) % NZ

    def yi(self, yr):
        return (self.yl + yr) % NY

    def xi(self, xr):
        return (self.x + (xr + NX)) % NX

    def at(self, dz, dy, dx):
        y = (self.y + (dy + 4)) % 4
        chip = (self.zi(dz) * NY + y % 2) * NX + self.xi(dx)
        return {"ctx": chip * 2 + self.c, "dp": y // 2}

    def sibling(self):
        return {"ctx": self.k * 2 + (1 - self.c), "dp": self.dp}

    def on(self, chip, core):
        return {"ctx": chip * 2 + core, "dp": self.dp}


def kernel(hid_hbm, seg_hbm, wq_hbm, wk_hbm, wv_hbm, wo_hbm, freq_ref, out_hbm,
           hid, seg, qbuf, wbuf, wo_in, wo_sib, acc, cos_t, sin_t, bias, qrot, kvw, mixed, outv,
           load_sem, out_sem, wo_s, wo_r, q_s, q_r, qs_s, qs_r, w_s, w_r, ws_s, ws_r,
           kv_s, kv_r, kvs_s, kvs_r):
    me = Place()
    c, k, i = me.c, me.k, me.ctx

    def q_slot(core, zr, yr, xr, half):
        rows = pl.ds(0, SHARD) if half is None else pl.ds(half * 32, 32)
        x = slice(None) if xr is None else me.xi(xr)
        return qbuf.at[me.zi(zr), me.yi(yr), x, core, rows, :]

    def q_plane(core, zr):
        return qbuf.at[me.zi(zr), :, :, core]

    def w_slot(core, zr, yr, xr, half):
        first, count = W_ROWS[core]
        rows = pl.ds(first, count) if half is None else pl.ds(first + half * (count // 2), count // 2)
        x = slice(None) if xr is None else me.xi(xr)
        return wbuf.at[me.zi(zr), me.yi(yr), x, rows, :]

    def w_plane(core, zr):
        return wbuf.at[me.zi(zr), :, :, pl.ds(*W_ROWS[core]), :]

    gq = Gather(me, q_s, q_r, qs_s, qs_r, q_slot, q_plane)
    gw = Gather(me, w_s, w_r, ws_s, ws_r, w_slot, w_plane)

    def both(first, second):
        pl.when(c == 0)(first)
        pl.when(c == 1)(second)

    own = qbuf.at[me.z, me.yl, me.x, c]
    loads = [
        pltpu.make_async_copy(wq_hbm, own.at[:, pl.ds(0, QW)], load_sem.at[0]),
        pltpu.make_async_copy(wk_hbm, own.at[:, pl.ds(QW, HD)], load_sem.at[1]),
        pltpu.make_async_copy(wv_hbm, own.at[:, pl.ds(QW + HD, HD)], load_sem.at[2]),
        pltpu.make_async_copy(wo_hbm, wo_in, load_sem.at[3]),
        pltpu.make_async_copy(seg_hbm, seg, load_sem.at[4]),
        pltpu.make_async_copy(hid_hbm, hid, load_sem.at[5]),
    ]
    for load in loads:
        load.start()

    kvw[0, 0:REACH] = jnp.zeros((REACH, BLOCK, 2 * HD), jnp.bfloat16)

    def up(m):
        over = k + m >= CHIPS
        return (jnp.where(over, 2 * CHIPS - 1 - k - m, k + m), jnp.where(over, 1 - c, c))

    barrier = pltpu.get_barrier_semaphore()

    def greet(device):
        pl.semaphore_signal(barrier, inc=1, device_id=device, device_id_type=MESH)

    moves = [(0, 0, 1), (0, 0, -1), (0, 0, 2), (0, 1, 0), (0, -1, 0)]
    moves += [(way * far, 0, 0) for far in (1, 2, 3) for way in (1, -1)]
    for move in moves:
        greet(me.at(*move))
    greet(me.sibling())
    for m in range(1, 5):
        greet(me.on(*up(m)))
        pl.when(k >= m)(lambda m=m: greet(me.on(k - m, c)))
    pl.semaphore_wait(barrier, len(moves) + 5 + jnp.minimum(k, 4))

    for load in loads[:3]:
        load.wait()

    def b_begin():
        gq.b_x(0, 0)
        gq.b_start_z()
        gq.b_y(0)

    def a_begin():
        gq.a_start()
        gq.a_stream(0)

    both(a_begin, b_begin)

    loads[3].wait()
    wo_copy = pltpu.make_async_remote_copy(
        src_ref=wo_in, dst_ref=wo_sib, send_sem=wo_s, recv_sem=wo_r,
        device_id=me.sibling(), device_id_type=MESH)
    wo_copy.start()

    row = lax.broadcasted_iota(jnp.int32, (BLOCK, HD), 0)
    lane = lax.broadcasted_iota(jnp.int32, (BLOCK, HD), 1)
    late = 2 * 2 * CHIPS - 1 - i
    for b, block in enumerate((i, late)):
        angle = (block * BLOCK + row).astype(jnp.float32) * freq_ref[...]
        cos_t[b] = jnp.cos(angle)
        sine = jnp.sin(angle)
        sin_t[b] = jnp.where(lane < HD // 2, -sine, sine)

    wo_copy.wait()

    def join(core):
        rows = pl.ds(*W_ROWS[core])
        pair = [wo_in[rows, :], wo_sib[rows, :]]
        wbuf[me.z, me.yl, me.x, rows, :] = jnp.concatenate(pair if core == 0 else pair[::-1], axis=1)

    def a1():
        for j in (1, 2, 3):
            gq.a_stream(j)
        gq.a_y(0)
        join(0)
        gw.a_start()

    def b1():
        gq.b_z(1, -1)
        gq.b_ywait(0)
        join(1)

    both(a1, b1)

    loads[4].wait()
    for b in range(2):
        mine = seg[pl.ds(2 * i + b, 1), :]
        asks = jnp.transpose(jnp.broadcast_to(mine, (BLOCK, BLOCK)))
        for j in range(REACH + 1):
            if b == 0:
                block = i - REACH + j
                keys = seg[pl.ds(2 * jnp.maximum(block, 0), 1), :]
                keys = jnp.where(block >= 0, keys, -1)
            else:
                over = i + j >= 2 * CHIPS
                keys = seg[pl.ds(jnp.where(over, 2 * (4 * CHIPS - 1 - i - j), 2 * (i + j) + 1), 1), :]
            allowed = asks == keys
            if j == (REACH if b == 0 else 0):
                allowed = allowed & (lane <= row)
            bias[b, :, j * BLOCK:(j + 1) * BLOCK] = jnp.where(allowed, 0.0, FAR)

    def a2():
        gq.a_step(1)

    def b2():
        gq.b_z(2, -2)
        gq.b_ywait(1, -1)
        gq.b_relay(0, 0)

    both(a2, b2)

    def a3():
        gq.a_step(2)
        gq.a_done(0)

    def b3():
        gq.b_z(3, -3)
        gq.b_ywait(2, -2)
        gq.b_relay(1, 0)
        gq.b_relay(0, 1, -1)

    both(a3, b3)

    def a4():
        gq.a_step(3)
        gq.a_done(1, -1)

    def b4():
        gq.b_z(4)
        gq.b_ywait(3, -3)
        gq.b_relay(1, 1, -1)
        gq.b_relay(0, 2, -2)
        gq.b_ywait(4)
        gq.b_done(0)
        gw.b_start_z()
        gw.b_y(0)

    both(a4, b4)
    loads[5].wait()
    acc[...] = jnp.zeros_like(acc)

    def project(first, last):
        @pl.loop(first, last)
        def _(t):
            zr = ((t + 1) // 2) * (2 * (t % 2) - 1)
            zz = (me.z + zr + NZ) % NZ
            ref = qbuf.at[zz, :, :, 1 - c]
            index = (zr + NZ) % NZ
            pltpu.make_async_remote_copy(
                src_ref=ref, dst_ref=ref, send_sem=qs_s.at[index], recv_sem=qs_r.at[index],
                device_id=me.sibling(), device_id_type=MESH).wait_recv()
            part = NY * NX * 2 * SHARD
            weights = qbuf[zz].reshape(part, QKV)
            acc[...] += jnp.dot(hid[:, pl.ds(pl.multiple_of(zz * part, part), part)], weights,
                                preferred_element_type=jnp.float32)

    def a5():
        gq.a_step(4)
        for j in range(4):
            gw.a_stream(j)
        gw.a_y(0)
        gq.a_done(2, -2)

    def b5():
        gq.b_relay(1, 2, -2)
        gq.b_relay(0, 3, -3)
        gq.b_done(1, -1)
        gw.b_z(1, -1, x=False)

    both(a5, b5)
    project(0, 3)

    def a6():
        gq.a_done(3, -3, 4)
        gw.a_step(1)

    def b6():
        gq.b_relay(1, 3, -3)
        gq.b_relay(0, 4)
        gq.b_relay(1, 4)
        gq.b_done(2, -2, 3, -3, 4)

    both(a6, b6)
    project(3, 8)

    for b in range(2):
        rows = slice(b * BLOCK, (b + 1) * BLOCK)
        slot = REACH + c if b == 0 else c
        for h in range(HQ + 1):
            part = acc[rows, h * HD:(h + 1) * HD]
            turned = part * cos_t[b] + pltpu.roll(part, HD // 2, 1) * sin_t[b]
            turned = turned.astype(jnp.bfloat16)
            if h < HQ:
                qrot[b, h] = turned
            else:
                kvw[b, slot, :, 0:HD] = turned
        kvw[b, slot, :, HD:2 * HD] = acc[rows, QW + HD:QKV].astype(jnp.bfloat16)

    def kv_copy(src, dst, sent, got, device):
        return pltpu.make_async_remote_copy(
            src_ref=src, dst_ref=dst, send_sem=sent, recv_sem=got, device_id=device, device_id_type=MESH)

    early_own, late_own = kvw.at[0, REACH + c], kvw.at[1, c]

    def kv_up(m):
        return kv_copy(early_own, kvw.at[0, REACH - 2 * m + c], kv_s.at[0, m], kv_r.at[0, m], me.on(k + m, c))

    def kv_over(m):
        return kv_copy(early_own, kvw.at[1, 2 * m + 1 - c], kv_s.at[0, m], kv_r.at[1, m],
                       me.on(2 * CHIPS - 1 - k - m, 1 - c))

    def kv_down(m):
        return kv_copy(late_own, kvw.at[1, 2 * m + c], kv_s.at[1, m], kv_r.at[1, m], me.on(k - m, c))

    def kv_side(b, m, core):
        ref = kvw.at[0, REACH - 2 * m + core] if b == 0 else kvw.at[1, 2 * m + core]
        return kv_copy(ref, ref, kvs_s.at[b, m], kvs_r.at[b, m], me.sibling())

    for m in range(4, 0, -1):
        pl.when(k + m < CHIPS)(lambda m=m: kv_up(m).start())
        pl.when(k + m >= CHIPS)(lambda m=m: kv_over(m).start())
        pl.when(k >= m)(lambda m=m: kv_down(m).start())
    for b in range(2):
        kv_side(b, 0, c).start()

    def a7():
        gw.a_step(2)
        gw.a_done(0)

    def b7():
        for zr in (0, 1, -1):
            gw.b_x(zr, 0)
        gw.b_ywait(0, 1, -1)
        gw.b_z(2, -2)
        gw.b_ywait(2, -2)
        gw.b_z(3, -3)
        gw.b_ywait(3, -3)

    both(a7, b7)

    for m in range(1, 5):
        def early_in(m=m):
            kv_copy(early_own, kvw.at[0, REACH - 2 * m + c], kv_s.at[0, m], kv_r.at[0, m], me.sibling()).wait_recv()
            kv_side(0, m, c).start()

        pl.when(k >= m)(early_in)
        kv_copy(late_own, kvw.at[1, 2 * m + c], kv_s.at[1, m], kv_r.at[1, m], me.sibling()).wait_recv()
        kv_side(1, m, c).start()

    def a8():
        gw.a_step(3)
        gw.a_done(1, -1)

    def b8():
        gw.b_z(4)
        gw.b_ywait(4)
        gw.b_relay(0, 0, 1, -1, 2, -2)
        gw.b_relay(1, 0, 1, -1, 2, -2)

    both(a8, b8)

    def attend(b):
        window = kvw.at[b, pl.ds(c, REACH + 1)]
        span = (REACH + 1) * BLOCK
        keys = window[:, :, 0:HD].reshape(span, HD)
        values = window[:, :, HD:2 * HD].reshape(span, HD)
        scale = math.log2(math.e) / math.sqrt(HD)
        scores = lax.dot_general(qrot[b].reshape(HQ * BLOCK, HD), keys, (((1,), (1,)), ((), ())),
                                 preferred_element_type=jnp.float32)
        scores = scores.reshape(HQ, BLOCK, span) * scale + bias[b][None]
        scores = scores.reshape(HQ * BLOCK, span)
        peak = jnp.max(scores, axis=1, keepdims=True)
        terms = jnp.exp2(scores - peak)
        total = jnp.sum(terms, axis=1, keepdims=True)
        weights = (terms * (1.0 / total)).astype(jnp.bfloat16)
        result = jnp.dot(weights, values, preferred_element_type=jnp.float32).astype(jnp.bfloat16)
        for h in range(HQ):
            mixed[b * BLOCK:(b + 1) * BLOCK, h * HD:(h + 1) * HD] = result[h * BLOCK:(h + 1) * BLOCK]

    for m in range(0, 5):
        pl.when(k >= m)(lambda m=m: kv_side(0, m, 1 - c).wait_recv())
        kv_side(1, m, 1 - c).wait_recv()
    attend(0)

    def a9():
        gw.a_step(4)
        gw.a_done(2, -2)

    def b9():
        gw.b_relay(0, 3, -3, 4)
        gw.b_relay(1, 3, -3, 4)
        gw.b_done(0, 1, -1, 2, -2)

    both(a9, b9)
    attend(1)

    def a10():
        gw.a_done(3, -3, 4)

    def b10():
        gw.b_done(3, -3, 4)

    both(a10, b10)

    part = NY * NX * BLOCK

    def out_copy(t):
        zr = ((t + 1) // 2) * (2 * (t % 2) - 1)
        zz = (me.z + zr + NZ) % NZ
        columns = pl.ds(pl.multiple_of(zz * part, part), part)
        return pltpu.make_async_copy(outv.at[:, columns], out_hbm.at[:, columns], out_sem.at[t])

    @pl.loop(0, NZ)
    def _(t):
        zr = ((t + 1) // 2) * (2 * (t % 2) - 1)
        zz = (me.z + zr + NZ) % NZ
        index = (zr + NZ) % NZ

        def wait(core):
            ref = wbuf.at[zz, :, :, pl.ds(*W_ROWS[core]), :]
            pltpu.make_async_remote_copy(
                src_ref=ref, dst_ref=ref, send_sem=ws_s.at[index], recv_sem=ws_r.at[index],
                device_id=me.sibling(), device_id_type=MESH).wait_recv()

        both(lambda: wait(1), lambda: wait(0))
        for pair in range(NY * NX // 2):
            y, x = pair // 2, (pair % 2) * 2
            weights = jnp.concatenate([wbuf[zz, y, x], wbuf[zz, y, x + 1]], axis=1)
            result = jnp.dot(mixed[...], weights, preferred_element_type=jnp.float32)
            start = pl.multiple_of(zz * part + pair * 2 * BLOCK, 2 * BLOCK)
            outv[:, pl.ds(start, 2 * BLOCK)] = result.astype(jnp.bfloat16)
        out_copy(t).start()

    def finish(core):
        gq.drain(core)
        gw.drain(core)

    both(lambda: finish(0), lambda: finish(1))
    for m in range(1, 5):
        kv_copy(early_own, early_own, kv_s.at[0, m], kv_r.at[0, m], me.sibling()).wait_send()
        pl.when(k >= m)(lambda m=m: kv_down(m).wait_send())
    for m in range(0, 5):
        pl.when(k >= m)(lambda m=m: kv_side(0, m, c).wait_send())
        kv_side(1, m, c).wait_send()

    @pl.loop(0, NZ)
    def _(t):
        out_copy(t).wait()


def on_device(hidden_in, segment_ids, w_query, w_key, w_value, w_out):
    half = np.arange(HD // 2, dtype=np.float32) * np.float32(2.0) / np.float32(HD)
    freq = np.power(np.float32(ROPE_BASE), -half).astype(np.float32)
    freq = jnp.asarray(np.concatenate([freq, freq])[None, :])
    seg = segment_ids.reshape(4 * CHIPS, BLOCK)
    rows = hidden_in.shape[0]
    anywhere = pl.BlockSpec(memory_space=pl.ANY)
    dma = pltpu.SemaphoreType.DMA
    bf16, f32 = jnp.bfloat16, jnp.float32
    return pl.pallas_call(
        kernel,
        out_shape=jax.ShapeDtypeStruct((rows, D), bf16),
        in_specs=[anywhere] * 6 + [pl.BlockSpec(memory_space=pltpu.VMEM)],
        out_specs=anywhere,
        scratch_shapes=[
            pltpu.VMEM((rows, D), bf16),
            pltpu.VMEM((4 * CHIPS, BLOCK), jnp.int32),
            pltpu.VMEM((NZ, NY, NX, 2, SHARD, QKV), bf16),
            pltpu.VMEM((NZ, NY, NX, QW, BLOCK), bf16),
            pltpu.VMEM((QW, SHARD), bf16),
            pltpu.VMEM((QW, SHARD), bf16),
            pltpu.VMEM((rows, QKV), f32),
            pltpu.VMEM((2, BLOCK, HD), f32),
            pltpu.VMEM((2, BLOCK, HD), f32),
            pltpu.VMEM((2, BLOCK, (REACH + 1) * BLOCK), f32),
            pltpu.VMEM((2, HQ, BLOCK, HD), bf16),
            pltpu.VMEM((2, REACH + 2, BLOCK, 2 * HD), bf16),
            pltpu.VMEM((rows, QW), bf16),
            pltpu.VMEM((rows, D), bf16),
            dma((6,)), dma((NZ,)), dma, dma,
            dma((112,)), dma((112,)), dma((NZ,)), dma((NZ,)),
            dma((112,)), dma((112,)), dma((NZ,)), dma((NZ,)),
            dma((2, 5)), dma((2, 5)), dma((2, 5)), dma((2, 5)),
        ],
        compiler_params=pltpu.CompilerParams(
            collective_id=1, has_side_effects=True, vmem_limit_bytes=60 * 2**20),
        name="layer",
    )(hidden_in, seg, w_query, w_key, w_value, w_out, freq)


def solution(mesh):
    in_specs = (
        P(("dp", "ctx"), None),
        P("dp"),
        P("ctx", None),
        P("ctx", None),
        P("ctx", None),
        P(None, "ctx"),
    )
    out_specs = P(("dp", "ctx"), None)
    return jax.shard_map(
        on_device, mesh=mesh, in_specs=in_specs, out_specs=out_specs, check_vma=False
    )
```

```python
import functools
import math

import jax
import jax.numpy as jnp
import numpy as np
from jax import lax
from jax.experimental import pallas as pl
from jax.experimental.pallas import tpu as pltpu
from jax.sharding import PartitionSpec as P

MESH = pl.DeviceIdType.MESH
REACH = 8
ROPE_BASE = 500000.0
NZ, NY, NX = 8, 2, 4
CHIPS = NZ * NY * NX
BLOCK = 128
HD = 128
HQ = 4
D = 8192
QW = HQ * HD
QKV = QW + 2 * HD
SHARD = 64
ORDER = (0, 1, -1, 2, -2, 3, -3, 4)
FAR = -1e30
W_ROWS = ((0, 384), (384, 128))


SIDE = (0, -1, 1, 2)
DIRECT = (2, 1)
PLAN = (
    (
        (("q","x",1),("q","x",2),("q","z",0,1,1),("q","z",0,-1,1),("q","x",3),("q","y",0),("q","z",1,1,1),("q","z",1,-1,1),("q","z",2,1,1),("q","z",2,-1,1),("q","z",0,1,2),("q","z",0,-1,2),("q","z",3,1,1),("q","z",3,-1,1),("q","y",1),("q","y",-1),("q","d",0),("w","s"),("q","z",1,1,2),("q","z",1,-1,2),("q","z",2,1,2),("q","z",2,-1,2),("q","z",0,1,3),("q","z",0,-1,3),("q","d",1),("q","z",3,1,2),("q","z",3,-1,2),("q","y",2),("q","y",-2),("w","x",2),),
        (("w","x",1),("w","z",0,1,1),("w","z",0,-1,1),("q","d",-1),("q","z",1,1,3),("q","z",1,-1,3),("q","z",2,1,3),("q","z",2,-1,3),("q","f",0),("q","d",2),("q","z",3,1,3),("q","z",3,-1,3),("q","y",3),("q","y",-3),("w","z",2,1,1),("w","z",2,-1,1),("q","d",-2),("w","z",1,1,1),("w","z",1,-1,1),("w","x",3),("w","y",0),("w","z",0,1,2),("w","z",0,-1,2),),
        (("q","f",1),("q","f",2),("q","d",3),("q","f",3),("q","y",4),("w","z",2,1,2),("w","z",2,-1,2),("q","d",-3),("w","z",1,1,2),("w","z",1,-1,2),("w","z",3,1,1),("w","z",3,-1,1),("w","y",1),("w","y",-1),("w","d",0),("w","z",0,1,3),("w","z",0,-1,3),("w","z",2,1,3),("w","z",2,-1,3),),
        (("q","d",4),("w","z",1,1,3),("w","z",1,-1,3),("w","z",3,1,2),("w","z",3,-1,2),("w","y",2),("w","y",-2),("w","f",0),("w","d",1),("w","f",2),("w","f",1),("w","d",-1),("w","z",3,1,3),("w","z",3,-1,3),("w","y",3),("w","y",-3),),
        (("w","d",2),("w","f",3),("w","y",4),),
        (("w","d",-2),("w","d",3),("w","d",-3),("w","d",4),),
        (),
        (),
        (),
        (),
        (),
        (),
    ),
    (
        (("q","y",0),("q","z",-1),("q","z",1),("q","y",-1),("q","z",2),("q","z",-2),("q","y",1),("q","r",0,-1),("q","r",0,1),("q","r",-1,-1),("q","r",-1,1),("q","y",2),("q","z",3),("q","z",-3),("q","y",-2),("w","s"),("q","r",1,-1),("q","r",1,1),("q","d",0),),
        (("q","d",-1),("q","r",2,-1),("q","z",4),("w","z",-1),("q","y",3),("w","z",1),("q","y",-3),("w","y",0),("q","r",2,1),("q","r",-2,-1),("q","r",-2,1),("q","y",4),("q","d",1),("w","y",-1),("w","y",1),),
        (("w","z",2),("w","z",-2),("q","r",3,-1),("q","r",-3,-1),("q","r",3,1),("w","r",0,-1),("q","r",-3,1),("w","r",0,1),("q","r",4,-1),("w","r",-1,-1),("q","d",2),("w","r",1,-1),("w","y",2),("w","y",-2),("q","d",-2),),
        (("w","z",3),("w","z",-3),("q","r",4,1),("w","r",1,1),("w","r",-1,1),("q","d",3),("w","r",2,-1),("q","d",-3),("w","z",4),("w","d",0),("w","r",-2,-1),("w","r",2,1),("w","r",-2,1),("w","y",3),("w","y",-3),("q","d",4),),
        (("w","d",1),("w","d",-1),("w","d",2),("w","r",3,-1),("w","d",-2),("w","r",3,1),("w","r",-3,-1),("w","r",-3,1),),
        (("w","y",4),("w","d",3),("w","d",-3),("w","r",4,1),("w","r",4,-1),),
        (("w","d",4),),
        (),
        (),
        (),
        (),
        (),
    ),
)


class Gather:
    def __init__(self, direct, place, ssem, rsem, sib_r, slot, most):
        self.direct, self.place = direct, place
        self.ssem, self.rsem, self.sib_r = ssem, rsem, sib_r
        self.slot, self.most = slot, most
        self.keys = ({}, {})

    def copy(self, ref, sem, device):
        return pltpu.make_async_remote_copy(
            src_ref=ref, dst_ref=ref, send_sem=self.ssem, recv_sem=sem, device_id=device, device_id_type=MESH)

    def sem(self, core, key):
        table = self.keys[core]
        return self.rsem.at[table.setdefault(key, len(table))]

    def send(self, core, where, key, move):
        self.copy(self.slot(core, *where), self.sem(core, key), self.place.at(*move)).start()

    def recv(self, core, where, key):
        self.copy(self.slot(core, *where), self.sem(core, key), self.place.sibling()).wait_recv()

    def sib(self, core, zr, part):
        where = (zr, part, None, None) if core == 0 else (zr, None, part, None)
        self.copy(self.slot(core, *where), self.sib_r.at[(zr + NZ) % NZ], self.place.sibling()).start()

    def sib_recv(self, core, zr):
        index = (zr + NZ) % NZ
        self.copy(self.slot(core, zr, None, None, None), self.sib_r.at[index], self.place.sibling()).wait_recv()

    def drain(self, core):
        for ref in self.most(core):
            self.copy(ref, self.sib_r.at[0], self.place.sibling()).wait_send()

    def a_s(self):
        for step in (1, -1, 2):
            self.send(0, (0, 0, 0, None), ("X", step), (0, 0, step))
        self.a_up(0)

    def a_up(self, j):
        for way in (1, -1):
            self.send(0, (0, 0, SIDE[j], None), ("Z", j, way, 1), (way, 0, 0))

    def a_x(self, j):
        self.recv(0, (0, 0, SIDE[j], None), ("X", -SIDE[j] if j < 3 else 2))
        self.a_up(j)

    def a_z(self, j, way, s):
        self.recv(0, (-way * s, 0, SIDE[j], None), ("Z", j, way, s))
        if s < 3:
            self.send(0, (-way * s, 0, SIDE[j], None), ("Z", j, way, s + 1), (way, 0, 0))
        else:
            self.send(0, (-way * s, 0, SIDE[j], (1 - way) // 2), ("Z", j), (way, 0, 0))

    def a_f(self, j):
        self.recv(0, (4, 0, SIDE[j], None), ("Z", j))

    def a_y(self, zr):
        for way in (1, -1):
            self.send(0, (zr, 0, None, (1 - way) // 2), ("Y", zr), (0, way, 0))
        self.sib(0, zr, 0)

    def a_d(self, zr):
        self.recv(0, (zr, 1, None, None), ("Y", zr))
        self.sib(0, zr, 1)

    def b_s(self):
        self.b_fan(0, 0)
        for far in range(1, self.direct + 1):
            for way in (1, -1):
                self.send(1, (0, 0, 0, None), ("Z", way, far), (way * far, 0, 0))
        self.b_cross(0)

    def b_fan(self, zr, yr):
        for way in (1, -1):
            self.send(1, (zr, yr, 0, None), ("X", zr, way), (0, 0, way))

    def b_cross(self, zr):
        for way in (1, -1):
            self.send(1, (zr, 0, 0, (1 - way) // 2), ("Y", zr), (0, way, 0))

    def b_z(self, zr):
        if zr == 4:
            self.recv(1, (4, 0, 0, None), ("Z", 4))
        else:
            way, far = (-1 if zr > 0 else 1), abs(zr)
            self.recv(1, (zr, 0, 0, None), ("Z", way, far))
            if far == 3:
                self.send(1, (zr, 0, 0, (1 - way) // 2), ("Z", 4), (way, 0, 0))
            elif far + 1 > self.direct:
                self.send(1, (zr, 0, 0, None), ("Z", way, far + 1), (way, 0, 0))
        self.b_fan(zr, 0)
        self.b_cross(zr)

    def b_y(self, zr):
        self.recv(1, (zr, 1, 0, None), ("Y", zr))
        self.b_fan(zr, 1)
        self.sib(1, zr, 0)

    def b_r(self, zr, way):
        self.recv(1, (zr, None, -way, None), ("X", zr, way))
        self.send(1, (zr, None, -way, (1 - way) // 2), ("XR", zr), (0, 0, way))
        self.sib(1, zr, -way)

    def b_d(self, zr):
        self.recv(1, (zr, None, 2, None), ("XR", zr))
        self.sib(1, zr, 2)


class Place:
    def __init__(self):
        ctx, dp = lax.axis_index("ctx"), lax.axis_index("dp")
        self.ctx, self.dp = ctx, dp
        self.c = ctx % 2
        self.k = ctx // 2
        self.x = self.k % NX
        self.yl = (self.k // NX) % NY
        self.z = self.k // (NX * NY)
        self.y = dp * 2 + self.yl

    def zi(self, zr):
        return (self.z + (zr + NZ)) % NZ

    def yi(self, yr):
        return (self.yl + yr) % NY

    def xi(self, xr):
        return (self.x + (xr + NX)) % NX

    def at(self, dz, dy, dx):
        y = (self.y + (dy + 4)) % 4
        chip = (self.zi(dz) * NY + y % 2) * NX + self.xi(dx)
        return {"ctx": chip * 2 + self.c, "dp": y // 2}

    def sibling(self):
        return {"ctx": self.k * 2 + (1 - self.c), "dp": self.dp}

    def on(self, chip, core):
        return {"ctx": chip * 2 + core, "dp": self.dp}


def kernel(hid_hbm, seg_hbm, wq_hbm, wk_hbm, wv_hbm, wo_hbm, freq_ref, out_hbm,
           hid, seg, qbuf, wbuf, wo_in, wo_sib, acc, cos_t, sin_t, bias, qrot, kvw, mixed, outv,
           load_sem, out_sem, wo_s, wo_r, q_s, q_r, qs_r, w_s, w_r, ws_r,
           kv_s, kv_r, kvs_s, kvs_r):
    me = Place()
    c, k, i = me.c, me.k, me.ctx

    def chips(zr, yr, xr):
        every = slice(None)
        return me.zi(zr), every if yr is None else me.yi(yr), every if xr is None else me.xi(xr)

    def q_slot(core, zr, yr, xr, half):
        rows = pl.ds(0, SHARD) if half is None else pl.ds(half * (SHARD // 2), SHARD // 2)
        return qbuf.at[*chips(zr, yr, xr), core, rows, :]

    def q_most(core):
        return (qbuf.at[:, :, :, core], qbuf.at[0:NZ - 1, :, :, core],
                qbuf.at[NZ - 1, 0, :, core], qbuf.at[NZ - 1, 1, 0:NX - 1, core])

    def w_slot(core, zr, yr, xr, half):
        first, count = W_ROWS[core]
        rows = pl.ds(first, count) if half is None else pl.ds(first + half * (count // 2), count // 2)
        return wbuf.at[*chips(zr, yr, xr), rows, :]

    def w_most(core):
        rows = pl.ds(*W_ROWS[core])
        return (wbuf.at[:, :, :, rows], wbuf.at[0:NZ - 1, :, :, rows],
                wbuf.at[NZ - 1, 0, :, rows], wbuf.at[NZ - 1, 1, 0:NX - 1, rows])

    gq = Gather(DIRECT[0], me, q_s, q_r, qs_r, q_slot, q_most)
    gw = Gather(DIRECT[1], me, w_s, w_r, ws_r, w_slot, w_most)

    def both(first, second):
        pl.when(c == 0)(first)
        pl.when(c == 1)(second)

    own = qbuf.at[me.z, me.yl, me.x, c]
    loads = [
        pltpu.make_async_copy(wq_hbm, own.at[:, pl.ds(0, QW)], load_sem.at[0]),
        pltpu.make_async_copy(wk_hbm, own.at[:, pl.ds(QW, HD)], load_sem.at[1]),
        pltpu.make_async_copy(wv_hbm, own.at[:, pl.ds(QW + HD, HD)], load_sem.at[2]),
        pltpu.make_async_copy(wo_hbm, wo_in, load_sem.at[3]),
        pltpu.make_async_copy(seg_hbm, seg, load_sem.at[4]),
        pltpu.make_async_copy(hid_hbm, hid, load_sem.at[5]),
    ]
    for load in loads:
        load.start()

    kvw[0, 0:REACH] = jnp.zeros((REACH, BLOCK, 2 * HD), jnp.bfloat16)

    def up(m):
        over = k + m >= CHIPS
        return (jnp.where(over, 2 * CHIPS - 1 - k - m, k + m), jnp.where(over, 1 - c, c))

    barrier = pltpu.get_barrier_semaphore()

    def greet(device):
        pl.semaphore_signal(barrier, inc=1, device_id=device, device_id_type=MESH)

    moves = [(0, 0, 1), (0, 0, -1), (0, 0, 2), (0, 1, 0), (0, -1, 0)]
    moves += [(way * far, 0, 0) for far in (1, 2, 3) for way in (1, -1)]
    for move in moves:
        greet(me.at(*move))
    greet(me.sibling())
    for m in range(1, 5):
        greet(me.on(*up(m)))
        pl.when(k >= m)(lambda m=m: greet(me.on(k - m, c)))
    pl.semaphore_wait(barrier, len(moves) + 5 + jnp.minimum(k, 4))

    for load in loads[:3]:
        load.wait()

    gathers = {"q": gq, "w": gw}

    def run(step):
        def core(which):
            for op in PLAN[which][step]:
                if op[:2] == ("w", "s"):
                    join(which)
                getattr(gathers[op[0]], "ab"[which] + "_" + op[1])(*op[2:])

        both(lambda: core(0), lambda: core(1))

    wo_copy = pltpu.make_async_remote_copy(
        src_ref=wo_in, dst_ref=wo_sib, send_sem=wo_s, recv_sem=wo_r,
        device_id=me.sibling(), device_id_type=MESH)

    def join(core):
        wo_copy.wait()
        rows = pl.ds(*W_ROWS[core])
        pair = [wo_in[:, rows], wo_sib[:, rows]]
        block = jnp.concatenate(pair if core == 0 else pair[::-1], axis=0)
        wbuf[me.z, me.yl, me.x, rows, :] = jnp.transpose(block)

    both(gq.a_s, gq.b_s)
    loads[3].wait()
    wo_copy.start()
    row = lax.broadcasted_iota(jnp.int32, (BLOCK, HD), 0)
    lane = lax.broadcasted_iota(jnp.int32, (BLOCK, HD), 1)
    late = 2 * 2 * CHIPS - 1 - i
    for b, block in enumerate((i, late)):
        angle = (block * BLOCK + row).astype(jnp.float32) * freq_ref[...]
        cos_t[b] = jnp.cos(angle)
        sine = jnp.sin(angle)
        sin_t[b] = jnp.where(lane < HD // 2, -sine, sine)

    loads[4].wait()
    for b in range(2):
        mine = seg[pl.ds(2 * i + b, 1), :]
        asks = jnp.transpose(jnp.broadcast_to(mine, (BLOCK, BLOCK)))
        for j in range(REACH + 1):
            if b == 0:
                block = i - REACH + j
                keys = seg[pl.ds(2 * jnp.maximum(block, 0), 1), :]
                keys = jnp.where(block >= 0, keys, -1)
            else:
                over = i + j >= 2 * CHIPS
                keys = seg[pl.ds(jnp.where(over, 2 * (4 * CHIPS - 1 - i - j), 2 * (i + j) + 1), 1), :]
            allowed = asks == keys
            if j == (REACH if b == 0 else 0):
                allowed = allowed & (lane <= row)
            bias[b, :, j * BLOCK:(j + 1) * BLOCK] = jnp.where(allowed, 0.0, FAR)

    loads[5].wait()
    acc[...] = jnp.zeros_like(acc)

    def project(first, last):
        @pl.loop(first, last)
        def _(t):
            zr = ((t + 1) // 2) * (2 * (t % 2) - 1)
            zz = (me.z + zr + NZ) % NZ
            both(lambda: gq.sib_recv(1, zr), lambda: gq.sib_recv(0, zr))
            part = NY * NX * 2 * SHARD
            weights = qbuf[zz].reshape(part, QKV)
            acc[...] += jnp.dot(hid[:, pl.ds(pl.multiple_of(zz * part, part), part)], weights,
                                preferred_element_type=jnp.float32)

    edges = (0, 1, 3, 5, 8)
    for n in range(4):
        run(n)
        project(edges[n], edges[n + 1])
    run(4)

    for b in range(2):
        rows = slice(b * BLOCK, (b + 1) * BLOCK)
        slot = REACH + c if b == 0 else c
        for h in range(HQ + 1):
            part = acc[rows, h * HD:(h + 1) * HD]
            turned = part * cos_t[b] + pltpu.roll(part, HD // 2, 1) * sin_t[b]
            turned = turned.astype(jnp.bfloat16)
            if h < HQ:
                qrot[b, h] = turned
            else:
                kvw[b, slot, :, 0:HD] = turned
        kvw[b, slot, :, HD:2 * HD] = acc[rows, QW + HD:QKV].astype(jnp.bfloat16)

    def kv_copy(src, dst, sent, got, device):
        return pltpu.make_async_remote_copy(
            src_ref=src, dst_ref=dst, send_sem=sent, recv_sem=got, device_id=device, device_id_type=MESH)

    early_own, late_own = kvw.at[0, REACH + c], kvw.at[1, c]

    def kv_up(m):
        return kv_copy(early_own, kvw.at[0, REACH - 2 * m + c], kv_s.at[0, m], kv_r.at[0, m], me.on(k + m, c))

    def kv_over(m):
        return kv_copy(early_own, kvw.at[1, 2 * m + 1 - c], kv_s.at[0, m], kv_r.at[1, m],
                       me.on(2 * CHIPS - 1 - k - m, 1 - c))

    def kv_down(m):
        return kv_copy(late_own, kvw.at[1, 2 * m + c], kv_s.at[1, m], kv_r.at[1, m], me.on(k - m, c))

    def kv_side(b, m, core):
        ref = kvw.at[0, REACH - 2 * m + core] if b == 0 else kvw.at[1, 2 * m + core]
        return kv_copy(ref, ref, kvs_s.at[b, m], kvs_r.at[b, m], me.sibling())

    for m in range(4, 0, -1):
        pl.when(k + m < CHIPS)(lambda m=m: kv_up(m).start())
        pl.when(k + m >= CHIPS)(lambda m=m: kv_over(m).start())
        pl.when(k >= m)(lambda m=m: kv_down(m).start())
    for b in range(2):
        kv_side(b, 0, c).start()

    run(5)
    for m in range(1, 5):
        def early_in(m=m):
            kv_copy(early_own, kvw.at[0, REACH - 2 * m + c], kv_s.at[0, m], kv_r.at[0, m], me.sibling()).wait_recv()
            kv_side(0, m, c).start()

        pl.when(k >= m)(early_in)
        kv_copy(late_own, kvw.at[1, 2 * m + c], kv_s.at[1, m], kv_r.at[1, m], me.sibling()).wait_recv()
        kv_side(1, m, c).start()

    run(6)

    def attend(b):
        window = kvw.at[b, pl.ds(c, REACH + 1)]
        span = (REACH + 1) * BLOCK
        keys = window[:, :, 0:HD].reshape(span, HD)
        values = window[:, :, HD:2 * HD].reshape(span, HD)
        scale = math.log2(math.e) / math.sqrt(HD)
        scores = lax.dot_general(qrot[b].reshape(HQ * BLOCK, HD), keys, (((1,), (1,)), ((), ())),
                                 preferred_element_type=jnp.float32)
        scores = scores.reshape(HQ, BLOCK, span) * scale + bias[b][None]
        scores = scores.reshape(HQ * BLOCK, span)
        peak = jnp.max(scores, axis=1, keepdims=True)
        terms = jnp.exp2(scores - peak)
        total = jnp.sum(terms, axis=1, keepdims=True)
        weights = (terms * (1.0 / total)).astype(jnp.bfloat16)
        result = jnp.dot(weights, values, preferred_element_type=jnp.float32).astype(jnp.bfloat16)
        for h in range(HQ):
            mixed[b * BLOCK:(b + 1) * BLOCK, h * HD:(h + 1) * HD] = result[h * BLOCK:(h + 1) * BLOCK]

    for m in range(0, 5):
        pl.when(k >= m)(lambda m=m: kv_side(0, m, 1 - c).wait_recv())
        kv_side(1, m, 1 - c).wait_recv()
    attend(0)

    run(7)
    attend(1)

    part = NY * NX * BLOCK

    def out_copy(t):
        zr = ((t + 1) // 2) * (2 * (t % 2) - 1)
        zz = (me.z + zr + NZ) % NZ
        columns = pl.ds(pl.multiple_of(zz * part, part), part)
        return pltpu.make_async_copy(outv.at[:, columns], out_hbm.at[:, columns], out_sem.at[t])

    def emit(t):
        zr = ((t + 1) // 2) * (2 * (t % 2) - 1)
        zz = (me.z + zr + NZ) % NZ
        both(lambda: gw.sib_recv(1, zr), lambda: gw.sib_recv(0, zr))
        for pair in range(NY * NX // 2):
            y, x = pair // 2, (pair % 2) * 2
            weights = jnp.concatenate([wbuf[zz, y, x], wbuf[zz, y, x + 1]], axis=1)
            result = jnp.dot(mixed[...], weights, preferred_element_type=jnp.float32)
            start = pl.multiple_of(zz * part + pair * 2 * BLOCK, 2 * BLOCK)
            outv[:, pl.ds(start, 2 * BLOCK)] = result.astype(jnp.bfloat16)
        out_copy(t).start()

    for n in range(3):
        run(8 + n)
        pl.loop(edges[n + 1] if n else 0, edges[n + 2])(emit)

    def finish(core):
        gq.drain(core)
        gw.drain(core)

    both(lambda: finish(0), lambda: finish(1))
    for m in range(1, 5):
        kv_copy(early_own, early_own, kv_s.at[0, m], kv_r.at[0, m], me.sibling()).wait_send()
        pl.when(k >= m)(lambda m=m: kv_down(m).wait_send())
    for m in range(0, 5):
        pl.when(k >= m)(lambda m=m: kv_side(0, m, c).wait_send())
        kv_side(1, m, c).wait_send()

    @pl.loop(0, NZ)
    def _(t):
        out_copy(t).wait()


def on_device(hidden_in, segment_ids, w_query, w_key, w_value, w_out):
    half = np.arange(HD // 2, dtype=np.float32) * np.float32(2.0) / np.float32(HD)
    freq = np.power(np.float32(ROPE_BASE), -half).astype(np.float32)
    freq = jnp.asarray(np.concatenate([freq, freq])[None, :])
    seg = segment_ids.reshape(4 * CHIPS, BLOCK)
    rows = hidden_in.shape[0]
    anywhere = pl.BlockSpec(memory_space=pl.ANY)
    dma = pltpu.SemaphoreType.DMA
    bf16, f32 = jnp.bfloat16, jnp.float32
    return pl.pallas_call(
        kernel,
        out_shape=jax.ShapeDtypeStruct((rows, D), bf16),
        in_specs=[anywhere] * 6 + [pl.BlockSpec(memory_space=pltpu.VMEM)],
        out_specs=anywhere,
        scratch_shapes=[
            pltpu.VMEM((rows, D), bf16),
            pltpu.VMEM((4 * CHIPS, BLOCK), jnp.int32),
            pltpu.VMEM((NZ, NY, NX, 2, SHARD, QKV), bf16),
            pltpu.VMEM((NZ, NY, NX, QW, BLOCK), bf16),
            pltpu.VMEM((SHARD, QW), bf16),
            pltpu.VMEM((SHARD, QW), bf16),
            pltpu.VMEM((rows, QKV), f32),
            pltpu.VMEM((2, BLOCK, HD), f32),
            pltpu.VMEM((2, BLOCK, HD), f32),
            pltpu.VMEM((2, BLOCK, (REACH + 1) * BLOCK), f32),
            pltpu.VMEM((2, HQ, BLOCK, HD), bf16),
            pltpu.VMEM((2, REACH + 2, BLOCK, 2 * HD), bf16),
            pltpu.VMEM((rows, QW), bf16),
            pltpu.VMEM((rows, D), bf16),
            dma((6,)), dma((NZ,)), dma, dma,
            dma, dma((40,)), dma((NZ,)),
            dma, dma((40,)), dma((NZ,)),
            dma((2, 5)), dma((2, 5)), dma((2, 5)), dma((2, 5)),
        ],
        compiler_params=pltpu.CompilerParams(
            collective_id=1, has_side_effects=True, vmem_limit_bytes=60 * 2**20),
        name="layer",
    )(hidden_in, seg, w_query, w_key, w_value, w_out.T, freq)


def solution(mesh):
    in_specs = (
        P(("dp", "ctx"), None),
        P("dp"),
        P("ctx", None),
        P("ctx", None),
        P("ctx", None),
        P(None, "ctx"),
    )
    out_specs = P(("dp", "ctx"), None)
    return jax.shard_map(
        on_device, mesh=mesh, in_specs=in_specs, out_specs=out_specs, check_vma=False
    )
```

```python
import functools
import math

import jax
import jax.numpy as jnp
import numpy as np
from jax import lax
from jax.experimental import pallas as pl
from jax.experimental.pallas import tpu as pltpu
from jax.sharding import PartitionSpec as P

MESH = pl.DeviceIdType.MESH
REACH = 8
ROPE_BASE = 500000.0
NZ, NY, NX = 8, 2, 4
CHIPS = NZ * NY * NX
BLOCK = 128
HD = 128
HQ = 4
D = 8192
QW = HQ * HD
QKV = QW + 2 * HD
SHARD = 64
ORDER = (0, 1, -1, 2, -2, 3, -3, 4)
FAR = -1e30
W_ROWS = ((0, 384), (384, 128))


SIDE = (0, -1, 1, 2)
DIRECT = (1, 2, 1)
RELAY = (False, False, True)
PLAN = (
    (
        (("k","s"),("q","s"),),
        (("k","x",1),("k","x",2),("k","z",0,1,1),("k","z",0,-1,1),("q","z",0,1,1),("q","z",0,-1,1),("q","x",1),("q","x",2),("k","x",3),("k","y",0),("k","z",1,1,1),("k","z",1,-1,1),("k","z",2,1,1),("k","z",2,-1,1),("k","z",0,1,2),("k","z",0,-1,2),("q","x",3),("q","y",0),("q","z",0,1,2),("q","z",0,-1,2),("k","d",0),("q","z",1,1,1),("q","z",1,-1,1),("k","z",3,1,1),("k","z",3,-1,1),("k","y",1),("k","y",-1),("k","z",1,1,2),("k","z",1,-1,2),("k","z",2,1,2),("k","z",2,-1,2),("k","z",0,1,3),("k","z",0,-1,3),("q","z",2,1,1),("q","z",2,-1,1),("q","d",0),("q","z",3,1,1),("q","z",3,-1,1),("q","y",1),),
        (("q","z",0,1,3),("q","y",-1),("q","z",0,-1,3),("k","d",1),("q","z",1,1,2),("q","z",1,-1,2),("k","z",3,1,2),("k","z",3,-1,2),("k","y",2),("k","y",-2),("k","d",-1),("k","z",1,1,3),("k","z",1,-1,3),("k","z",2,1,3),("k","z",2,-1,3),),
        (("k","f",0),("q","z",2,1,2),("q","z",2,-1,2),("q","z",3,1,2),("q","z",3,-1,2),("q","y",2),("q","y",-2),("q","d",1),("q","f",0),("q","z",1,1,3),("q","z",1,-1,3),("k","z",3,1,3),("k","z",3,-1,3),("k","y",3),("k","y",-3),("k","f",1),("k","f",2),("q","d",-1),("k","d",2),("w","s"),("k","d",-2),),
        (("q","z",2,1,3),("q","z",2,-1,3),("q","z",3,1,3),("q","z",3,-1,3),("q","y",3),("q","y",-3),("q","f",1),("k","f",3),("k","y",4),("q","d",2),("w","x",2),("w","x",1),("w","z",0,1,1),("w","z",0,-1,1),("q","d",-2),("q","f",2),("k","d",3),("q","f",3),("q","y",4),("k","d",-3),("w","z",2,1,1),("w","z",2,-1,1),("q","d",3),("w","x",3),("w","y",0),("w","z",1,1,1),("w","z",1,-1,1),("q","d",-3),("w","z",0,1,2),("w","z",0,-1,2),("k","d",4),),
        (("w","z",2,1,2),("w","z",2,-1,2),),
        (),
        (),
        (("w","z",3,1,1),("w","z",3,-1,1),("w","y",1),("w","y",-1),("q","d",4),("w","z",1,1,2),("w","z",1,-1,2),("w","z",0,1,3),("w","z",0,-1,3),("w","d",0),),
        (("w","z",2,1,3),("w","z",2,-1,3),("w","z",3,1,2),("w","y",-2),("w","z",3,-1,2),("w","y",2),("w","z",1,1,3),("w","z",1,-1,3),("w","d",1),("w","f",0),("w","f",2),("w","d",-1),("w","z",3,1,3),("w","y",-3),("w","z",3,-1,3),("w","y",3),("w","f",1),("w","d",-2),),
        (("w","f",3),("w","y",4),("w","d",2),),
        (),
        (),
        (("w","d",-3),),
        (("w","d",3),),
        (("w","d",4),),
        (),
    ),
    (
        (("k","s"),("q","s"),),
        (("k","z",1),("k","z",-1),("k","y",0),("q","y",0),("q","z",1),("k","y",1),("k","y",-1),("k","r",0,-1),("q","z",-1),("k","z",2),("k","z",-2),("q","r",0,-1),("k","r",0,1),("q","y",1),("k","r",1,-1),("k","r",-1,-1),("q","r",0,1),("k","r",1,1),("k","r",-1,1),("k","y",2),("k","y",-2),("k","z",3),("k","z",-3),("k","d",0),),
        (("q","y",-1),("q","r",1,-1),("q","r",1,1),("q","d",0),("k","r",2,-1),("k","d",1),("k","r",-2,-1),("k","d",-1),("k","r",2,1),("k","y",3),("k","y",-3),("k","r",-2,1),("k","z",4),("q","z",2),("q","z",-2),("q","r",-1,-1),),
        (("q","r",-1,1),("q","d",1),("k","d",2),("k","r",3,-1),("k","r",3,1),("k","r",-3,-1),("k","r",-3,1),("k","d",-2),("w","s"),("q","z",3),("q","z",-3),("k","y",4),("q","y",2),("q","y",-2),),
        (("q","d",-1),("k","d",3),("k","d",-3),("w","z",-1),("w","z",1),("q","z",4),("k","r",4,-1),("k","r",4,1),("w","y",0),("w","z",2),("w","z",-2),("q","y",3),("q","y",-3),("q","r",2,1),("q","r",2,-1),("q","r",-2,1),("q","r",-2,-1),("k","d",4),("w","r",0,-1),("w","r",0,1),("w","z",3),("w","y",-1),("w","y",1),("w","z",-3),("q","y",4),("q","r",3,-1),("q","r",3,1),),
        (("q","r",-3,1),("q","r",-3,-1),),
        (("w","y",2),("w","y",-2),("q","d",2),),
        (("q","d",-2),("w","d",0),),
        (("w","r",-1,1),("w","r",-1,-1),("w","r",1,1),("w","r",1,-1),("w","z",4),("w","y",3),("w","y",-3),("q","r",4,-1),("q","r",4,1),),
        (("q","d",3),("q","d",-3),("w","y",4),("w","r",2,-1),("w","r",2,1),("w","r",-2,-1),("w","r",-2,1),("w","d",-1),("w","d",1),("w","r",3,-1),("w","r",3,1),("w","r",-3,-1),("w","r",-3,1),("q","d",4),("w","r",4,-1),("w","r",4,1),),
        (("w","d",2),),
        (("w","d",-2),("w","d",3),("w","d",-3),),
        (),
        (("w","d",4),),
        (),
        (),
        (),
    ),
)


class Gather:
    def __init__(self, direct, relay, place, ssem, rsem, sib_r, slot, most):
        self.direct, self.relay, self.place = direct, relay, place
        self.ssem, self.rsem, self.sib_r = ssem, rsem, sib_r
        self.slot, self.most = slot, most
        self.keys = ({}, {})

    def copy(self, ref, sem, device):
        return pltpu.make_async_remote_copy(
            src_ref=ref, dst_ref=ref, send_sem=self.ssem, recv_sem=sem, device_id=device, device_id_type=MESH)

    def sem(self, core, key):
        table = self.keys[core]
        return self.rsem.at[table.setdefault(key, len(table))]

    def send(self, core, where, key, move):
        self.copy(self.slot(core, *where), self.sem(core, key), self.place.at(*move)).start()

    def recv(self, core, where, key):
        self.copy(self.slot(core, *where), self.sem(core, key), self.place.sibling()).wait_recv()

    def sib(self, core, zr, part):
        where = (zr, part, None, None) if core == 0 else (zr, None, part, None)
        self.copy(self.slot(core, *where), self.sib_r.at[(zr + NZ) % NZ], self.place.sibling()).start()

    def sib_recv(self, core, zr):
        index = (zr + NZ) % NZ
        self.copy(self.slot(core, zr, None, None, None), self.sib_r.at[index], self.place.sibling()).wait_recv()

    def drain(self, core):
        for ref in self.most(core):
            self.copy(ref, self.sib_r.at[0], self.place.sibling()).wait_send()

    def a_s(self):
        for step in (1, -1) if self.relay else (1, -1, 2):
            self.send(0, (0, 0, 0, None), ("X", step), (0, 0, step))
        self.a_up(0)

    def a_up(self, j):
        for way in (1, -1):
            self.send(0, (0, 0, SIDE[j], None), ("Z", j, way, 1), (way, 0, 0))

    def a_x(self, j):
        self.recv(0, (0, 0, SIDE[j], None), ("X", -SIDE[j] if j < 3 else 2))
        if self.relay and j < 3:
            self.send(0, (0, 0, SIDE[j], j - 1), ("X", 2), (0, 0, -SIDE[j]))
        self.a_up(j)

    def a_z(self, j, way, s):
        self.recv(0, (-way * s, 0, SIDE[j], None), ("Z", j, way, s))
        if s < 3:
            self.send(0, (-way * s, 0, SIDE[j], None), ("Z", j, way, s + 1), (way, 0, 0))
        else:
            self.send(0, (-way * s, 0, SIDE[j], (1 - way) // 2), ("Z", j), (way, 0, 0))

    def a_f(self, j):
        self.recv(0, (4, 0, SIDE[j], None), ("Z", j))

    def a_y(self, zr):
        for way in (1, -1):
            self.send(0, (zr, 0, None, (1 - way) // 2), ("Y", zr), (0, way, 0))
        self.sib(0, zr, 0)

    def a_d(self, zr):
        self.recv(0, (zr, 1, None, None), ("Y", zr))
        self.sib(0, zr, 1)

    def b_s(self):
        self.b_fan(0, 0)
        for far in range(1, self.direct + 1):
            for way in (1, -1):
                self.send(1, (0, 0, 0, None), ("Z", way, far), (way * far, 0, 0))
        self.b_cross(0)

    def b_fan(self, zr, yr):
        for way in (1, -1):
            self.send(1, (zr, yr, 0, None), ("X", zr, way), (0, 0, way))

    def b_cross(self, zr):
        for way in (1, -1):
            self.send(1, (zr, 0, 0, (1 - way) // 2), ("Y", zr), (0, way, 0))

    def b_z(self, zr):
        if zr == 4:
            self.recv(1, (4, 0, 0, None), ("Z", 4))
        else:
            way, far = (-1 if zr > 0 else 1), abs(zr)
            self.recv(1, (zr, 0, 0, None), ("Z", way, far))
            if far == 3:
                self.send(1, (zr, 0, 0, (1 - way) // 2), ("Z", 4), (way, 0, 0))
            elif far + 1 > self.direct:
                self.send(1, (zr, 0, 0, None), ("Z", way, far + 1), (way, 0, 0))
        self.b_fan(zr, 0)
        self.b_cross(zr)

    def b_y(self, zr):
        self.recv(1, (zr, 1, 0, None), ("Y", zr))
        self.b_fan(zr, 1)
        self.sib(1, zr, 0)

    def b_r(self, zr, way):
        self.recv(1, (zr, None, -way, None), ("X", zr, way))
        self.send(1, (zr, None, -way, (1 - way) // 2), ("XR", zr), (0, 0, way))
        self.sib(1, zr, -way)

    def b_d(self, zr):
        self.recv(1, (zr, None, 2, None), ("XR", zr))
        self.sib(1, zr, 2)


class Place:
    def __init__(self):
        ctx, dp = lax.axis_index("ctx"), lax.axis_index("dp")
        self.ctx, self.dp = ctx, dp
        self.c = ctx % 2
        self.k = ctx // 2
        self.x = self.k % NX
        self.yl = (self.k // NX) % NY
        self.z = self.k // (NX * NY)
        self.y = dp * 2 + self.yl

    def zi(self, zr):
        return (self.z + (zr + NZ)) % NZ

    def yi(self, yr):
        return (self.yl + yr) % NY

    def xi(self, xr):
        return (self.x + (xr + NX)) % NX

    def at(self, dz, dy, dx):
        y = (self.y + (dy + 4)) % 4
        chip = (self.zi(dz) * NY + y % 2) * NX + self.xi(dx)
        return {"ctx": chip * 2 + self.c, "dp": y // 2}

    def sibling(self):
        return {"ctx": self.k * 2 + (1 - self.c), "dp": self.dp}

    def on(self, chip, core):
        return {"ctx": chip * 2 + core, "dp": self.dp}


def kernel(hid_hbm, seg_hbm, wq_hbm, wk_hbm, wv_hbm, wo_hbm, freq_ref, out_hbm,
           hid, seg, kbuf, qbuf, wbuf, wo_in, wo_sib, acc, cos_t, sin_t, bias, qrot, kvw, mixed, outv,
           load_sem, out_sem, wo_s, wo_r, k_s, k_r, ks_r, q_s, q_r, qs_r, w_s, w_r, ws_r,
           kv_s, kv_r, kvs_s, kvs_r):
    me = Place()
    c, k, i = me.c, me.k, me.ctx

    def chips(zr, yr, xr):
        every = slice(None)
        return me.zi(zr), every if yr is None else me.yi(yr), every if xr is None else me.xi(xr)

    def rows_of(buf):
        def slot(core, zr, yr, xr, half):
            rows = pl.ds(0, SHARD) if half is None else pl.ds(half * (SHARD // 2), SHARD // 2)
            return buf.at[*chips(zr, yr, xr), core, rows, :]

        def most(core):
            return (buf.at[:, :, :, core], buf.at[0:NZ - 1, :, :, core],
                    buf.at[NZ - 1, 0, :, core], buf.at[NZ - 1, 1, 0:NX - 1, core])

        return slot, most

    def w_slot(core, zr, yr, xr, half):
        first, count = W_ROWS[core]
        rows = pl.ds(first, count) if half is None else pl.ds(first + half * (count // 2), count // 2)
        return wbuf.at[*chips(zr, yr, xr), rows, :]

    def w_most(core):
        rows = pl.ds(*W_ROWS[core])
        return (wbuf.at[:, :, :, rows], wbuf.at[0:NZ - 1, :, :, rows],
                wbuf.at[NZ - 1, 0, :, rows], wbuf.at[NZ - 1, 1, 0:NX - 1, rows])

    gk = Gather(DIRECT[0], RELAY[0], me, k_s, k_r, ks_r, *rows_of(kbuf))
    gq = Gather(DIRECT[1], RELAY[1], me, q_s, q_r, qs_r, *rows_of(qbuf))
    gw = Gather(DIRECT[2], RELAY[2], me, w_s, w_r, ws_r, w_slot, w_most)

    def both(first, second):
        pl.when(c == 0)(first)
        pl.when(c == 1)(second)

    own_k, own_q = kbuf.at[me.z, me.yl, me.x, c], qbuf.at[me.z, me.yl, me.x, c]
    loads = [
        pltpu.make_async_copy(wk_hbm, own_k.at[:, pl.ds(0, HD)], load_sem.at[0]),
        pltpu.make_async_copy(wv_hbm, own_k.at[:, pl.ds(HD, HD)], load_sem.at[1]),
        pltpu.make_async_copy(wq_hbm, own_q, load_sem.at[2]),
        pltpu.make_async_copy(wo_hbm, wo_in, load_sem.at[3]),
        pltpu.make_async_copy(seg_hbm, seg, load_sem.at[4]),
        pltpu.make_async_copy(hid_hbm, hid, load_sem.at[5]),
    ]
    for load in loads:
        load.start()

    kvw[0, 0:REACH] = jnp.zeros((REACH, BLOCK, 2 * HD), jnp.bfloat16)

    def up(m):
        over = k + m >= CHIPS
        return (jnp.where(over, 2 * CHIPS - 1 - k - m, k + m), jnp.where(over, 1 - c, c))

    barrier = pltpu.get_barrier_semaphore()

    def greet(device):
        pl.semaphore_signal(barrier, inc=1, device_id=device, device_id_type=MESH)

    moves = [(0, 0, 1), (0, 0, -1), (0, 0, 2), (0, 1, 0), (0, -1, 0)]
    moves += [(way * far, 0, 0) for far in (1, 2, 3) for way in (1, -1)]
    for move in moves:
        greet(me.at(*move))
    greet(me.sibling())
    for m in range(1, 5):
        greet(me.on(*up(m)))
        pl.when(k >= m)(lambda m=m: greet(me.on(k - m, c)))
    pl.semaphore_wait(barrier, len(moves) + 5 + jnp.minimum(k, 4))

    for load in loads[:3]:
        load.wait()

    gathers = {"k": gk, "q": gq, "w": gw}

    def run(step):
        def core(which):
            for op in PLAN[which][step]:
                if op[:2] == ("w", "s"):
                    join(which)
                getattr(gathers[op[0]], "ab"[which] + "_" + op[1])(*op[2:])

        both(lambda: core(0), lambda: core(1))

    wo_copy = pltpu.make_async_remote_copy(
        src_ref=wo_in, dst_ref=wo_sib, send_sem=wo_s, recv_sem=wo_r,
        device_id=me.sibling(), device_id_type=MESH)

    def join(core):
        wo_copy.wait()
        rows = pl.ds(*W_ROWS[core])
        pair = [wo_in[:, rows], wo_sib[:, rows]]
        block = jnp.concatenate(pair if core == 0 else pair[::-1], axis=0)
        wbuf[me.z, me.yl, me.x, rows, :] = jnp.transpose(block)

    run(0)
    loads[3].wait()
    wo_copy.start()
    row = lax.broadcasted_iota(jnp.int32, (BLOCK, HD), 0)
    lane = lax.broadcasted_iota(jnp.int32, (BLOCK, HD), 1)
    late = 2 * 2 * CHIPS - 1 - i
    for b, block in enumerate((i, late)):
        angle = (block * BLOCK + row).astype(jnp.float32) * freq_ref[...]
        cos_t[b] = jnp.cos(angle)
        sine = jnp.sin(angle)
        sin_t[b] = jnp.where(lane < HD // 2, -sine, sine)

    loads[4].wait()
    for b in range(2):
        mine = seg[pl.ds(2 * i + b, 1), :]
        asks = jnp.transpose(jnp.broadcast_to(mine, (BLOCK, BLOCK)))
        for j in range(REACH + 1):
            if b == 0:
                block = i - REACH + j
                keys = seg[pl.ds(2 * jnp.maximum(block, 0), 1), :]
                keys = jnp.where(block >= 0, keys, -1)
            else:
                over = i + j >= 2 * CHIPS
                keys = seg[pl.ds(jnp.where(over, 2 * (4 * CHIPS - 1 - i - j), 2 * (i + j) + 1), 1), :]
            allowed = asks == keys
            if j == (REACH if b == 0 else 0):
                allowed = allowed & (lane <= row)
            bias[b, :, j * BLOCK:(j + 1) * BLOCK] = jnp.where(allowed, 0.0, FAR)

    loads[5].wait()
    acc[...] = jnp.zeros_like(acc)

    part = NY * NX * 2 * SHARD
    edges = (0, 1, 3, 5, 8)

    def project(gather, buf, first, last, columns):
        @pl.loop(first, last)
        def _(t):
            zr = ((t + 1) // 2) * (2 * (t % 2) - 1)
            zz = (me.z + zr + NZ) % NZ
            both(lambda: gather.sib_recv(1, zr), lambda: gather.sib_recv(0, zr))
            weights = buf[zz].reshape(part, buf.shape[-1])
            acc[:, columns] += jnp.dot(hid[:, pl.ds(pl.multiple_of(zz * part, part), part)], weights,
                                       preferred_element_type=jnp.float32)

    def rotated(b, h):
        piece = acc[b * BLOCK:(b + 1) * BLOCK, h * HD:(h + 1) * HD]
        return (piece * cos_t[b] + pltpu.roll(piece, HD // 2, 1) * sin_t[b]).astype(jnp.bfloat16)

    for n in range(4):
        run(1 + n)
        project(gk, kbuf, edges[n], edges[n + 1], slice(QW, QKV))
    run(5)
    for b in range(2):
        slot = REACH + c if b == 0 else c
        kvw[b, slot, :, 0:HD] = rotated(b, HQ)
        kvw[b, slot, :, HD:2 * HD] = acc[b * BLOCK:(b + 1) * BLOCK, QW + HD:QKV].astype(jnp.bfloat16)

    def kv_copy(src, dst, sent, got, device):
        return pltpu.make_async_remote_copy(
            src_ref=src, dst_ref=dst, send_sem=sent, recv_sem=got, device_id=device, device_id_type=MESH)

    early_own, late_own = kvw.at[0, REACH + c], kvw.at[1, c]

    def kv_up(m):
        return kv_copy(early_own, kvw.at[0, REACH - 2 * m + c], kv_s.at[0, m], kv_r.at[0, m], me.on(k + m, c))

    def kv_over(m):
        return kv_copy(early_own, kvw.at[1, 2 * m + 1 - c], kv_s.at[0, m], kv_r.at[1, m],
                       me.on(2 * CHIPS - 1 - k - m, 1 - c))

    def kv_down(m):
        return kv_copy(late_own, kvw.at[1, 2 * m + c], kv_s.at[1, m], kv_r.at[1, m], me.on(k - m, c))

    def kv_side(b, m, core):
        ref = kvw.at[0, REACH - 2 * m + core] if b == 0 else kvw.at[1, 2 * m + core]
        return kv_copy(ref, ref, kvs_s.at[b, m], kvs_r.at[b, m], me.sibling())

    for m in range(4, 0, -1):
        pl.when(k + m < CHIPS)(lambda m=m: kv_up(m).start())
        pl.when(k + m >= CHIPS)(lambda m=m: kv_over(m).start())
        pl.when(k >= m)(lambda m=m: kv_down(m).start())
    for b in range(2):
        kv_side(b, 0, c).start()

    for n in range(3):
        run(6 + n)
        project(gq, qbuf, edges[n], edges[n + 1], slice(0, QW))
    run(9)

    for m in range(1, 5):
        def early_in(m=m):
            kv_copy(early_own, kvw.at[0, REACH - 2 * m + c], kv_s.at[0, m], kv_r.at[0, m], me.sibling()).wait_recv()
            kv_side(0, m, c).start()

        pl.when(k >= m)(early_in)
        kv_copy(late_own, kvw.at[1, 2 * m + c], kv_s.at[1, m], kv_r.at[1, m], me.sibling()).wait_recv()
        kv_side(1, m, c).start()

    run(10)
    project(gq, qbuf, edges[3], edges[4], slice(0, QW))
    run(11)
    for b in range(2):
        for h in range(HQ):
            qrot[b, h] = rotated(b, h)
    run(12)

    def attend(b):
        window = kvw.at[b, pl.ds(c, REACH + 1)]
        span = (REACH + 1) * BLOCK
        keys = window[:, :, 0:HD].reshape(span, HD)
        values = window[:, :, HD:2 * HD].reshape(span, HD)
        scale = math.log2(math.e) / math.sqrt(HD)
        scores = lax.dot_general(qrot[b].reshape(HQ * BLOCK, HD), keys, (((1,), (1,)), ((), ())),
                                 preferred_element_type=jnp.float32)
        scores = scores.reshape(HQ, BLOCK, span) * scale + bias[b][None]
        scores = scores.reshape(HQ * BLOCK, span)
        peak = jnp.max(scores, axis=1, keepdims=True)
        terms = jnp.exp2(scores - peak)
        total = jnp.sum(terms, axis=1, keepdims=True)
        weights = (terms * (1.0 / total)).astype(jnp.bfloat16)
        result = jnp.dot(weights, values, preferred_element_type=jnp.float32).astype(jnp.bfloat16)
        for h in range(HQ):
            mixed[b * BLOCK:(b + 1) * BLOCK, h * HD:(h + 1) * HD] = result[h * BLOCK:(h + 1) * BLOCK]

    for m in range(0, 5):
        pl.when(k >= m)(lambda m=m: kv_side(0, m, 1 - c).wait_recv())
        kv_side(1, m, 1 - c).wait_recv()
    attend(0)

    run(13)
    attend(1)


    def out_copy(t):
        zr = ((t + 1) // 2) * (2 * (t % 2) - 1)
        zz = (me.z + zr + NZ) % NZ
        columns = pl.ds(pl.multiple_of(zz * part, part), part)
        return pltpu.make_async_copy(outv.at[:, columns], out_hbm.at[:, columns], out_sem.at[t])

    def emit(t):
        zr = ((t + 1) // 2) * (2 * (t % 2) - 1)
        zz = (me.z + zr + NZ) % NZ
        both(lambda: gw.sib_recv(1, zr), lambda: gw.sib_recv(0, zr))
        for pair in range(NY * NX // 2):
            y, x = pair // 2, (pair % 2) * 2
            weights = jnp.concatenate([wbuf[zz, y, x], wbuf[zz, y, x + 1]], axis=1)
            result = jnp.dot(mixed[...], weights, preferred_element_type=jnp.float32)
            start = pl.multiple_of(zz * part + pair * 2 * BLOCK, 2 * BLOCK)
            outv[:, pl.ds(start, 2 * BLOCK)] = result.astype(jnp.bfloat16)
        out_copy(t).start()

    for n in range(3):
        run(14 + n)
        pl.loop(edges[n + 1] if n else 0, edges[n + 2])(emit)

    def finish(core):
        gk.drain(core)
        gq.drain(core)
        gw.drain(core)

    both(lambda: finish(0), lambda: finish(1))
    for m in range(1, 5):
        kv_copy(early_own, early_own, kv_s.at[0, m], kv_r.at[0, m], me.sibling()).wait_send()
        pl.when(k >= m)(lambda m=m: kv_down(m).wait_send())
    for m in range(0, 5):
        pl.when(k >= m)(lambda m=m: kv_side(0, m, c).wait_send())
        kv_side(1, m, c).wait_send()

    @pl.loop(0, NZ)
    def _(t):
        out_copy(t).wait()


def on_device(hidden_in, segment_ids, w_query, w_key, w_value, w_out):
    half = np.arange(HD // 2, dtype=np.float32) * np.float32(2.0) / np.float32(HD)
    freq = np.power(np.float32(ROPE_BASE), -half).astype(np.float32)
    freq = jnp.asarray(np.concatenate([freq, freq])[None, :])
    seg = segment_ids.reshape(4 * CHIPS, BLOCK)
    rows = hidden_in.shape[0]
    anywhere = pl.BlockSpec(memory_space=pl.ANY)
    dma = pltpu.SemaphoreType.DMA
    bf16, f32 = jnp.bfloat16, jnp.float32
    return pl.pallas_call(
        kernel,
        out_shape=jax.ShapeDtypeStruct((rows, D), bf16),
        in_specs=[anywhere] * 6 + [pl.BlockSpec(memory_space=pltpu.VMEM)],
        out_specs=anywhere,
        scratch_shapes=[
            pltpu.VMEM((rows, D), bf16),
            pltpu.VMEM((4 * CHIPS, BLOCK), jnp.int32),
            pltpu.VMEM((NZ, NY, NX, 2, SHARD, 2 * HD), bf16),
            pltpu.VMEM((NZ, NY, NX, 2, SHARD, QW), bf16),
            pltpu.VMEM((NZ, NY, NX, QW, BLOCK), bf16),
            pltpu.VMEM((SHARD, QW), bf16),
            pltpu.VMEM((SHARD, QW), bf16),
            pltpu.VMEM((rows, QKV), f32),
            pltpu.VMEM((2, BLOCK, HD), f32),
            pltpu.VMEM((2, BLOCK, HD), f32),
            pltpu.VMEM((2, BLOCK, (REACH + 1) * BLOCK), f32),
            pltpu.VMEM((2, HQ, BLOCK, HD), bf16),
            pltpu.VMEM((2, REACH + 2, BLOCK, 2 * HD), bf16),
            pltpu.VMEM((rows, QW), bf16),
            pltpu.VMEM((rows, D), bf16),
            dma((6,)), dma((NZ,)), dma, dma,
            dma, dma((40,)), dma((NZ,)),
            dma, dma((40,)), dma((NZ,)),
            dma, dma((40,)), dma((NZ,)),
            dma((2, 5)), dma((2, 5)), dma((2, 5)), dma((2, 5)),
        ],
        compiler_params=pltpu.CompilerParams(
            collective_id=1, has_side_effects=True, vmem_limit_bytes=60 * 2**20),
        name="layer",
    )(hidden_in, seg, w_query, w_key, w_value, w_out.T, freq)


def solution(mesh):
    in_specs = (
        P(("dp", "ctx"), None),
        P("dp"),
        P("ctx", None),
        P("ctx", None),
        P("ctx", None),
        P(None, "ctx"),
    )
    out_specs = P(("dp", "ctx"), None)
    return jax.shard_map(
        on_device, mesh=mesh, in_specs=in_specs, out_specs=out_specs, check_vma=False
    )
```

```python
import functools
import math

import jax
import jax.numpy as jnp
import numpy as np
from jax import lax
from jax.experimental import pallas as pl
from jax.experimental.pallas import tpu as pltpu
from jax.sharding import PartitionSpec as P

MESH = pl.DeviceIdType.MESH
REACH = 8
ROPE_BASE = 500000.0
NZ, NY, NX = 8, 2, 4
CHIPS = NZ * NY * NX
BLOCK = 128
HD = 128
HQ = 4
D = 8192
QW = HQ * HD
QKV = QW + 2 * HD
SHARD = 64
ORDER = (0, 1, -1, 2, -2, 3, -3, 4)
FAR = -1e30
FREQ = np.power(np.float32(ROPE_BASE), -np.arange(HD // 2, dtype=np.float32) * np.float32(2 / HD)).tolist()
W_ROWS = ((0, 384), (384, 128))


SIDE = (0, -1, 1, 2)
DIRECT = (3, 2, 1)
RELAY = (False, False, True)
PLAN = (
    (
        (("k","s"),("q","s"),),
        (("k","x",1),("k","x",2),("k","z",0,1,1),("k","z",0,-1,1),("q","z",0,1,1),("q","z",0,-1,1),("q","x",1),("k","x",3),("k","y",0),("q","x",2),("k","z",1,1,1),("k","z",1,-1,1),("q","x",3),("q","y",0),("k","z",2,1,1),("k","z",2,-1,1),("k","z",0,1,2),("k","z",0,-1,2),("q","z",0,1,2),("k","d",0),("q","z",0,-1,2),("q","z",1,1,1),("k","z",3,1,1),("k","z",3,-1,1),("k","y",1),("k","y",-1),("q","z",1,-1,1),("q","z",2,1,1),("k","z",1,1,2),("k","z",1,-1,2),("q","z",2,-1,1),("q","z",3,1,1),("q","y",-1),("q","d",0),),
        (("k","z",2,1,2),("k","z",0,1,3),("q","z",3,-1,1),("q","y",1),("k","z",2,-1,2),("k","z",0,-1,3),("q","z",0,1,3),("w","s"),("k","d",1),("k","z",3,1,2),("k","z",3,-1,2),("k","y",2),("k","y",-2),("k","d",-1),("q","z",1,1,2),("q","z",1,-1,2),("k","z",1,1,3),("k","z",1,-1,3),("q","z",2,1,2),),
        (("k","z",2,1,3),("q","z",2,-1,2),("q","d",-1),("k","z",2,-1,3),("q","z",3,1,2),("k","f",0),("q","z",3,-1,2),("q","y",2),("q","d",1),("w","z",0,1,1),("q","z",0,-1,3),("q","y",-2),("k","d",2),("k","z",3,1,3),("k","y",-3),("w","x",1),("k","z",3,-1,3),("k","y",3),("w","x",2),("k","d",-2),("w","z",0,-1,1),("q","z",1,1,3),("q","z",1,-1,3),("k","f",1),("q","z",2,1,3),("q","z",2,-1,3),),
        (("k","f",2),("q","z",3,1,3),("q","z",3,-1,3),("q","y",3),("q","y",-3),("q","d",2),("q","f",0),("w","z",0,1,2),("w","z",1,-1,1),("q","d",-2),("k","f",3),("k","y",4),("k","d",-3),("w","x",3),("w","y",0),("w","z",1,1,1),("w","z",2,-1,1),("k","d",3),("w","z",2,1,1),("w","z",0,-1,2),("q","f",1),("q","f",2),("q","d",3),("q","f",3),("q","y",4),("q","d",-3),("w","z",0,1,3),("w","z",1,-1,2),("k","d",4),("w","z",3,1,1),("w","z",3,-1,1),("w","y",1),("w","y",-1),),
        (("w","z",1,1,2),("w","z",2,-1,2),),
        (("w","d",0),("w","z",2,1,2),("w","z",0,-1,3),),
        (),
        (("w","z",1,-1,3),("q","d",4),),
        (("w","z",3,1,2),("w","z",3,-1,2),("w","y",2),("w","y",-2),("w","z",1,1,3),("w","z",2,-1,3),("w","f",0),("w","d",1),("w","z",2,1,3),("w","d",-1),("w","z",3,1,3),("w","z",3,-1,3),("w","y",3),("w","y",-3),("w","f",1),("w","f",2),("w","d",2),("w","f",3),("w","y",4),("w","d",-2),),
        (),
        (),
        (("w","d",3),),
        (("w","d",-3),),
        (("w","d",4),),
        (),
        (),
    ),
    (
        (("k","s"),("q","s"),),
        (("k","z",-1),("k","z",1),("k","y",0),("q","y",0),("q","z",-1),("q","z",1),("k","y",-1),("k","z",-2),("k","z",2),("k","y",1),("k","r",0,-1),("k","r",0,1),("q","z",2),("q","r",0,1),("q","r",0,-1),("k","z",-3),("k","z",3),("q","y",1),("k","y",-2),("k","y",2),("k","r",-1,1),("k","r",-1,-1),("k","r",1,1),("k","r",1,-1),("k","d",0),),
        (("q","y",-1),("q","y",2),("k","y",-3),("k","y",3),("q","d",0),("k","z",4),("w","s"),("k","r",-2,1),("k","r",-2,-1),("k","r",2,1),("k","r",2,-1),("k","d",-1),("k","d",1),("q","z",-2),),
        (("q","z",3),("k","r",-3,1),("k","r",-3,-1),("k","r",3,1),("k","r",3,-1),("w","z",-1),("w","z",1),("k","y",4),("w","y",0),("q","r",1,1),("q","r",1,-1),("k","d",-2),("q","r",-1,1),("q","r",-1,-1),("k","d",2),("q","y",-2),("q","r",2,1),("q","y",3),("q","r",2,-1),),
        (("q","z",-3),("k","d",-3),("k","d",3),("w","y",-1),("w","z",2),("w","z",-2),("k","r",4,1),("k","r",4,-1),("w","y",1),("w","r",0,1),("w","r",0,-1),("q","d",1),("q","d",-1),("q","y",-3),("q","r",-2,1),("q","r",-2,-1),("q","r",3,-1),("q","z",4),("q","r",3,1),("w","z",3),("w","z",-3),("q","d",2),("w","r",-1,1),("w","r",-1,-1),("w","y",2),("w","y",-2),("k","d",4),("w","r",1,1),("w","r",1,-1),("w","d",0),),
        (("q","r",-3,1),("q","r",-3,-1),),
        (("w","z",4),("q","y",4),("q","d",-2),),
        (),
        (("q","d",3),("w","y",3),("w","y",-3),),
        (("w","r",2,1),("w","r",2,-1),("w","r",-2,1),("w","r",-2,-1),("w","d",1),("w","d",-1),("q","d",-3),("w","y",4),("q","r",4,1),("q","r",4,-1),("w","r",3,1),("w","r",3,-1),("w","r",-3,1),("w","r",-3,-1),("w","d",2),("w","d",-2),("w","r",4,1),("w","r",4,-1),("q","d",4),),
        (("w","d",3),),
        (("w","d",-3),),
        (),
        (("w","d",4),),
        (),
        (),
        (),
    ),
)


class Gather:
    def __init__(self, direct, relay, place, ssem, rsem, sib_r, slot, most):
        self.direct, self.relay, self.place = direct, relay, place
        self.ssem, self.rsem, self.sib_r = ssem, rsem, sib_r
        self.slot, self.most = slot, most
        self.keys = ({}, {})

    def copy(self, ref, sem, device):
        return pltpu.make_async_remote_copy(
            src_ref=ref, dst_ref=ref, send_sem=self.ssem, recv_sem=sem, device_id=device, device_id_type=MESH)

    def sem(self, core, key):
        table = self.keys[core]
        return self.rsem.at[table.setdefault(key, len(table))]

    def send(self, core, where, key, move):
        self.copy(self.slot(core, *where), self.sem(core, key), self.place.at(*move)).start()

    def recv(self, core, where, key):
        self.copy(self.slot(core, *where), self.sem(core, key), self.place.sibling()).wait_recv()

    def sib(self, core, zr, part):
        where = (zr, part, None, None) if core == 0 else (zr, None, part, None)
        self.copy(self.slot(core, *where), self.sib_r.at[(zr + NZ) % NZ], self.place.sibling()).start()

    def sib_recv(self, core, zr):
        index = (zr + NZ) % NZ
        self.copy(self.slot(core, zr, None, None, None), self.sib_r.at[index], self.place.sibling()).wait_recv()

    def drain(self, core):
        for ref in self.most(core):
            self.copy(ref, self.sib_r.at[0], self.place.sibling()).wait_send()

    def a_s(self):
        for step in (1, -1) if self.relay else (1, -1, 2):
            self.send(0, (0, 0, 0, None), ("X", step), (0, 0, step))
        self.a_up(0)

    def a_up(self, j):
        for way in (1, -1):
            self.send(0, (0, 0, SIDE[j], None), ("Z", j, way, 1), (way, 0, 0))

    def a_x(self, j):
        self.recv(0, (0, 0, SIDE[j], None), ("X", -SIDE[j] if j < 3 else 2))
        if self.relay and j < 3:
            self.send(0, (0, 0, SIDE[j], j - 1), ("X", 2), (0, 0, -SIDE[j]))
        self.a_up(j)

    def a_z(self, j, way, s):
        self.recv(0, (-way * s, 0, SIDE[j], None), ("Z", j, way, s))
        if s < 3:
            self.send(0, (-way * s, 0, SIDE[j], None), ("Z", j, way, s + 1), (way, 0, 0))
        else:
            self.send(0, (-way * s, 0, SIDE[j], (1 - way) // 2), ("Z", j), (way, 0, 0))

    def a_f(self, j):
        self.recv(0, (4, 0, SIDE[j], None), ("Z", j))

    def a_y(self, zr):
        for way in (1, -1):
            self.send(0, (zr, 0, None, (1 - way) // 2), ("Y", zr), (0, way, 0))
        self.sib(0, zr, 0)

    def a_d(self, zr):
        self.recv(0, (zr, 1, None, None), ("Y", zr))
        self.sib(0, zr, 1)

    def b_s(self):
        self.b_fan(0, 0)
        for far in range(1, self.direct + 1):
            for way in (1, -1):
                self.send(1, (0, 0, 0, None), ("Z", way, far), (way * far, 0, 0))
        self.b_cross(0)

    def b_fan(self, zr, yr):
        for way in (1, -1):
            self.send(1, (zr, yr, 0, None), ("X", zr, way), (0, 0, way))

    def b_cross(self, zr):
        for way in (1, -1):
            self.send(1, (zr, 0, 0, (1 - way) // 2), ("Y", zr), (0, way, 0))

    def b_z(self, zr):
        if zr == 4:
            self.recv(1, (4, 0, 0, None), ("Z", 4))
        else:
            way, far = (-1 if zr > 0 else 1), abs(zr)
            self.recv(1, (zr, 0, 0, None), ("Z", way, far))
            if far == 3:
                self.send(1, (zr, 0, 0, (1 - way) // 2), ("Z", 4), (way, 0, 0))
            elif far + 1 > self.direct:
                self.send(1, (zr, 0, 0, None), ("Z", way, far + 1), (way, 0, 0))
        self.b_fan(zr, 0)
        self.b_cross(zr)

    def b_y(self, zr):
        self.recv(1, (zr, 1, 0, None), ("Y", zr))
        self.b_fan(zr, 1)
        self.sib(1, zr, 0)

    def b_r(self, zr, way):
        self.recv(1, (zr, None, -way, None), ("X", zr, way))
        self.send(1, (zr, None, -way, (1 - way) // 2), ("XR", zr), (0, 0, way))
        self.sib(1, zr, -way)

    def b_d(self, zr):
        self.recv(1, (zr, None, 2, None), ("XR", zr))
        self.sib(1, zr, 2)


class Place:
    def __init__(self):
        ctx, dp = lax.axis_index("ctx"), lax.axis_index("dp")
        self.ctx, self.dp = ctx, dp
        self.c = ctx % 2
        self.k = ctx // 2
        self.x = self.k % NX
        self.yl = (self.k // NX) % NY
        self.z = self.k // (NX * NY)
        self.y = dp * 2 + self.yl

    def zi(self, zr):
        return (self.z + (zr + NZ)) % NZ

    def yi(self, yr):
        return (self.yl + yr) % NY

    def xi(self, xr):
        return (self.x + (xr + NX)) % NX

    def at(self, dz, dy, dx):
        y = (self.y + (dy + 4)) % 4
        chip = (self.zi(dz) * NY + y % 2) * NX + self.xi(dx)
        return {"ctx": chip * 2 + self.c, "dp": y // 2}

    def sibling(self):
        return {"ctx": self.k * 2 + (1 - self.c), "dp": self.dp}

    def on(self, chip, core):
        return {"ctx": chip * 2 + core, "dp": self.dp}


def kernel(hid_hbm, seg_hbm, packed, out_hbm,
           hid, seg, kbuf, qbuf, wbuf, wo_in, wo_sib, acc, cos_t, sin_t, bias, qrot, kvw, mixed, outv,
           load_sem, out_sem, wo_s, wo_r, k_s, k_r, ks_r, q_s, q_r, qs_r, w_s, w_r, ws_r,
           kv_s, kv_r, kvs_s, kvs_r):
    me = Place()
    c, k, i = me.c, me.k, me.ctx

    def chips(zr, yr, xr):
        every = slice(None)
        return me.zi(zr), every if yr is None else me.yi(yr), every if xr is None else me.xi(xr)

    def rows_of(buf):
        def slot(core, zr, yr, xr, half):
            rows = pl.ds(0, SHARD) if half is None else pl.ds(half * (SHARD // 2), SHARD // 2)
            return buf.at[*chips(zr, yr, xr), core, rows, :]

        def most(core):
            return (buf.at[:, :, :, core], buf.at[0:NZ - 1, :, :, core],
                    buf.at[NZ - 1, 0, :, core], buf.at[NZ - 1, 1, 0:NX - 1, core])

        return slot, most

    def w_slot(core, zr, yr, xr, half):
        first, count = W_ROWS[core]
        rows = pl.ds(first, count) if half is None else pl.ds(first + half * (count // 2), count // 2)
        return wbuf.at[*chips(zr, yr, xr), rows, :]

    def w_most(core):
        rows = pl.ds(*W_ROWS[core])
        return (wbuf.at[:, :, :, rows], wbuf.at[0:NZ - 1, :, :, rows],
                wbuf.at[NZ - 1, 0, :, rows], wbuf.at[NZ - 1, 1, 0:NX - 1, rows])

    gk = Gather(DIRECT[0], RELAY[0], me, k_s, k_r, ks_r, *rows_of(kbuf))
    gq = Gather(DIRECT[1], RELAY[1], me, q_s, q_r, qs_r, *rows_of(qbuf))
    gw = Gather(DIRECT[2], RELAY[2], me, w_s, w_r, ws_r, w_slot, w_most)

    def both(first, second):
        pl.when(c == 0)(first)
        pl.when(c == 1)(second)

    own_k, own_q = kbuf.at[me.z, me.yl, me.x, c], qbuf.at[me.z, me.yl, me.x, c]
    loads = [
        pltpu.make_async_copy(packed.at[:, pl.ds(0, 2 * HD)], own_k, load_sem.at[0]),
        pltpu.make_async_copy(packed.at[:, pl.ds(2 * HD, QW)], own_q, load_sem.at[1]),
        pltpu.make_async_copy(packed.at[:, pl.ds(QKV, QW)], wo_in, load_sem.at[2]),
        pltpu.make_async_copy(seg_hbm, seg, load_sem.at[3]),
        pltpu.make_async_copy(hid_hbm, hid, load_sem.at[4]),
    ]
    for load in loads:
        load.start()

    kvw[0, 0:REACH] = jnp.zeros((REACH, BLOCK, 2 * HD), jnp.bfloat16)

    def up(m):
        over = k + m >= CHIPS
        return (jnp.where(over, 2 * CHIPS - 1 - k - m, k + m), jnp.where(over, 1 - c, c))

    barrier = pltpu.get_barrier_semaphore()

    def greet(device):
        pl.semaphore_signal(barrier, inc=1, device_id=device, device_id_type=MESH)

    moves = [(0, 0, 1), (0, 0, -1), (0, 0, 2), (0, 1, 0), (0, -1, 0)]
    moves += [(way * far, 0, 0) for far in (1, 2, 3) for way in (1, -1)]
    for move in moves:
        greet(me.at(*move))
    greet(me.sibling())
    for m in range(1, 5):
        greet(me.on(*up(m)))
        pl.when(k >= m)(lambda m=m: greet(me.on(k - m, c)))
    pl.semaphore_wait(barrier, len(moves) + 5 + jnp.minimum(k, 4))

    for load in loads[:2]:
        load.wait()

    gathers = {"k": gk, "q": gq, "w": gw}

    def run(step):
        def core(which):
            for op in PLAN[which][step]:
                if op[:2] == ("w", "s"):
                    join(which)
                getattr(gathers[op[0]], "ab"[which] + "_" + op[1])(*op[2:])

        both(lambda: core(0), lambda: core(1))

    wo_copy = pltpu.make_async_remote_copy(
        src_ref=wo_in, dst_ref=wo_sib, send_sem=wo_s, recv_sem=wo_r,
        device_id=me.sibling(), device_id_type=MESH)

    def join(core):
        wo_copy.wait()
        rows = pl.ds(*W_ROWS[core])
        pair = [wo_in[:, rows], wo_sib[:, rows]]
        block = jnp.concatenate(pair if core == 0 else pair[::-1], axis=0)
        wbuf[me.z, me.yl, me.x, rows, :] = jnp.transpose(block)

    run(0)
    loads[2].wait()
    wo_copy.start()
    wave = lax.broadcasted_iota(jnp.int32, (1, HD), 1) % (HD // 2)
    freq = jnp.zeros((1, HD), jnp.float32)
    for j in range(HD // 2):
        freq = jnp.where(wave == j, FREQ[j], freq)
    row = lax.broadcasted_iota(jnp.int32, (BLOCK, HD), 0)
    lane = lax.broadcasted_iota(jnp.int32, (BLOCK, HD), 1)
    late = 2 * 2 * CHIPS - 1 - i
    for b, block in enumerate((i, late)):
        angle = (block * BLOCK + row).astype(jnp.float32) * freq
        cos_t[b] = jnp.cos(angle)
        sine = jnp.sin(angle)
        sin_t[b] = jnp.where(lane < HD // 2, -sine, sine)

    loads[3].wait()
    for b in range(2):
        mine = seg[pl.ds(2 * i + b, 1), :]
        asks = jnp.transpose(jnp.broadcast_to(mine, (BLOCK, BLOCK)))
        for j in range(REACH + 1):
            if b == 0:
                block = i - REACH + j
                keys = seg[pl.ds(2 * jnp.maximum(block, 0), 1), :]
                keys = jnp.where(block >= 0, keys, -1)
            else:
                over = i + j >= 2 * CHIPS
                keys = seg[pl.ds(jnp.where(over, 2 * (4 * CHIPS - 1 - i - j), 2 * (i + j) + 1), 1), :]
            allowed = asks == keys
            if j == (REACH if b == 0 else 0):
                allowed = allowed & (lane <= row)
            bias[b, :, j * BLOCK:(j + 1) * BLOCK] = jnp.where(allowed, 0.0, FAR)

    loads[4].wait()
    acc[...] = jnp.zeros_like(acc)

    part = NY * NX * 2 * SHARD
    edges = (0, 1, 3, 5, 8)

    def project(gather, buf, first, last, columns):
        @pl.loop(first, last)
        def _(t):
            zr = ((t + 1) // 2) * (2 * (t % 2) - 1)
            zz = (me.z + zr + NZ) % NZ
            both(lambda: gather.sib_recv(1, zr), lambda: gather.sib_recv(0, zr))
            weights = buf[zz].reshape(part, buf.shape[-1])
            acc[:, columns] += jnp.dot(hid[:, pl.ds(pl.multiple_of(zz * part, part), part)], weights,
                                       preferred_element_type=jnp.float32)

    def rotated(b, h):
        piece = acc[b * BLOCK:(b + 1) * BLOCK, h * HD:(h + 1) * HD]
        return (piece * cos_t[b] + pltpu.roll(piece, HD // 2, 1) * sin_t[b]).astype(jnp.bfloat16)

    for n in range(4):
        run(1 + n)
        project(gk, kbuf, edges[n], edges[n + 1], slice(QW, QKV))
    run(5)
    for b in range(2):
        slot = REACH + c if b == 0 else c
        kvw[b, slot, :, 0:HD] = rotated(b, HQ)
        kvw[b, slot, :, HD:2 * HD] = acc[b * BLOCK:(b + 1) * BLOCK, QW + HD:QKV].astype(jnp.bfloat16)

    def kv_copy(src, dst, sent, got, device):
        return pltpu.make_async_remote_copy(
            src_ref=src, dst_ref=dst, send_sem=sent, recv_sem=got, device_id=device, device_id_type=MESH)

    early_own, late_own = kvw.at[0, REACH + c], kvw.at[1, c]

    def kv_up(m):
        return kv_copy(early_own, kvw.at[0, REACH - 2 * m + c], kv_s.at[0, m], kv_r.at[0, m], me.on(k + m, c))

    def kv_over(m):
        return kv_copy(early_own, kvw.at[1, 2 * m + 1 - c], kv_s.at[0, m], kv_r.at[1, m],
                       me.on(2 * CHIPS - 1 - k - m, 1 - c))

    def kv_down(m):
        return kv_copy(late_own, kvw.at[1, 2 * m + c], kv_s.at[1, m], kv_r.at[1, m], me.on(k - m, c))

    def kv_side(b, m, core):
        ref = kvw.at[0, REACH - 2 * m + core] if b == 0 else kvw.at[1, 2 * m + core]
        return kv_copy(ref, ref, kvs_s.at[b, m], kvs_r.at[b, m], me.sibling())

    for m in range(4, 0, -1):
        pl.when(k + m < CHIPS)(lambda m=m: kv_up(m).start())
        pl.when(k + m >= CHIPS)(lambda m=m: kv_over(m).start())
        pl.when(k >= m)(lambda m=m: kv_down(m).start())
    for b in range(2):
        kv_side(b, 0, c).start()

    for n in range(3):
        run(6 + n)
        project(gq, qbuf, edges[n], edges[n + 1], slice(0, QW))
    run(9)

    for m in range(1, 5):
        def early_in(m=m):
            kv_copy(early_own, kvw.at[0, REACH - 2 * m + c], kv_s.at[0, m], kv_r.at[0, m], me.sibling()).wait_recv()
            kv_side(0, m, c).start()

        pl.when(k >= m)(early_in)
        kv_copy(late_own, kvw.at[1, 2 * m + c], kv_s.at[1, m], kv_r.at[1, m], me.sibling()).wait_recv()
        kv_side(1, m, c).start()

    run(10)
    project(gq, qbuf, edges[3], edges[4], slice(0, QW))
    run(11)
    for b in range(2):
        for h in range(HQ):
            qrot[b, h] = rotated(b, h)
    run(12)

    def attend(b):
        window = kvw.at[b, pl.ds(c, REACH + 1)]
        span = (REACH + 1) * BLOCK
        keys = window[:, :, 0:HD].reshape(span, HD)
        values = window[:, :, HD:2 * HD].reshape(span, HD)
        scale = math.log2(math.e) / math.sqrt(HD)
        scores = lax.dot_general(qrot[b].reshape(HQ * BLOCK, HD), keys, (((1,), (1,)), ((), ())),
                                 preferred_element_type=jnp.float32)
        scores = scores.reshape(HQ, BLOCK, span) * scale + bias[b][None]
        scores = scores.reshape(HQ * BLOCK, span)
        peak = jnp.max(scores, axis=1, keepdims=True)
        terms = jnp.exp2(scores - peak)
        total = jnp.sum(terms, axis=1, keepdims=True)
        result = jnp.dot(terms.astype(jnp.bfloat16), values, preferred_element_type=jnp.float32)
        result = (result * (1.0 / total)).astype(jnp.bfloat16)
        for h in range(HQ):
            mixed[b * BLOCK:(b + 1) * BLOCK, h * HD:(h + 1) * HD] = result[h * BLOCK:(h + 1) * BLOCK]

    for m in range(0, 5):
        pl.when(k >= m)(lambda m=m: kv_side(0, m, 1 - c).wait_recv())
        kv_side(1, m, 1 - c).wait_recv()
    attend(0)

    run(13)
    attend(1)


    def out_copy(t):
        zr = ((t + 1) // 2) * (2 * (t % 2) - 1)
        zz = (me.z + zr + NZ) % NZ
        columns = pl.ds(pl.multiple_of(zz * part, part), part)
        return pltpu.make_async_copy(outv.at[:, columns], out_hbm.at[:, columns], out_sem.at[t])

    def emit(t):
        zr = ((t + 1) // 2) * (2 * (t % 2) - 1)
        zz = (me.z + zr + NZ) % NZ
        both(lambda: gw.sib_recv(1, zr), lambda: gw.sib_recv(0, zr))
        for pair in range(NY * NX // 2):
            y, x = pair // 2, (pair % 2) * 2
            weights = jnp.concatenate([wbuf[zz, y, x], wbuf[zz, y, x + 1]], axis=1)
            result = jnp.dot(mixed[...], weights, preferred_element_type=jnp.float32)
            start = pl.multiple_of(zz * part + pair * 2 * BLOCK, 2 * BLOCK)
            outv[:, pl.ds(start, 2 * BLOCK)] = result.astype(jnp.bfloat16)
        out_copy(t).start()

    for n in range(3):
        run(14 + n)
        pl.loop(edges[n + 1] if n else 0, edges[n + 2])(emit)

    def finish(core):
        gk.drain(core)
        gq.drain(core)
        gw.drain(core)

    both(lambda: finish(0), lambda: finish(1))
    for m in range(1, 5):
        kv_copy(early_own, early_own, kv_s.at[0, m], kv_r.at[0, m], me.sibling()).wait_send()
        pl.when(k >= m)(lambda m=m: kv_down(m).wait_send())
    for m in range(0, 5):
        pl.when(k >= m)(lambda m=m: kv_side(0, m, c).wait_send())
        kv_side(1, m, c).wait_send()

    @pl.loop(0, NZ)
    def _(t):
        out_copy(t).wait()


def on_device(hidden_in, segment_ids, w_query, w_key, w_value, w_out):
    seg = segment_ids.reshape(4 * CHIPS, BLOCK)
    rows = hidden_in.shape[0]
    anywhere = pl.BlockSpec(memory_space=pl.ANY)
    dma = pltpu.SemaphoreType.DMA
    bf16, f32 = jnp.bfloat16, jnp.float32
    return pl.pallas_call(
        kernel,
        out_shape=jax.ShapeDtypeStruct((rows, D), bf16),
        in_specs=[anywhere] * 3,
        out_specs=anywhere,
        scratch_shapes=[
            pltpu.VMEM((rows, D), bf16),
            pltpu.VMEM((4 * CHIPS, BLOCK), jnp.int32),
            pltpu.VMEM((NZ, NY, NX, 2, SHARD, 2 * HD), bf16),
            pltpu.VMEM((NZ, NY, NX, 2, SHARD, QW), bf16),
            pltpu.VMEM((NZ, NY, NX, QW, BLOCK), bf16),
            pltpu.VMEM((SHARD, QW), bf16),
            pltpu.VMEM((SHARD, QW), bf16),
            pltpu.VMEM((rows, QKV), f32),
            pltpu.VMEM((2, BLOCK, HD), f32),
            pltpu.VMEM((2, BLOCK, HD), f32),
            pltpu.VMEM((2, BLOCK, (REACH + 1) * BLOCK), f32),
            pltpu.VMEM((2, HQ, BLOCK, HD), bf16),
            pltpu.VMEM((2, REACH + 2, BLOCK, 2 * HD), bf16),
            pltpu.VMEM((rows, QW), bf16),
            pltpu.VMEM((rows, D), bf16),
            dma((5,)), dma((NZ,)), dma, dma,
            dma, dma((40,)), dma((NZ,)),
            dma, dma((40,)), dma((NZ,)),
            dma, dma((40,)), dma((NZ,)),
            dma((2, 5)), dma((2, 5)), dma((2, 5)), dma((2, 5)),
        ],
        compiler_params=pltpu.CompilerParams(
            collective_id=1, has_side_effects=True, vmem_limit_bytes=48 * 2**20),
        name="layer",
    )(hidden_in, seg, jnp.concatenate([w_key, w_value, w_query, w_out.T], axis=1))


def solution(mesh):
    in_specs = (
        P(("dp", "ctx"), None),
        P("dp"),
        P("ctx", None),
        P("ctx", None),
        P("ctx", None),
        P(None, "ctx"),
    )
    out_specs = P(("dp", "ctx"), None)
    return jax.shard_map(
        on_device, mesh=mesh, in_specs=in_specs, out_specs=out_specs, check_vma=False
    )
```

```python
import functools
import math

import jax
import jax.numpy as jnp
import numpy as np
from jax import lax
from jax.experimental import pallas as pl
from jax.experimental.pallas import tpu as pltpu
from jax.sharding import PartitionSpec as P

MESH = pl.DeviceIdType.MESH
REACH = 8
ROPE_BASE = 500000.0
NZ, NY, NX = 8, 2, 4
CHIPS = NZ * NY * NX
BLOCK = 128
HD = 128
HQ = 4
D = 8192
QW = HQ * HD
QKV = QW + 2 * HD
SHARD = 64
ORDER = (0, 1, -1, 2, -2, 3, -3, 4)
FAR = -1e30
FREQ = np.power(np.float32(ROPE_BASE), -np.arange(HD // 2, dtype=np.float32) * np.float32(2 / HD)).tolist()
W_ROWS = ((0, 384), (384, 128))


SIDE = (0, -1, 1, 2)
DIRECT = (1, 2, 1)
RELAY = (True, True, True)
Y_FIRST = (False, False, True)
PLAN = (
    (
        (("k","s"),("q","s"),),
        (("k","x",1),("k","x",2),("k","z",0,1,1),("k","z",0,-1,1),("q","x",1),("q","x",2),("q","z",0,1,1),("q","z",0,-1,1),("k","z",1,1,1),("k","z",1,-1,1),("k","x",3),("k","y",0),("k","z",2,1,1),("k","z",2,-1,1),("k","z",0,1,2),("k","z",0,-1,2),("q","z",1,1,1),("q","z",1,-1,1),("q","x",3),("q","y",0),("q","z",2,1,1),("q","z",2,-1,1),("k","z",1,-1,2),("q","z",0,1,2),("k","z",3,-1,1),("k","y",1),("k","d",0),("k","z",1,1,2),("k","z",2,-1,2),("k","z",3,1,1),("k","y",-1),("k","z",0,-1,3),("k","z",2,1,2),("k","z",0,1,3),("q","z",0,-1,2),),
        (("q","z",1,-1,2),("q","z",1,1,2),("q","z",3,-1,1),("q","y",1),("q","z",3,1,1),("q","d",0),("q","z",2,1,2),("w","s"),("q","y",-1),("k","d",1),("k","z",1,-1,3),("k","z",3,-1,2),("k","y",2),("k","z",1,1,3),("k","d",-1),("k","z",2,-1,3),("k","z",3,1,2),("k","y",-2),("k","z",2,1,3),("q","z",2,-1,2),("k","f",0),("q","z",0,-1,3),("q","z",0,1,3),("q","z",1,-1,3),("q","z",1,1,3),("q","d",1),("q","z",3,-1,2),("q","y",2),),
        (("q","z",3,1,2),("q","z",2,1,3),("w","z",0,-1,1),("q","y",-2),("w","x",1),("w","x",2),("k","z",3,-1,3),("k","y",3),("w","z",0,1,1),("q","d",-1),("k","f",1),("k","d",2),("q","z",2,-1,3),("k","z",3,1,3),("k","y",-3),("k","f",2),("k","d",-2),("q","f",0),("q","f",1),("q","z",3,-1,3),("q","y",3),("q","z",3,1,3),("q","y",-3),),
        (("q","d",2),("w","z",0,-1,2),("w","z",1,1,1),("q","d",-2),("w","z",1,-1,1),("w","x",3),("k","d",3),("w","y",0),("w","z",2,1,1),("w","z",2,-1,1),("k","d",-3),("w","z",0,1,2),("k","f",3),("k","y",4),("q","f",2),("q","f",3),("q","y",4),("q","d",3),("w","z",1,1,2),("w","z",0,-1,3),("q","d",-3),("w","z",3,1,1),("w","y",-1),("w","z",1,-1,2),("w","z",2,1,2),("w","z",3,-1,1),("w","y",1),("w","d",0),("w","z",0,1,3),("w","z",2,-1,2),("k","d",4),("w","z",1,1,3),("q","d",4),),
        (("w","z",3,1,2),("w","y",-2),("w","z",1,-1,3),),
        (("w","z",3,-1,2),("w","y",2),("w","d",-1),("w","z",2,1,3),),
        (),
        (("w","z",2,-1,3),("w","f",0),),
        (("w","d",1),("w","f",1),("w","z",3,1,3),("w","y",-3),("w","z",3,-1,3),("w","y",3),("w","d",-2),("w","f",2),("w","d",2),("w","f",3),("w","y",4),),
        (),
        (),
        (("w","d",-3),),
        (("w","d",3),),
        (("w","d",4),),
        (),
        (),
    ),
    (
        (("k","s"),("q","s"),),
        (("k","y",0),("k","z",-1),("k","z",1),("q","y",0),("q","z",-1),("q","z",1),("q","z",-2),("k","r",0,-1),("k","r",0,1),("k","y",-1),("k","y",1),("k","z",-2),("k","z",2),("q","r",0,1),("q","r",0,-1),("q","z",2),("q","y",1),("q","y",-1),("k","d",0),("k","y",-2),("k","r",-1,1),("k","y",2),("k","z",3),("k","r",1,1),("k","r",1,-1),("k","r",-1,-1),("k","z",-3),),
        (("q","d",0),("q","z",-3),("q","y",2),("w","s"),("k","r",-2,1),("k","r",-2,-1),("k","y",3),("k","y",-3),("k","r",2,-1),("k","r",2,1),("k","z",4),("k","d",1),("k","d",-1),),
        (("q","r",1,1),("q","r",1,-1),("q","r",-1,1),("q","r",-1,-1),("q","r",2,1),("w","v",1,0),("q","r",2,-1),("w","y",0),("w","p",0),("q","z",3),("w","v",-1,0),("k","d",-2),("k","r",3,1),("k","r",3,-1),("q","y",-2),("k","r",-3,1),("k","r",-3,-1),("k","y",4),("k","d",2),("q","y",-3),),
        (("q","d",1),("q","d",-1),("w","v",2,0),("q","d",2),("w","r",0,1),("w","r",0,-1),("w","v",-1,1),("w","p",-1),("q","y",3),("w","v",1,1),("w","p",1),("q","z",4),("k","d",3),("w","v",-2,0),("q","r",-2,1),("q","r",-2,-1),("k","d",-3),("k","r",4,1),("k","r",4,-1),("q","r",-3,1),("w","v",3,0),("q","r",-3,-1),("w","d",0),("w","r",-1,1),("w","r",-1,-1),("q","r",3,1),("q","r",3,-1),("w","r",1,1),("w","v",-2,1),("w","r",1,-1),("w","p",-2),("q","y",4),("w","v",-3,0),("w","v",2,1),("w","p",2),("q","d",-2),("k","d",4),),
        (),
        (("w","d",-1),("q","d",-3),),
        (),
        (("w","r",-2,-1),("w","v",-3,1),("w","r",-2,1),("w","d",1),("w","p",-3),("q","d",3),("q","r",4,1),("w","v",3,1),("w","v",4,0),("w","p",3),("q","r",4,-1),),
        (("w","r",2,1),("w","r",2,-1),("w","v",4,1),("w","p",4),("w","r",-3,1),("w","r",-3,-1),("w","d",-2),("w","r",3,-1),),
        (("w","r",3,1),("q","d",4),),
        (("w","d",2),),
        (("w","r",4,1),("w","r",4,-1),("w","d",-3),),
        (("w","d",3),),
        (("w","d",4),),
        (),
        (),
    ),
)


class Gather:
    def __init__(self, direct, relay, y_first, place, ssem, rsem, sib_r, slot, most):
        self.direct, self.relay, self.y_first, self.place = direct, relay, y_first, place
        self.ssem, self.rsem, self.sib_r = ssem, rsem, sib_r
        self.slot, self.most = slot, most
        self.keys = ({}, {})

    def copy(self, ref, sem, device):
        return pltpu.make_async_remote_copy(
            src_ref=ref, dst_ref=ref, send_sem=self.ssem, recv_sem=sem, device_id=device, device_id_type=MESH)

    def sem(self, core, key):
        table = self.keys[core]
        return self.rsem.at[table.setdefault(key, len(table))]

    def send(self, core, where, key, move):
        self.copy(self.slot(core, *where), self.sem(core, key), self.place.at(*move)).start()

    def recv(self, core, where, key):
        self.copy(self.slot(core, *where), self.sem(core, key), self.place.sibling()).wait_recv()

    def sib(self, core, zr, part):
        where = (zr, part, None, None) if core == 0 else (zr, None, part, None)
        self.copy(self.slot(core, *where), self.sib_r.at[(zr + NZ) % NZ], self.place.sibling()).start()

    def sib_recv(self, core, zr):
        index = (zr + NZ) % NZ
        self.copy(self.slot(core, zr, None, None, None), self.sib_r.at[index], self.place.sibling()).wait_recv()

    def drain(self, core):
        for ref in self.most(core):
            self.copy(ref, self.sib_r.at[0], self.place.sibling()).wait_send()

    def a_s(self):
        for step in (1, -1) if self.relay else (1, -1, 2):
            self.send(0, (0, 0, 0, None), ("X", step), (0, 0, step))
        self.a_up(0)

    def a_up(self, j):
        for way in (1, -1):
            self.send(0, (0, 0, SIDE[j], None), ("Z", j, way, 1), (way, 0, 0))

    def a_x(self, j):
        self.recv(0, (0, 0, SIDE[j], None), ("X", -SIDE[j] if j < 3 else 2))
        if self.relay and j < 3:
            self.send(0, (0, 0, SIDE[j], j - 1), ("X", 2), (0, 0, -SIDE[j]))
        self.a_up(j)

    def a_z(self, j, way, s):
        self.recv(0, (-way * s, 0, SIDE[j], None), ("Z", j, way, s))
        if s < 3:
            self.send(0, (-way * s, 0, SIDE[j], None), ("Z", j, way, s + 1), (way, 0, 0))
        else:
            self.send(0, (-way * s, 0, SIDE[j], (1 - way) // 2), ("Z", j), (way, 0, 0))

    def a_f(self, j):
        self.recv(0, (4, 0, SIDE[j], None), ("Z", j))

    def a_y(self, zr):
        for way in (1, -1):
            self.send(0, (zr, 0, None, (1 - way) // 2), ("Y", zr), (0, way, 0))
        self.sib(0, zr, 0)

    def a_d(self, zr):
        self.recv(0, (zr, 1, None, None), ("Y", zr))
        self.sib(0, zr, 1)

    def b_s(self):
        self.b_fan(0, 0)
        self.b_up(0)
        self.b_cross(0)

    def b_up(self, yr):
        for far in range(1, self.direct + 1):
            for way in (1, -1):
                self.send(1, (0, yr, 0, None), ("Z", way, far, yr), (way * far, 0, 0))

    def b_fan(self, zr, yr):
        for way in (1, -1):
            self.send(1, (zr, yr, 0, None), ("X", zr, way), (0, 0, way))

    def b_cross(self, zr):
        for way in (1, -1):
            self.send(1, (zr, 0, 0, (1 - way) // 2), ("Y", zr), (0, way, 0))

    def b_v(self, zr, yr):
        if zr == 4:
            self.recv(1, (4, yr, 0, None), ("Z", 4, yr))
        else:
            way, far = (-1 if zr > 0 else 1), abs(zr)
            self.recv(1, (zr, yr, 0, None), ("Z", way, far, yr))
            if far == 3:
                self.send(1, (zr, yr, 0, (1 - way) // 2), ("Z", 4, yr), (way, 0, 0))
            elif far + 1 > self.direct:
                self.send(1, (zr, yr, 0, None), ("Z", way, far + 1, yr), (way, 0, 0))
        self.b_fan(zr, yr)

    def b_z(self, zr):
        self.b_v(zr, 0)
        self.b_cross(zr)

    def b_y(self, zr):
        self.recv(1, (zr, 1, 0, None), ("Y", zr))
        self.b_fan(zr, 1)
        if self.y_first:
            self.b_up(1)
        else:
            self.b_p(zr)

    def b_p(self, zr):
        self.sib(1, zr, 0)

    def b_r(self, zr, way):
        self.recv(1, (zr, None, -way, None), ("X", zr, way))
        self.send(1, (zr, None, -way, (1 - way) // 2), ("XR", zr), (0, 0, way))
        self.sib(1, zr, -way)

    def b_d(self, zr):
        self.recv(1, (zr, None, 2, None), ("XR", zr))
        self.sib(1, zr, 2)


class Place:
    def __init__(self):
        ctx, dp = lax.axis_index("ctx"), lax.axis_index("dp")
        self.ctx, self.dp = ctx, dp
        self.c = ctx % 2
        self.k = ctx // 2
        self.x = self.k % NX
        self.yl = (self.k // NX) % NY
        self.z = self.k // (NX * NY)
        self.y = dp * 2 + self.yl

    def zi(self, zr):
        return (self.z + (zr + NZ)) % NZ

    def yi(self, yr):
        return (self.yl + yr) % NY

    def xi(self, xr):
        return (self.x + (xr + NX)) % NX

    def at(self, dz, dy, dx):
        y = (self.y + (dy + 4)) % 4
        chip = (self.zi(dz) * NY + y % 2) * NX + self.xi(dx)
        return {"ctx": chip * 2 + self.c, "dp": y // 2}

    def sibling(self):
        return {"ctx": self.k * 2 + (1 - self.c), "dp": self.dp}

    def on(self, chip, core):
        return {"ctx": chip * 2 + core, "dp": self.dp}


def kernel(hid_hbm, seg_hbm, packed, out_hbm,
           hid, seg, kbuf, qbuf, wbuf, wo_in, wo_sib, acc, cos_t, sin_t, bias, qrot, kvw, mixed, outv,
           load_sem, out_sem, wo_s, wo_r, k_s, k_r, ks_r, q_s, q_r, qs_r, w_s, w_r, ws_r,
           kv_s, kv_r, kvs_s, kvs_r):
    me = Place()
    c, k, i = me.c, me.k, me.ctx

    def chips(zr, yr, xr):
        every = slice(None)
        return me.zi(zr), every if yr is None else me.yi(yr), every if xr is None else me.xi(xr)

    def rows_of(buf):
        def slot(core, zr, yr, xr, half):
            rows = pl.ds(0, SHARD) if half is None else pl.ds(half * (SHARD // 2), SHARD // 2)
            return buf.at[*chips(zr, yr, xr), core, rows, :]

        def most(core):
            return (buf.at[:, :, :, core], buf.at[0:NZ - 1, :, :, core],
                    buf.at[NZ - 1, 0, :, core], buf.at[NZ - 1, 1, 0:NX - 1, core])

        return slot, most

    def w_slot(core, zr, yr, xr, half):
        first, count = W_ROWS[core]
        rows = pl.ds(first, count) if half is None else pl.ds(first + half * (count // 2), count // 2)
        return wbuf.at[*chips(zr, yr, xr), rows, :]

    def w_most(core):
        rows = pl.ds(*W_ROWS[core])
        return (wbuf.at[:, :, :, rows], wbuf.at[0:NZ - 1, :, :, rows],
                wbuf.at[NZ - 1, 0, :, rows], wbuf.at[NZ - 1, 1, 0:NX - 1, rows])

    gk = Gather(DIRECT[0], RELAY[0], Y_FIRST[0], me, k_s, k_r, ks_r, *rows_of(kbuf))
    gq = Gather(DIRECT[1], RELAY[1], Y_FIRST[1], me, q_s, q_r, qs_r, *rows_of(qbuf))
    gw = Gather(DIRECT[2], RELAY[2], Y_FIRST[2], me, w_s, w_r, ws_r, w_slot, w_most)

    def both(first, second):
        pl.when(c == 0)(first)
        pl.when(c == 1)(second)

    own_k, own_q = kbuf.at[me.z, me.yl, me.x, c], qbuf.at[me.z, me.yl, me.x, c]
    loads = [
        pltpu.make_async_copy(packed.at[:, pl.ds(0, 2 * HD)], own_k, load_sem.at[0]),
        pltpu.make_async_copy(packed.at[:, pl.ds(2 * HD, QW)], own_q, load_sem.at[1]),
        pltpu.make_async_copy(packed.at[:, pl.ds(QKV, QW)], wo_in, load_sem.at[2]),
        pltpu.make_async_copy(seg_hbm, seg, load_sem.at[3]),
        pltpu.make_async_copy(hid_hbm, hid, load_sem.at[4]),
    ]
    for load in loads:
        load.start()

    kvw[0, 0:REACH] = jnp.zeros((REACH, BLOCK, 2 * HD), jnp.bfloat16)

    def up(m):
        over = k + m >= CHIPS
        return (jnp.where(over, 2 * CHIPS - 1 - k - m, k + m), jnp.where(over, 1 - c, c))

    barrier = pltpu.get_barrier_semaphore()

    def greet(device):
        pl.semaphore_signal(barrier, inc=1, device_id=device, device_id_type=MESH)

    moves = [(0, 0, 1), (0, 0, -1), (0, 0, 2), (0, 1, 0), (0, -1, 0)]
    moves += [(way * far, 0, 0) for far in (1, 2, 3) for way in (1, -1)]
    for move in moves:
        greet(me.at(*move))
    greet(me.sibling())
    for m in range(1, 5):
        greet(me.on(*up(m)))
        pl.when(k >= m)(lambda m=m: greet(me.on(k - m, c)))
    pl.semaphore_wait(barrier, len(moves) + 5 + jnp.minimum(k, 4))

    for load in loads[:2]:
        load.wait()

    gathers = {"k": gk, "q": gq, "w": gw}

    def run(step):
        def core(which):
            for op in PLAN[which][step]:
                if op[:2] == ("w", "s"):
                    join(which)
                getattr(gathers[op[0]], "ab"[which] + "_" + op[1])(*op[2:])

        both(lambda: core(0), lambda: core(1))

    wo_copy = pltpu.make_async_remote_copy(
        src_ref=wo_in, dst_ref=wo_sib, send_sem=wo_s, recv_sem=wo_r,
        device_id=me.sibling(), device_id_type=MESH)

    def join(core):
        wo_copy.wait()
        rows = pl.ds(*W_ROWS[core])
        pair = [wo_in[:, rows], wo_sib[:, rows]]
        block = jnp.concatenate(pair if core == 0 else pair[::-1], axis=0)
        wbuf[me.z, me.yl, me.x, rows, :] = jnp.transpose(block)

    run(0)
    loads[2].wait()
    wo_copy.start()
    wave = lax.broadcasted_iota(jnp.int32, (1, HD), 1) % (HD // 2)
    freq = jnp.zeros((1, HD), jnp.float32)
    for j in range(HD // 2):
        freq = jnp.where(wave == j, FREQ[j], freq)
    row = lax.broadcasted_iota(jnp.int32, (BLOCK, HD), 0)
    lane = lax.broadcasted_iota(jnp.int32, (BLOCK, HD), 1)
    late = 2 * 2 * CHIPS - 1 - i
    for b, block in enumerate((i, late)):
        angle = (block * BLOCK + row).astype(jnp.float32) * freq
        cos_t[b] = jnp.cos(angle)
        sine = jnp.sin(angle)
        sin_t[b] = jnp.where(lane < HD // 2, -sine, sine)

    loads[3].wait()
    for b in range(2):
        mine = seg[pl.ds(2 * i + b, 1), :]
        asks = jnp.transpose(jnp.broadcast_to(mine, (BLOCK, BLOCK)))
        for j in range(REACH + 1):
            if b == 0:
                block = i - REACH + j
                keys = seg[pl.ds(2 * jnp.maximum(block, 0), 1), :]
                keys = jnp.where(block >= 0, keys, -1)
            else:
                over = i + j >= 2 * CHIPS
                keys = seg[pl.ds(jnp.where(over, 2 * (4 * CHIPS - 1 - i - j), 2 * (i + j) + 1), 1), :]
            allowed = asks == keys
            if j == (REACH if b == 0 else 0):
                allowed = allowed & (lane <= row)
            bias[b, :, j * BLOCK:(j + 1) * BLOCK] = jnp.where(allowed, 0.0, FAR)

    loads[4].wait()
    acc[...] = jnp.zeros_like(acc)

    part = NY * NX * 2 * SHARD
    edges = (0, 1, 3, 5, 8)

    def project(gather, buf, first, last, columns):
        @pl.loop(first, last)
        def _(t):
            zr = ((t + 1) // 2) * (2 * (t % 2) - 1)
            zz = (me.z + zr + NZ) % NZ
            both(lambda: gather.sib_recv(1, zr), lambda: gather.sib_recv(0, zr))
            weights = buf[zz].reshape(part, buf.shape[-1])
            acc[:, columns] += jnp.dot(hid[:, pl.ds(pl.multiple_of(zz * part, part), part)], weights,
                                       preferred_element_type=jnp.float32)

    def rotated(b, h):
        piece = acc[b * BLOCK:(b + 1) * BLOCK, h * HD:(h + 1) * HD]
        return (piece * cos_t[b] + pltpu.roll(piece, HD // 2, 1) * sin_t[b]).astype(jnp.bfloat16)

    for n in range(4):
        run(1 + n)
        project(gk, kbuf, edges[n], edges[n + 1], slice(QW, QKV))
    run(5)
    for b in range(2):
        slot = REACH + c if b == 0 else c
        kvw[b, slot, :, 0:HD] = rotated(b, HQ)
        kvw[b, slot, :, HD:2 * HD] = acc[b * BLOCK:(b + 1) * BLOCK, QW + HD:QKV].astype(jnp.bfloat16)

    def kv_copy(src, dst, sent, got, device):
        return pltpu.make_async_remote_copy(
            src_ref=src, dst_ref=dst, send_sem=sent, recv_sem=got, device_id=device, device_id_type=MESH)

    early_own, late_own = kvw.at[0, REACH + c], kvw.at[1, c]

    def kv_up(m):
        return kv_copy(early_own, kvw.at[0, REACH - 2 * m + c], kv_s.at[0, m], kv_r.at[0, m], me.on(k + m, c))

    def kv_over(m):
        return kv_copy(early_own, kvw.at[1, 2 * m + 1 - c], kv_s.at[0, m], kv_r.at[1, m],
                       me.on(2 * CHIPS - 1 - k - m, 1 - c))

    def kv_down(m):
        return kv_copy(late_own, kvw.at[1, 2 * m + c], kv_s.at[1, m], kv_r.at[1, m], me.on(k - m, c))

    def kv_side(b, m, core):
        ref = kvw.at[0, REACH - 2 * m + core] if b == 0 else kvw.at[1, 2 * m + core]
        return kv_copy(ref, ref, kvs_s.at[b, m], kvs_r.at[b, m], me.sibling())

    for m in range(4, 0, -1):
        pl.when(k + m < CHIPS)(lambda m=m: kv_up(m).start())
        pl.when(k + m >= CHIPS)(lambda m=m: kv_over(m).start())
        pl.when(k >= m)(lambda m=m: kv_down(m).start())
    for b in range(2):
        kv_side(b, 0, c).start()

    for n in range(3):
        run(6 + n)
        project(gq, qbuf, edges[n], edges[n + 1], slice(0, QW))
    run(9)

    for m in range(1, 5):
        def early_in(m=m):
            kv_copy(early_own, kvw.at[0, REACH - 2 * m + c], kv_s.at[0, m], kv_r.at[0, m], me.sibling()).wait_recv()
            kv_side(0, m, c).start()

        pl.when(k >= m)(early_in)
        kv_copy(late_own, kvw.at[1, 2 * m + c], kv_s.at[1, m], kv_r.at[1, m], me.sibling()).wait_recv()
        kv_side(1, m, c).start()

    run(10)
    project(gq, qbuf, edges[3], edges[4], slice(0, QW))
    run(11)
    for b in range(2):
        for h in range(HQ):
            qrot[b, h] = rotated(b, h)
    run(12)

    def attend(b):
        window = kvw.at[b, pl.ds(c, REACH + 1)]
        span = (REACH + 1) * BLOCK
        keys = window[:, :, 0:HD].reshape(span, HD)
        values = window[:, :, HD:2 * HD].reshape(span, HD)
        scale = math.log2(math.e) / math.sqrt(HD)
        scores = lax.dot_general(qrot[b].reshape(HQ * BLOCK, HD), keys, (((1,), (1,)), ((), ())),
                                 preferred_element_type=jnp.float32)
        scores = scores.reshape(HQ, BLOCK, span) * scale + bias[b][None]
        scores = scores.reshape(HQ * BLOCK, span)
        peak = jnp.max(scores, axis=1, keepdims=True)
        terms = jnp.exp2(scores - peak)
        total = jnp.sum(terms, axis=1, keepdims=True)
        result = jnp.dot(terms.astype(jnp.bfloat16), values, preferred_element_type=jnp.float32)
        result = (result * (1.0 / total)).astype(jnp.bfloat16)
        for h in range(HQ):
            mixed[b * BLOCK:(b + 1) * BLOCK, h * HD:(h + 1) * HD] = result[h * BLOCK:(h + 1) * BLOCK]

    for m in range(0, 5):
        pl.when(k >= m)(lambda m=m: kv_side(0, m, 1 - c).wait_recv())
        kv_side(1, m, 1 - c).wait_recv()
    attend(0)

    run(13)
    attend(1)


    def out_copy(t):
        zr = ((t + 1) // 2) * (2 * (t % 2) - 1)
        zz = (me.z + zr + NZ) % NZ
        columns = pl.ds(pl.multiple_of(zz * part, part), part)
        return pltpu.make_async_copy(outv.at[:, columns], out_hbm.at[:, columns], out_sem.at[t])

    def emit(t):
        zr = ((t + 1) // 2) * (2 * (t % 2) - 1)
        zz = (me.z + zr + NZ) % NZ
        both(lambda: gw.sib_recv(1, zr), lambda: gw.sib_recv(0, zr))
        for pair in range(NY * NX // 2):
            y, x = pair // 2, (pair % 2) * 2
            weights = jnp.concatenate([wbuf[zz, y, x], wbuf[zz, y, x + 1]], axis=1)
            result = jnp.dot(mixed[...], weights, preferred_element_type=jnp.float32)
            start = pl.multiple_of(zz * part + pair * 2 * BLOCK, 2 * BLOCK)
            outv[:, pl.ds(start, 2 * BLOCK)] = result.astype(jnp.bfloat16)
        out_copy(t).start()

    for n in range(3):
        run(14 + n)
        pl.loop(edges[n + 1] if n else 0, edges[n + 2])(emit)

    def finish(core):
        gk.drain(core)
        gq.drain(core)
        gw.drain(core)

    both(lambda: finish(0), lambda: finish(1))
    for m in range(1, 5):
        kv_copy(early_own, early_own, kv_s.at[0, m], kv_r.at[0, m], me.sibling()).wait_send()
        pl.when(k >= m)(lambda m=m: kv_down(m).wait_send())
    for m in range(0, 5):
        pl.when(k >= m)(lambda m=m: kv_side(0, m, c).wait_send())
        kv_side(1, m, c).wait_send()

    @pl.loop(0, NZ)
    def _(t):
        out_copy(t).wait()


def on_device(hidden_in, segment_ids, w_query, w_key, w_value, w_out):
    seg = segment_ids.reshape(4 * CHIPS, BLOCK)
    rows = hidden_in.shape[0]
    anywhere = pl.BlockSpec(memory_space=pl.ANY)
    dma = pltpu.SemaphoreType.DMA
    bf16, f32 = jnp.bfloat16, jnp.float32
    return pl.pallas_call(
        kernel,
        out_shape=jax.ShapeDtypeStruct((rows, D), bf16),
        in_specs=[anywhere] * 3,
        out_specs=anywhere,
        scratch_shapes=[
            pltpu.VMEM((rows, D), bf16),
            pltpu.VMEM((4 * CHIPS, BLOCK), jnp.int32),
            pltpu.VMEM((NZ, NY, NX, 2, SHARD, 2 * HD), bf16),
            pltpu.VMEM((NZ, NY, NX, 2, SHARD, QW), bf16),
            pltpu.VMEM((NZ, NY, NX, QW, BLOCK), bf16),
            pltpu.VMEM((SHARD, QW), bf16),
            pltpu.VMEM((SHARD, QW), bf16),
            pltpu.VMEM((rows, QKV), f32),
            pltpu.VMEM((2, BLOCK, HD), f32),
            pltpu.VMEM((2, BLOCK, HD), f32),
            pltpu.VMEM((2, BLOCK, (REACH + 1) * BLOCK), f32),
            pltpu.VMEM((2, HQ, BLOCK, HD), bf16),
            pltpu.VMEM((2, REACH + 2, BLOCK, 2 * HD), bf16),
            pltpu.VMEM((rows, QW), bf16),
            pltpu.VMEM((rows, D), bf16),
            dma((5,)), dma((NZ,)), dma, dma,
            dma, dma((40,)), dma((NZ,)),
            dma, dma((40,)), dma((NZ,)),
            dma, dma((40,)), dma((NZ,)),
            dma((2, 5)), dma((2, 5)), dma((2, 5)), dma((2, 5)),
        ],
        compiler_params=pltpu.CompilerParams(
            collective_id=1, has_side_effects=True, vmem_limit_bytes=48 * 2**20),
        name="layer",
    )(hidden_in, seg, jnp.concatenate([w_key, w_value, w_query, w_out.T], axis=1))


def solution(mesh):
    in_specs = (
        P(("dp", "ctx"), None),
        P("dp"),
        P("ctx", None),
        P("ctx", None),
        P("ctx", None),
        P(None, "ctx"),
    )
    out_specs = P(("dp", "ctx"), None)
    return jax.shard_map(
        on_device, mesh=mesh, in_specs=in_specs, out_specs=out_specs, check_vma=False
    )
```

```python
import functools
import math

import jax
import jax.numpy as jnp
import numpy as np
from jax import lax
from jax.experimental import pallas as pl
from jax.experimental.pallas import tpu as pltpu
from jax.sharding import PartitionSpec as P

MESH = pl.DeviceIdType.MESH
REACH = 8
ROPE_BASE = 500000.0
NZ, NY, NX = 8, 2, 4
CHIPS = NZ * NY * NX
BLOCK = 128
HD = 128
HQ = 4
D = 8192
QW = HQ * HD
QKV = QW + 2 * HD
SHARD = 64
ORDER = (0, 1, -1, 2, -2, 3, -3, 4)
FAR = -1e30
FREQ = np.power(np.float32(ROPE_BASE), -np.arange(HD // 2, dtype=np.float32) * np.float32(2 / HD)).tolist()
W_ROWS = ((0, 384), (384, 128))


SIDE = (0, -1, 1, 2)
DIRECT = (1, 2, 1)
RELAY = (True, True, True)
Y_FIRST = (False, False, True)
PLAN = (
    (
        (("k","s"),("q","s"),),
        (("k","x",1),("k","x",2),("k","z",0,1,1),("k","z",0,-1,1),("q","x",1),("q","x",2),("q","z",0,1,1),("q","z",0,-1,1),("k","z",1,1,1),("k","z",1,-1,1),("k","x",3),("k","y",0),("k","z",2,1,1),("k","z",2,-1,1),("k","z",0,1,2),("k","z",0,-1,2),("q","z",1,1,1),("q","z",1,-1,1),("q","x",3),("q","y",0),("q","z",2,1,1),("q","z",2,-1,1),("k","z",1,-1,2),("q","z",0,1,2),("k","z",3,-1,1),("k","y",1),("k","d",0),("k","z",1,1,2),("k","z",2,-1,2),("k","z",3,1,1),("k","y",-1),("k","z",0,-1,3),("k","z",2,1,2),("k","z",0,1,3),("q","z",0,-1,2),),
        (("q","z",1,-1,2),("q","z",1,1,2),("q","z",3,-1,1),("q","y",1),("q","z",3,1,1),("q","d",0),("q","z",2,1,2),("w","s"),("q","y",-1),("k","d",1),("k","z",1,-1,3),("k","z",3,-1,2),("k","y",2),("k","z",1,1,3),("k","d",-1),("k","z",2,-1,3),("k","z",3,1,2),("k","y",-2),("k","z",2,1,3),("q","z",2,-1,2),("k","f",0),("q","z",0,-1,3),("q","z",0,1,3),("q","z",1,-1,3),("q","z",1,1,3),("q","d",1),("q","z",3,-1,2),("q","y",2),),
        (("q","z",3,1,2),("q","z",2,1,3),("w","z",0,-1,1),("q","y",-2),("w","x",1),("w","x",2),("k","z",3,-1,3),("k","y",3),("w","z",0,1,1),("q","d",-1),("k","f",1),("k","d",2),("q","z",2,-1,3),("k","z",3,1,3),("k","y",-3),("k","f",2),("k","d",-2),("q","f",0),("q","f",1),("q","z",3,-1,3),("q","y",3),("q","z",3,1,3),("q","y",-3),),
        (("q","d",2),("w","z",0,-1,2),("w","z",1,1,1),("q","d",-2),("w","z",1,-1,1),("w","x",3),("k","d",3),("w","y",0),("w","z",2,1,1),("w","z",2,-1,1),("k","d",-3),("w","z",0,1,2),("k","f",3),("k","y",4),("q","f",2),("q","f",3),("q","y",4),("q","d",3),("w","z",1,1,2),("w","z",0,-1,3),("q","d",-3),("w","z",3,1,1),("w","y",-1),("w","z",1,-1,2),("w","z",2,1,2),("w","z",3,-1,1),("w","y",1),("w","d",0),("w","z",0,1,3),("w","z",2,-1,2),("k","d",4),("w","z",1,1,3),("q","d",4),),
        (("w","z",3,1,2),("w","y",-2),("w","z",1,-1,3),),
        (("w","z",3,-1,2),("w","y",2),("w","d",-1),("w","z",2,1,3),),
        (),
        (("w","z",2,-1,3),("w","f",0),),
        (("w","d",1),("w","f",1),("w","z",3,1,3),("w","y",-3),("w","z",3,-1,3),("w","y",3),("w","d",-2),("w","f",2),("w","d",2),("w","f",3),("w","y",4),),
        (),
        (),
        (("w","d",-3),),
        (),
        (("w","d",3),),
        (),
        (("w","d",4),),
        (),
        (),
    ),
    (
        (("k","s"),("q","s"),),
        (("k","y",0),("k","z",-1),("k","z",1),("q","y",0),("q","z",-1),("q","z",1),("q","z",-2),("k","r",0,-1),("k","r",0,1),("k","y",-1),("k","y",1),("k","z",-2),("k","z",2),("q","r",0,1),("q","r",0,-1),("q","z",2),("q","y",1),("q","y",-1),("k","d",0),("k","y",-2),("k","r",-1,1),("k","y",2),("k","z",3),("k","r",1,1),("k","r",1,-1),("k","r",-1,-1),("k","z",-3),),
        (("q","d",0),("q","z",-3),("q","y",2),("w","s"),("k","r",-2,1),("k","r",-2,-1),("k","y",3),("k","y",-3),("k","r",2,-1),("k","r",2,1),("k","z",4),("k","d",1),("k","d",-1),),
        (("q","r",1,1),("q","r",1,-1),("q","r",-1,1),("q","r",-1,-1),("q","r",2,1),("w","v",1,0),("q","r",2,-1),("w","y",0),("w","p",0),("q","z",3),("w","v",-1,0),("k","d",-2),("k","r",3,1),("k","r",3,-1),("q","y",-2),("k","r",-3,1),("k","r",-3,-1),("k","y",4),("k","d",2),("q","y",-3),),
        (("q","d",1),("q","d",-1),("w","v",2,0),("q","d",2),("w","r",0,1),("w","r",0,-1),("w","v",-1,1),("w","p",-1),("q","y",3),("w","v",1,1),("w","p",1),("q","z",4),("k","d",3),("w","v",-2,0),("q","r",-2,1),("q","r",-2,-1),("k","d",-3),("k","r",4,1),("k","r",4,-1),("q","r",-3,1),("w","v",3,0),("q","r",-3,-1),("w","d",0),("w","r",-1,1),("w","r",-1,-1),("q","r",3,1),("q","r",3,-1),("w","r",1,1),("w","v",-2,1),("w","r",1,-1),("w","p",-2),("q","y",4),("w","v",-3,0),("w","v",2,1),("w","p",2),("q","d",-2),("k","d",4),),
        (),
        (("w","d",-1),("q","d",-3),),
        (),
        (("w","r",-2,-1),("w","v",-3,1),("w","r",-2,1),("w","d",1),("w","p",-3),("q","d",3),("q","r",4,1),("w","v",3,1),("w","v",4,0),("w","p",3),("q","r",4,-1),),
        (("w","r",2,1),("w","r",2,-1),("w","v",4,1),("w","p",4),("w","r",-3,1),("w","r",-3,-1),("w","d",-2),("w","r",3,-1),),
        (("w","r",3,1),("q","d",4),),
        (("w","d",2),),
        (("w","r",4,1),("w","r",4,-1),("w","d",-3),),
        (("w","d",3),),
        (),
        (),
        (("w","d",4),),
        (),
        (),
    ),
)


class Gather:
    def __init__(self, direct, relay, y_first, place, ssem, rsem, sib_r, slot, most):
        self.direct, self.relay, self.y_first, self.place = direct, relay, y_first, place
        self.ssem, self.rsem, self.sib_r = ssem, rsem, sib_r
        self.slot, self.most = slot, most
        self.keys = ({}, {})

    def copy(self, ref, sem, device):
        return pltpu.make_async_remote_copy(
            src_ref=ref, dst_ref=ref, send_sem=self.ssem, recv_sem=sem, device_id=device, device_id_type=MESH)

    def sem(self, core, key):
        table = self.keys[core]
        return self.rsem.at[table.setdefault(key, len(table))]

    def send(self, core, where, key, move):
        self.copy(self.slot(core, *where), self.sem(core, key), self.place.at(*move)).start()

    def recv(self, core, where, key):
        self.copy(self.slot(core, *where), self.sem(core, key), self.place.sibling()).wait_recv()

    def sib(self, core, zr, part):
        where = (zr, part, None, None) if core == 0 else (zr, None, part, None)
        self.copy(self.slot(core, *where), self.sib_r.at[(zr + NZ) % NZ], self.place.sibling()).start()

    def sib_recv(self, core, zr):
        index = (zr + NZ) % NZ
        self.copy(self.slot(core, zr, None, None, None), self.sib_r.at[index], self.place.sibling()).wait_recv()

    def drain(self, core):
        for ref in self.most(core):
            self.copy(ref, self.sib_r.at[0], self.place.sibling()).wait_send()

    def a_s(self):
        for step in (1, -1) if self.relay else (1, -1, 2):
            self.send(0, (0, 0, 0, None), ("X", step), (0, 0, step))
        self.a_up(0)

    def a_up(self, j):
        for way in (1, -1):
            self.send(0, (0, 0, SIDE[j], None), ("Z", j, way, 1), (way, 0, 0))

    def a_x(self, j):
        self.recv(0, (0, 0, SIDE[j], None), ("X", -SIDE[j] if j < 3 else 2))
        if self.relay and j < 3:
            self.send(0, (0, 0, SIDE[j], j - 1), ("X", 2), (0, 0, -SIDE[j]))
        self.a_up(j)

    def a_z(self, j, way, s):
        self.recv(0, (-way * s, 0, SIDE[j], None), ("Z", j, way, s))
        if s < 3:
            self.send(0, (-way * s, 0, SIDE[j], None), ("Z", j, way, s + 1), (way, 0, 0))
        else:
            self.send(0, (-way * s, 0, SIDE[j], (1 - way) // 2), ("Z", j), (way, 0, 0))

    def a_f(self, j):
        self.recv(0, (4, 0, SIDE[j], None), ("Z", j))

    def a_y(self, zr):
        for way in (1, -1):
            self.send(0, (zr, 0, None, (1 - way) // 2), ("Y", zr), (0, way, 0))
        self.sib(0, zr, 0)

    def a_d(self, zr):
        self.recv(0, (zr, 1, None, None), ("Y", zr))
        self.sib(0, zr, 1)

    def b_s(self):
        self.b_fan(0, 0)
        self.b_up(0)
        self.b_cross(0)

    def b_up(self, yr):
        for far in range(1, self.direct + 1):
            for way in (1, -1):
                self.send(1, (0, yr, 0, None), ("Z", way, far, yr), (way * far, 0, 0))

    def b_fan(self, zr, yr):
        for way in (1, -1):
            self.send(1, (zr, yr, 0, None), ("X", zr, way), (0, 0, way))

    def b_cross(self, zr):
        for way in (1, -1):
            self.send(1, (zr, 0, 0, (1 - way) // 2), ("Y", zr), (0, way, 0))

    def b_v(self, zr, yr):
        if zr == 4:
            self.recv(1, (4, yr, 0, None), ("Z", 4, yr))
        else:
            way, far = (-1 if zr > 0 else 1), abs(zr)
            self.recv(1, (zr, yr, 0, None), ("Z", way, far, yr))
            if far == 3:
                self.send(1, (zr, yr, 0, (1 - way) // 2), ("Z", 4, yr), (way, 0, 0))
            elif far + 1 > self.direct:
                self.send(1, (zr, yr, 0, None), ("Z", way, far + 1, yr), (way, 0, 0))
        self.b_fan(zr, yr)

    def b_z(self, zr):
        self.b_v(zr, 0)
        self.b_cross(zr)

    def b_y(self, zr):
        self.recv(1, (zr, 1, 0, None), ("Y", zr))
        self.b_fan(zr, 1)
        if self.y_first:
            self.b_up(1)
        else:
            self.b_p(zr)

    def b_p(self, zr):
        self.sib(1, zr, 0)

    def b_r(self, zr, way):
        self.recv(1, (zr, None, -way, None), ("X", zr, way))
        self.send(1, (zr, None, -way, (1 - way) // 2), ("XR", zr), (0, 0, way))
        self.sib(1, zr, -way)

    def b_d(self, zr):
        self.recv(1, (zr, None, 2, None), ("XR", zr))
        self.sib(1, zr, 2)


class Place:
    def __init__(self):
        ctx, dp = lax.axis_index("ctx"), lax.axis_index("dp")
        self.ctx, self.dp = ctx, dp
        self.c = ctx % 2
        self.k = ctx // 2
        self.x = self.k % NX
        self.yl = (self.k // NX) % NY
        self.z = self.k // (NX * NY)
        self.y = dp * 2 + self.yl

    def zi(self, zr):
        return (self.z + (zr + NZ)) % NZ

    def yi(self, yr):
        return (self.yl + yr) % NY

    def xi(self, xr):
        return (self.x + (xr + NX)) % NX

    def at(self, dz, dy, dx):
        y = (self.y + (dy + 4)) % 4
        chip = (self.zi(dz) * NY + y % 2) * NX + self.xi(dx)
        return {"ctx": chip * 2 + self.c, "dp": y // 2}

    def sibling(self):
        return {"ctx": self.k * 2 + (1 - self.c), "dp": self.dp}

    def on(self, chip, core):
        return {"ctx": chip * 2 + core, "dp": self.dp}


def kernel(hid_hbm, seg_hbm, packed, out_hbm,
           hid, seg, kbuf, qbuf, wbuf, wo_in, wo_sib, acc, cos_t, sin_t, bias, qrot, kvw, mixed, outv,
           load_sem, out_sem, wo_s, wo_r, k_s, k_r, ks_r, q_s, q_r, qs_r, w_s, w_r, ws_r,
           kv_s, kv_r, kvs_s, kvs_r):
    me = Place()
    c, k, i = me.c, me.k, me.ctx

    def chips(zr, yr, xr):
        every = slice(None)
        return me.zi(zr), every if yr is None else me.yi(yr), every if xr is None else me.xi(xr)

    def rows_of(buf):
        def slot(core, zr, yr, xr, half):
            rows = pl.ds(0, SHARD) if half is None else pl.ds(half * (SHARD // 2), SHARD // 2)
            return buf.at[*chips(zr, yr, xr), core, rows, :]

        def most(core):
            return (buf.at[:, :, :, core], buf.at[0:NZ - 1, :, :, core],
                    buf.at[NZ - 1, 0, :, core], buf.at[NZ - 1, 1, 0:NX - 1, core])

        return slot, most

    def w_slot(core, zr, yr, xr, half):
        first, count = W_ROWS[core]
        rows = pl.ds(first, count) if half is None else pl.ds(first + half * (count // 2), count // 2)
        return wbuf.at[*chips(zr, yr, xr), rows, :]

    def w_most(core):
        rows = pl.ds(*W_ROWS[core])
        return (wbuf.at[:, :, :, rows], wbuf.at[0:NZ - 1, :, :, rows],
                wbuf.at[NZ - 1, 0, :, rows], wbuf.at[NZ - 1, 1, 0:NX - 1, rows])

    gk = Gather(DIRECT[0], RELAY[0], Y_FIRST[0], me, k_s, k_r, ks_r, *rows_of(kbuf))
    gq = Gather(DIRECT[1], RELAY[1], Y_FIRST[1], me, q_s, q_r, qs_r, *rows_of(qbuf))
    gw = Gather(DIRECT[2], RELAY[2], Y_FIRST[2], me, w_s, w_r, ws_r, w_slot, w_most)

    def both(first, second):
        pl.when(c == 0)(first)
        pl.when(c == 1)(second)

    own_k, own_q = kbuf.at[me.z, me.yl, me.x, c], qbuf.at[me.z, me.yl, me.x, c]
    loads = [
        pltpu.make_async_copy(packed.at[:, pl.ds(0, 2 * HD)], own_k, load_sem.at[0]),
        pltpu.make_async_copy(packed.at[:, pl.ds(2 * HD, QW)], own_q, load_sem.at[1]),
        pltpu.make_async_copy(packed.at[:, pl.ds(QKV, QW)], wo_in, load_sem.at[2]),
        pltpu.make_async_copy(seg_hbm, seg, load_sem.at[3]),
        pltpu.make_async_copy(hid_hbm, hid, load_sem.at[4]),
    ]
    for load in loads:
        load.start()

    kvw[0, 0:REACH] = jnp.zeros((REACH, BLOCK, 2 * HD), jnp.bfloat16)

    def up(m):
        over = k + m >= CHIPS
        return (jnp.where(over, 2 * CHIPS - 1 - k - m, k + m), jnp.where(over, 1 - c, c))

    barrier = pltpu.get_barrier_semaphore()

    def greet(device):
        pl.semaphore_signal(barrier, inc=1, device_id=device, device_id_type=MESH)

    moves = [(0, 0, 1), (0, 0, -1), (0, 1, 0), (0, -1, 0)]
    moves += [(way * far, 0, 0) for far in range(1, max(DIRECT) + 1) for way in (1, -1)]
    for move in moves:
        greet(me.at(*move))
    greet(me.sibling())
    for m in range(1, 5):
        greet(me.on(*up(m)))
        pl.when(k >= m)(lambda m=m: greet(me.on(k - m, c)))
    pl.semaphore_wait(barrier, len(moves) + 5 + jnp.minimum(k, 4))

    for load in loads[:2]:
        load.wait()

    gathers = {"k": gk, "q": gq, "w": gw}

    def run(step):
        def core(which):
            for op in PLAN[which][step]:
                if op[:2] == ("w", "s"):
                    join(which)
                getattr(gathers[op[0]], "ab"[which] + "_" + op[1])(*op[2:])

        both(lambda: core(0), lambda: core(1))

    wo_copy = pltpu.make_async_remote_copy(
        src_ref=wo_in, dst_ref=wo_sib, send_sem=wo_s, recv_sem=wo_r,
        device_id=me.sibling(), device_id_type=MESH)

    def join(core):
        wo_copy.wait()
        rows = pl.ds(*W_ROWS[core])
        pair = [wo_in[:, rows], wo_sib[:, rows]]
        block = jnp.concatenate(pair if core == 0 else pair[::-1], axis=0)
        wbuf[me.z, me.yl, me.x, rows, :] = jnp.transpose(block)

    run(0)
    loads[2].wait()
    wo_copy.start()
    wave = lax.broadcasted_iota(jnp.int32, (1, HD), 1) % (HD // 2)
    freq = jnp.zeros((1, HD), jnp.float32)
    for j in range(HD // 2):
        freq = jnp.where(wave == j, FREQ[j], freq)
    row = lax.broadcasted_iota(jnp.int32, (BLOCK, HD), 0)
    lane = lax.broadcasted_iota(jnp.int32, (BLOCK, HD), 1)
    late = 2 * 2 * CHIPS - 1 - i
    for b, block in enumerate((i, late)):
        angle = (block * BLOCK + row).astype(jnp.float32) * freq
        cos_t[b] = jnp.cos(angle)
        sine = jnp.sin(angle)
        sin_t[b] = jnp.where(lane < HD // 2, -sine, sine)

    loads[3].wait()
    for b in range(2):
        mine = seg[pl.ds(2 * i + b, 1), :]
        asks = jnp.transpose(jnp.broadcast_to(mine, (BLOCK, BLOCK)))
        for j in range(REACH + 1):
            if b == 0:
                block = i - REACH + j
                keys = seg[pl.ds(2 * jnp.maximum(block, 0), 1), :]
                keys = jnp.where(block >= 0, keys, -1)
            else:
                over = i + j >= 2 * CHIPS
                keys = seg[pl.ds(jnp.where(over, 2 * (4 * CHIPS - 1 - i - j), 2 * (i + j) + 1), 1), :]
            allowed = asks == keys
            if j == (REACH if b == 0 else 0):
                allowed = allowed & (lane <= row)
            bias[b, :, j * BLOCK:(j + 1) * BLOCK] = jnp.where(allowed, 0.0, FAR)

    loads[4].wait()
    acc[...] = jnp.zeros_like(acc)

    part = NY * NX * 2 * SHARD
    edges = (0, 1, 3, 5, 8)

    def project(gather, buf, first, last, columns):
        @pl.loop(first, last)
        def _(t):
            zr = ((t + 1) // 2) * (2 * (t % 2) - 1)
            zz = (me.z + zr + NZ) % NZ
            both(lambda: gather.sib_recv(1, zr), lambda: gather.sib_recv(0, zr))
            weights = buf[zz].reshape(part, buf.shape[-1])
            acc[:, columns] += jnp.dot(hid[:, pl.ds(pl.multiple_of(zz * part, part), part)], weights,
                                       preferred_element_type=jnp.float32)

    def rotated(b, h):
        piece = acc[b * BLOCK:(b + 1) * BLOCK, h * HD:(h + 1) * HD]
        return (piece * cos_t[b] + pltpu.roll(piece, HD // 2, 1) * sin_t[b]).astype(jnp.bfloat16)

    for n in range(4):
        run(1 + n)
        project(gk, kbuf, edges[n], edges[n + 1], slice(QW, QKV))
    run(5)
    for b in range(2):
        slot = REACH + c if b == 0 else c
        kvw[b, slot, :, 0:HD] = rotated(b, HQ)
        kvw[b, slot, :, HD:2 * HD] = acc[b * BLOCK:(b + 1) * BLOCK, QW + HD:QKV].astype(jnp.bfloat16)

    def kv_copy(src, dst, sent, got, device):
        return pltpu.make_async_remote_copy(
            src_ref=src, dst_ref=dst, send_sem=sent, recv_sem=got, device_id=device, device_id_type=MESH)

    early_own, late_own = kvw.at[0, REACH + c], kvw.at[1, c]

    def kv_up(m):
        return kv_copy(early_own, kvw.at[0, REACH - 2 * m + c], kv_s.at[0, m], kv_r.at[0, m], me.on(k + m, c))

    def kv_over(m):
        return kv_copy(early_own, kvw.at[1, 2 * m + 1 - c], kv_s.at[0, m], kv_r.at[1, m],
                       me.on(2 * CHIPS - 1 - k - m, 1 - c))

    def kv_down(m):
        return kv_copy(late_own, kvw.at[1, 2 * m + c], kv_s.at[1, m], kv_r.at[1, m], me.on(k - m, c))

    def kv_side(b, m, core):
        ref = kvw.at[0, REACH - 2 * m + core] if b == 0 else kvw.at[1, 2 * m + core]
        return kv_copy(ref, ref, kvs_s.at[b, m], kvs_r.at[b, m], me.sibling())

    for m in range(4, 0, -1):
        pl.when(k + m < CHIPS)(lambda m=m: kv_up(m).start())
        pl.when(k + m >= CHIPS)(lambda m=m: kv_over(m).start())
        pl.when(k >= m)(lambda m=m: kv_down(m).start())
    for b in range(2):
        kv_side(b, 0, c).start()

    for n in range(3):
        run(6 + n)
        project(gq, qbuf, edges[n], edges[n + 1], slice(0, QW))
    run(9)

    for m in range(1, 5):
        def early_in(m=m):
            kv_copy(early_own, kvw.at[0, REACH - 2 * m + c], kv_s.at[0, m], kv_r.at[0, m], me.sibling()).wait_recv()
            kv_side(0, m, c).start()

        pl.when(k >= m)(early_in)
        kv_copy(late_own, kvw.at[1, 2 * m + c], kv_s.at[1, m], kv_r.at[1, m], me.sibling()).wait_recv()
        kv_side(1, m, c).start()

    run(10)
    project(gq, qbuf, edges[3], edges[4], slice(0, QW))
    run(11)
    for b in range(2):
        for h in range(HQ):
            qrot[b, h] = rotated(b, h)
    run(12)

    def attend(b, first):
        window = kvw.at[b, pl.ds(c, REACH + 1)]
        span = (REACH + 1) * BLOCK
        keys = window[:, :, 0:HD].reshape(span, HD)
        values = window[:, :, HD:2 * HD].reshape(span, HD)
        scale = math.log2(math.e) / math.sqrt(HD)
        scores = lax.dot_general(qrot[b, first:first + 2].reshape(2 * BLOCK, HD), keys, (((1,), (1,)), ((), ())),
                                 preferred_element_type=jnp.float32)
        scores = scores.reshape(2, BLOCK, span) * scale + bias[b][None]
        scores = scores.reshape(2 * BLOCK, span)
        peak = jnp.max(scores, axis=1, keepdims=True)
        terms = jnp.exp2(scores - peak)
        total = jnp.sum(terms, axis=1, keepdims=True)
        result = jnp.dot(terms.astype(jnp.bfloat16), values, preferred_element_type=jnp.float32)
        result = (result * (1.0 / total)).astype(jnp.bfloat16)
        for h in range(2):
            columns = slice((first + h) * HD, (first + h + 1) * HD)
            mixed[b * BLOCK:(b + 1) * BLOCK, columns] = result[h * BLOCK:(h + 1) * BLOCK]

    for m in range(0, 5):
        pl.when(k >= m)(lambda m=m: kv_side(0, m, 1 - c).wait_recv())
        kv_side(1, m, 1 - c).wait_recv()
    attend(0, 0)
    for n in range(1, 4):
        run(12 + n)
        attend(n // 2, 2 * (n % 2))


    def out_copy(t):
        zr = ((t + 1) // 2) * (2 * (t % 2) - 1)
        zz = (me.z + zr + NZ) % NZ
        columns = pl.ds(pl.multiple_of(zz * part, part), part)
        return pltpu.make_async_copy(outv.at[:, columns], out_hbm.at[:, columns], out_sem.at[t])

    def emit(t):
        zr = ((t + 1) // 2) * (2 * (t % 2) - 1)
        zz = (me.z + zr + NZ) % NZ
        both(lambda: gw.sib_recv(1, zr), lambda: gw.sib_recv(0, zr))
        for pair in range(NY * NX // 2):
            y, x = pair // 2, (pair % 2) * 2
            weights = jnp.concatenate([wbuf[zz, y, x], wbuf[zz, y, x + 1]], axis=1)
            result = jnp.dot(mixed[...], weights, preferred_element_type=jnp.float32)
            start = pl.multiple_of(zz * part + pair * 2 * BLOCK, 2 * BLOCK)
            outv[:, pl.ds(start, 2 * BLOCK)] = result.astype(jnp.bfloat16)
        out_copy(t).start()

    for n in range(3):
        run(16 + n)
        pl.loop(edges[n + 1] if n else 0, edges[n + 2])(emit)

    def finish(core):
        gk.drain(core)
        gq.drain(core)
        gw.drain(core)

    both(lambda: finish(0), lambda: finish(1))
    for m in range(1, 5):
        kv_copy(early_own, early_own, kv_s.at[0, m], kv_r.at[0, m], me.sibling()).wait_send()
        pl.when(k >= m)(lambda m=m: kv_down(m).wait_send())
    for m in range(0, 5):
        pl.when(k >= m)(lambda m=m: kv_side(0, m, c).wait_send())
        kv_side(1, m, c).wait_send()

    @pl.loop(0, NZ)
    def _(t):
        out_copy(t).wait()


def on_device(hidden_in, segment_ids, w_query, w_key, w_value, w_out):
    seg = segment_ids.reshape(4 * CHIPS, BLOCK)
    rows = hidden_in.shape[0]
    anywhere = pl.BlockSpec(memory_space=pl.ANY)
    dma = pltpu.SemaphoreType.DMA
    bf16, f32 = jnp.bfloat16, jnp.float32
    return pl.pallas_call(
        kernel,
        out_shape=jax.ShapeDtypeStruct((rows, D), bf16),
        in_specs=[anywhere] * 3,
        out_specs=anywhere,
        scratch_shapes=[
            pltpu.VMEM((rows, D), bf16),
            pltpu.VMEM((4 * CHIPS, BLOCK), jnp.int32),
            pltpu.VMEM((NZ, NY, NX, 2, SHARD, 2 * HD), bf16),
            pltpu.VMEM((NZ, NY, NX, 2, SHARD, QW), bf16),
            pltpu.VMEM((NZ, NY, NX, QW, BLOCK), bf16),
            pltpu.VMEM((SHARD, QW), bf16),
            pltpu.VMEM((SHARD, QW), bf16),
            pltpu.VMEM((rows, QKV), f32),
            pltpu.VMEM((2, BLOCK, HD), f32),
            pltpu.VMEM((2, BLOCK, HD), f32),
            pltpu.VMEM((2, BLOCK, (REACH + 1) * BLOCK), f32),
            pltpu.VMEM((2, HQ, BLOCK, HD), bf16),
            pltpu.VMEM((2, REACH + 2, BLOCK, 2 * HD), bf16),
            pltpu.VMEM((rows, QW), bf16),
            pltpu.VMEM((rows, D), bf16),
            dma((5,)), dma((NZ,)), dma, dma,
            dma, dma((40,)), dma((NZ,)),
            dma, dma((40,)), dma((NZ,)),
            dma, dma((40,)), dma((NZ,)),
            dma((2, 5)), dma((2, 5)), dma((2, 5)), dma((2, 5)),
        ],
        compiler_params=pltpu.CompilerParams(
            collective_id=1, has_side_effects=True, vmem_limit_bytes=48 * 2**20),
        name="layer",
    )(hidden_in, seg, jnp.concatenate([w_key, w_value, w_query, w_out.T], axis=1))


def solution(mesh):
    in_specs = (
        P(("dp", "ctx"), None),
        P("dp"),
        P("ctx", None),
        P("ctx", None),
        P("ctx", None),
        P(None, "ctx"),
    )
    out_specs = P(("dp", "ctx"), None)
    return jax.shard_map(
        on_device, mesh=mesh, in_specs=in_specs, out_specs=out_specs, check_vma=False
    )
```

```python
import functools
import math

import jax
import jax.numpy as jnp
import numpy as np
from jax import lax
from jax.experimental import pallas as pl
from jax.experimental.pallas import tpu as pltpu
from jax.sharding import PartitionSpec as P

MESH = pl.DeviceIdType.MESH
REACH = 8
ROPE_BASE = 500000.0
NZ, NY, NX = 8, 2, 4
CHIPS = NZ * NY * NX
BLOCK = 128
HD = 128
HQ = 4
D = 8192
QW = HQ * HD
QKV = QW + 2 * HD
SHARD = 64
ORDER = (0, 1, -1, 2, -2, 3, -3, 4)
FAR = -1e30
FREQ = np.power(np.float32(ROPE_BASE), -np.arange(HD // 2, dtype=np.float32) * np.float32(2 / HD)).tolist()
W_ROWS = ((0, 384), (384, 128))


SIDE = (0, -1, 1, 2)
DIRECT = (1, 2, 1)
RELAY = (True, True, True)
Y_FIRST = (False, False, True)
PLAN = (
    (
        (("k","s"),("q","s"),),
        (("k","x",1),("k","x",2),("k","z",0,1,1),("k","z",0,-1,1),("q","x",1),("q","x",2),("q","z",0,1,1),("q","z",0,-1,1),("k","z",1,1,1),("k","z",1,-1,1),("k","x",3),("k","y",0),("k","z",2,1,1),("k","z",2,-1,1),("k","z",0,1,2),("k","z",0,-1,2),("q","z",1,1,1),("q","z",1,-1,1),("q","x",3),("q","y",0),("q","z",2,1,1),("q","z",2,-1,1),("k","z",1,-1,2),("q","z",0,1,2),("k","z",3,-1,1),("k","y",1),("k","d",0),("k","z",1,1,2),("k","z",2,-1,2),("k","z",3,1,1),("k","y",-1),("k","z",0,-1,3),("k","z",2,1,2),("k","z",0,1,3),("q","z",0,-1,2),),
        (("q","z",1,-1,2),("q","z",1,1,2),("q","z",3,-1,1),("q","y",1),("q","z",3,1,1),("q","d",0),("q","z",2,1,2),("w","s"),("q","y",-1),("k","d",1),("k","z",1,-1,3),("k","z",3,-1,2),("k","y",2),("k","z",1,1,3),("k","d",-1),("k","z",2,-1,3),("k","z",3,1,2),("k","y",-2),("k","z",2,1,3),("q","z",2,-1,2),("k","f",0),("q","z",0,-1,3),("q","z",0,1,3),("q","z",1,-1,3),("q","z",1,1,3),("q","d",1),("q","z",3,-1,2),("q","y",2),),
        (("q","z",3,1,2),("q","z",2,1,3),("w","z",0,-1,1),("q","y",-2),("w","x",1),("w","x",2),("k","z",3,-1,3),("k","y",3),("w","z",0,1,1),("q","d",-1),("k","f",1),("k","d",2),("q","z",2,-1,3),("k","z",3,1,3),("k","y",-3),("k","f",2),("k","d",-2),("q","f",0),("q","f",1),("q","z",3,-1,3),("q","y",3),("q","z",3,1,3),("q","y",-3),),
        (("q","d",2),("w","z",0,-1,2),("w","z",1,1,1),("q","d",-2),("w","z",1,-1,1),("w","x",3),("k","d",3),("w","y",0),("w","z",2,1,1),("w","z",2,-1,1),("k","d",-3),("w","z",0,1,2),("k","f",3),("k","y",4),("q","f",2),("q","f",3),("q","y",4),("q","d",3),("w","z",1,1,2),("w","z",0,-1,3),("q","d",-3),("w","z",3,1,1),("w","y",-1),("w","z",1,-1,2),("w","z",2,1,2),("w","z",3,-1,1),("w","y",1),("w","d",0),("w","z",0,1,3),("w","z",2,-1,2),("k","d",4),("w","z",1,1,3),("q","d",4),),
        (("w","z",3,1,2),("w","y",-2),("w","z",1,-1,3),),
        (("w","z",3,-1,2),("w","y",2),("w","d",-1),("w","z",2,1,3),),
        (),
        (("w","z",2,-1,3),("w","f",0),),
        (("w","d",1),("w","f",1),("w","z",3,1,3),("w","y",-3),("w","z",3,-1,3),("w","y",3),("w","d",-2),("w","f",2),("w","d",2),("w","f",3),("w","y",4),),
        (),
        (),
        (("w","d",-3),),
        (),
        (("w","d",3),),
        (),
        (("w","d",4),),
        (),
        (),
    ),
    (
        (("k","s"),("q","s"),),
        (("k","y",0),("k","z",-1),("k","z",1),("q","y",0),("q","z",-1),("q","z",1),("q","z",-2),("k","r",0,-1),("k","r",0,1),("k","y",-1),("k","y",1),("k","z",-2),("k","z",2),("q","r",0,1),("q","r",0,-1),("q","z",2),("q","y",1),("q","y",-1),("k","d",0),("k","y",-2),("k","r",-1,1),("k","y",2),("k","z",3),("k","r",1,1),("k","r",1,-1),("k","r",-1,-1),("k","z",-3),),
        (("q","d",0),("q","z",-3),("q","y",2),("w","s"),("k","r",-2,1),("k","r",-2,-1),("k","y",3),("k","y",-3),("k","r",2,-1),("k","r",2,1),("k","z",4),("k","d",1),("k","d",-1),),
        (("q","r",1,1),("q","r",1,-1),("q","r",-1,1),("q","r",-1,-1),("q","r",2,1),("w","v",1,0),("q","r",2,-1),("w","y",0),("w","p",0),("q","z",3),("w","v",-1,0),("k","d",-2),("k","r",3,1),("k","r",3,-1),("q","y",-2),("k","r",-3,1),("k","r",-3,-1),("k","y",4),("k","d",2),("q","y",-3),),
        (("q","d",1),("q","d",-1),("w","v",2,0),("q","d",2),("w","r",0,1),("w","r",0,-1),("w","v",-1,1),("w","p",-1),("q","y",3),("w","v",1,1),("w","p",1),("q","z",4),("k","d",3),("w","v",-2,0),("q","r",-2,1),("q","r",-2,-1),("k","d",-3),("k","r",4,1),("k","r",4,-1),("q","r",-3,1),("w","v",3,0),("q","r",-3,-1),("w","d",0),("w","r",-1,1),("w","r",-1,-1),("q","r",3,1),("q","r",3,-1),("w","r",1,1),("w","v",-2,1),("w","r",1,-1),("w","p",-2),("q","y",4),("w","v",-3,0),("w","v",2,1),("w","p",2),("q","d",-2),("k","d",4),),
        (),
        (("w","d",-1),("q","d",-3),),
        (),
        (("w","r",-2,-1),("w","v",-3,1),("w","r",-2,1),("w","d",1),("w","p",-3),("q","d",3),("q","r",4,1),("w","v",3,1),("w","v",4,0),("w","p",3),("q","r",4,-1),),
        (("w","r",2,1),("w","r",2,-1),("w","v",4,1),("w","p",4),("w","r",-3,1),("w","r",-3,-1),("w","d",-2),("w","r",3,-1),),
        (("w","r",3,1),("q","d",4),),
        (("w","d",2),),
        (("w","r",4,1),("w","r",4,-1),("w","d",-3),),
        (("w","d",3),),
        (),
        (),
        (("w","d",4),),
        (),
        (),
    ),
)


class Gather:
    def __init__(self, direct, relay, y_first, place, ssem, rsem, sib_r, slot, most):
        self.direct, self.relay, self.y_first, self.place = direct, relay, y_first, place
        self.ssem, self.rsem, self.sib_r = ssem, rsem, sib_r
        self.slot, self.most = slot, most
        self.keys = ({}, {})

    def copy(self, ref, sem, device):
        return pltpu.make_async_remote_copy(
            src_ref=ref, dst_ref=ref, send_sem=self.ssem, recv_sem=sem, device_id=device, device_id_type=MESH)

    def sem(self, core, key):
        table = self.keys[core]
        return self.rsem.at[table.setdefault(key, len(table))]

    def send(self, core, where, key, move):
        self.copy(self.slot(core, *where), self.sem(core, key), self.place.at(*move)).start()

    def recv(self, core, where, key):
        self.copy(self.slot(core, *where), self.sem(core, key), self.place.sibling()).wait_recv()

    def sib(self, core, zr, part):
        where = (zr, part, None, None) if core == 0 else (zr, None, part, None)
        self.copy(self.slot(core, *where), self.sib_r.at[(zr + NZ) % NZ], self.place.sibling()).start()

    def sib_recv(self, core, zr):
        index = (zr + NZ) % NZ
        self.copy(self.slot(core, zr, None, None, None), self.sib_r.at[index], self.place.sibling()).wait_recv()

    def drain(self, core):
        for ref in self.most(core):
            self.copy(ref, self.sib_r.at[0], self.place.sibling()).wait_send()

    def a_s(self):
        for step in (1, -1) if self.relay else (1, -1, 2):
            self.send(0, (0, 0, 0, None), ("X", step), (0, 0, step))
        self.a_up(0)

    def a_up(self, j):
        for way in (1, -1):
            self.send(0, (0, 0, SIDE[j], None), ("Z", j, way, 1), (way, 0, 0))

    def a_x(self, j):
        self.recv(0, (0, 0, SIDE[j], None), ("X", -SIDE[j] if j < 3 else 2))
        if self.relay and j < 3:
            self.send(0, (0, 0, SIDE[j], j - 1), ("X", 2), (0, 0, -SIDE[j]))
        self.a_up(j)

    def a_z(self, j, way, s):
        self.recv(0, (-way * s, 0, SIDE[j], None), ("Z", j, way, s))
        if s < 3:
            self.send(0, (-way * s, 0, SIDE[j], None), ("Z", j, way, s + 1), (way, 0, 0))
        else:
            self.send(0, (-way * s, 0, SIDE[j], (1 - way) // 2), ("Z", j), (way, 0, 0))

    def a_f(self, j):
        self.recv(0, (4, 0, SIDE[j], None), ("Z", j))

    def a_y(self, zr):
        for way in (1, -1):
            self.send(0, (zr, 0, None, (1 - way) // 2), ("Y", zr), (0, way, 0))
        self.sib(0, zr, 0)

    def a_d(self, zr):
        self.recv(0, (zr, 1, None, None), ("Y", zr))
        self.sib(0, zr, 1)

    def b_s(self):
        self.b_fan(0, 0)
        self.b_up(0)
        self.b_cross(0)

    def b_up(self, yr):
        for far in range(1, self.direct + 1):
            for way in (1, -1):
                self.send(1, (0, yr, 0, None), ("Z", way, far, yr), (way * far, 0, 0))

    def b_fan(self, zr, yr):
        for way in (1, -1):
            self.send(1, (zr, yr, 0, None), ("X", zr, way), (0, 0, way))

    def b_cross(self, zr):
        for way in (1, -1):
            self.send(1, (zr, 0, 0, (1 - way) // 2), ("Y", zr), (0, way, 0))

    def b_v(self, zr, yr):
        if zr == 4:
            self.recv(1, (4, yr, 0, None), ("Z", 4, yr))
        else:
            way, far = (-1 if zr > 0 else 1), abs(zr)
            self.recv(1, (zr, yr, 0, None), ("Z", way, far, yr))
            if far == 3:
                self.send(1, (zr, yr, 0, (1 - way) // 2), ("Z", 4, yr), (way, 0, 0))
            elif far + 1 > self.direct:
                self.send(1, (zr, yr, 0, None), ("Z", way, far + 1, yr), (way, 0, 0))
        self.b_fan(zr, yr)

    def b_z(self, zr):
        self.b_v(zr, 0)
        self.b_cross(zr)

    def b_y(self, zr):
        self.recv(1, (zr, 1, 0, None), ("Y", zr))
        self.b_fan(zr, 1)
        if self.y_first:
            self.b_up(1)
        else:
            self.b_p(zr)

    def b_p(self, zr):
        self.sib(1, zr, 0)

    def b_r(self, zr, way):
        self.recv(1, (zr, None, -way, None), ("X", zr, way))
        self.send(1, (zr, None, -way, (1 - way) // 2), ("XR", zr), (0, 0, way))
        self.sib(1, zr, -way)

    def b_d(self, zr):
        self.recv(1, (zr, None, 2, None), ("XR", zr))
        self.sib(1, zr, 2)


class Place:
    def __init__(self):
        ctx, dp = lax.axis_index("ctx"), lax.axis_index("dp")
        self.ctx, self.dp = ctx, dp
        self.c = ctx % 2
        self.k = ctx // 2
        self.x = self.k % NX
        self.yl = (self.k // NX) % NY
        self.z = self.k // (NX * NY)
        self.y = dp * 2 + self.yl

    def zi(self, zr):
        return (self.z + (zr + NZ)) % NZ

    def yi(self, yr):
        return (self.yl + yr) % NY

    def xi(self, xr):
        return (self.x + (xr + NX)) % NX

    def at(self, dz, dy, dx):
        y = (self.y + (dy + 4)) % 4
        chip = (self.zi(dz) * NY + y % 2) * NX + self.xi(dx)
        return {"ctx": chip * 2 + self.c, "dp": y // 2}

    def sibling(self):
        return {"ctx": self.k * 2 + (1 - self.c), "dp": self.dp}

    def on(self, chip, core):
        return {"ctx": chip * 2 + core, "dp": self.dp}


def kernel(hid_hbm, seg_hbm, packed, out_hbm,
           hid, seg, kbuf, qbuf, wbuf, wo_in, wo_sib, acc, cos_t, sin_t, bias, qrot, kvw, mixed, outv,
           load_sem, out_sem, wo_s, wo_r, k_s, k_r, ks_r, q_s, q_r, qs_r, w_s, w_r, ws_r,
           kv_s, kv_r, kvs_s, kvs_r):
    me = Place()
    c, k, i = me.c, me.k, me.ctx

    def chips(zr, yr, xr):
        every = slice(None)
        return me.zi(zr), every if yr is None else me.yi(yr), every if xr is None else me.xi(xr)

    def rows_of(buf):
        def slot(core, zr, yr, xr, half):
            rows = pl.ds(0, SHARD) if half is None else pl.ds(half * (SHARD // 2), SHARD // 2)
            return buf.at[*chips(zr, yr, xr), core, rows, :]

        def most(core):
            return (buf.at[:, :, :, core], buf.at[0:NZ - 1, :, :, core],
                    buf.at[NZ - 1, 0, :, core], buf.at[NZ - 1, 1, 0:NX - 1, core])

        return slot, most

    def w_slot(core, zr, yr, xr, half):
        first, count = W_ROWS[core]
        rows = pl.ds(first, count) if half is None else pl.ds(first + half * (count // 2), count // 2)
        return wbuf.at[*chips(zr, yr, xr), rows, :]

    def w_most(core):
        rows = pl.ds(*W_ROWS[core])
        return (wbuf.at[:, :, :, rows], wbuf.at[0:NZ - 1, :, :, rows],
                wbuf.at[NZ - 1, 0, :, rows], wbuf.at[NZ - 1, 1, 0:NX - 1, rows])

    gk = Gather(DIRECT[0], RELAY[0], Y_FIRST[0], me, k_s, k_r, ks_r, *rows_of(kbuf))
    gq = Gather(DIRECT[1], RELAY[1], Y_FIRST[1], me, q_s, q_r, qs_r, *rows_of(qbuf))
    gw = Gather(DIRECT[2], RELAY[2], Y_FIRST[2], me, w_s, w_r, ws_r, w_slot, w_most)

    def both(first, second):
        pl.when(c == 0)(first)
        pl.when(c == 1)(second)

    own_k, own_q = kbuf.at[me.z, me.yl, me.x, c], qbuf.at[me.z, me.yl, me.x, c]
    loads = [
        pltpu.make_async_copy(packed.at[:, pl.ds(0, 2 * HD)], own_k, load_sem.at[0]),
        pltpu.make_async_copy(packed.at[:, pl.ds(2 * HD, QW)], own_q, load_sem.at[1]),
        pltpu.make_async_copy(packed.at[:, pl.ds(QKV, QW)], wo_in, load_sem.at[2]),
        pltpu.make_async_copy(seg_hbm, seg, load_sem.at[3]),
        pltpu.make_async_copy(hid_hbm, hid, load_sem.at[4]),
    ]
    for load in loads:
        load.start()

    kvw[0, 0:REACH] = jnp.zeros((REACH, BLOCK, 2 * HD), jnp.bfloat16)

    def up(m):
        over = k + m >= CHIPS
        return (jnp.where(over, 2 * CHIPS - 1 - k - m, k + m), jnp.where(over, 1 - c, c))

    barrier = pltpu.get_barrier_semaphore()

    def greet(device):
        pl.semaphore_signal(barrier, inc=1, device_id=device, device_id_type=MESH)

    moves = [(0, 0, 1), (0, 0, -1), (0, 1, 0), (0, -1, 0)]
    moves += [(way * far, 0, 0) for far in range(1, max(DIRECT) + 1) for way in (1, -1)]
    for move in moves:
        greet(me.at(*move))
    greet(me.sibling())
    for m in range(1, 5):
        greet(me.on(*up(m)))
        pl.when(k >= m)(lambda m=m: greet(me.on(k - m, c)))
    pl.semaphore_wait(barrier, len(moves) + 5 + jnp.minimum(k, 4))

    for load in loads[:2]:
        load.wait()

    gathers = {"k": gk, "q": gq, "w": gw}

    def run(step):
        def core(which):
            for op in PLAN[which][step]:
                if op[:2] == ("w", "s"):
                    join(which)
                getattr(gathers[op[0]], "ab"[which] + "_" + op[1])(*op[2:])

        both(lambda: core(0), lambda: core(1))

    wo_copy = pltpu.make_async_remote_copy(
        src_ref=wo_in, dst_ref=wo_sib, send_sem=wo_s, recv_sem=wo_r,
        device_id=me.sibling(), device_id_type=MESH)

    def join(core):
        wo_copy.wait()
        rows = pl.ds(*W_ROWS[core])
        pair = [wo_in[:, rows], wo_sib[:, rows]]
        block = jnp.concatenate(pair if core == 0 else pair[::-1], axis=0)
        wbuf[me.z, me.yl, me.x, rows, :] = jnp.transpose(block)

    run(0)
    loads[2].wait()
    wo_copy.start()
    wave = lax.broadcasted_iota(jnp.int32, (1, HD), 1) % (HD // 2)
    freq = jnp.zeros((1, HD), jnp.float32)
    for j in range(HD // 2):
        freq = jnp.where(wave == j, FREQ[j], freq)
    row = lax.broadcasted_iota(jnp.int32, (BLOCK, HD), 0)
    lane = lax.broadcasted_iota(jnp.int32, (BLOCK, HD), 1)
    late = 2 * 2 * CHIPS - 1 - i
    for b, block in enumerate((i, late)):
        angle = (block * BLOCK + row).astype(jnp.float32) * freq
        cos_t[b] = jnp.cos(angle)
        sine = jnp.sin(angle)
        sin_t[b] = jnp.where(lane < HD // 2, -sine, sine)

    loads[3].wait()
    for b in range(2):
        mine = seg[pl.ds(2 * i + b, 1), :]
        asks = jnp.transpose(jnp.broadcast_to(mine, (BLOCK, BLOCK)))
        for j in range(REACH + 1):
            if b == 0:
                block = i - REACH + j
                keys = seg[pl.ds(2 * jnp.maximum(block, 0), 1), :]
                keys = jnp.where(block >= 0, keys, -1)
            else:
                over = i + j >= 2 * CHIPS
                keys = seg[pl.ds(jnp.where(over, 2 * (4 * CHIPS - 1 - i - j), 2 * (i + j) + 1), 1), :]
            allowed = asks == keys
            if j == (REACH if b == 0 else 0):
                allowed = allowed & (lane <= row)
            bias[b, :, j * BLOCK:(j + 1) * BLOCK] = jnp.where(allowed, 0.0, FAR)

    loads[4].wait()
    acc[...] = jnp.zeros_like(acc)

    part = NY * NX * 2 * SHARD
    edges = (0, 1, 3, 5, 8)

    def project(gather, buf, first, last, columns):
        @pl.loop(first, last)
        def _(t):
            zr = ((t + 1) // 2) * (2 * (t % 2) - 1)
            zz = (me.z + zr + NZ) % NZ
            both(lambda: gather.sib_recv(1, zr), lambda: gather.sib_recv(0, zr))
            weights = buf[zz].reshape(part, buf.shape[-1])
            acc[:, columns] += jnp.dot(hid[:, pl.ds(pl.multiple_of(zz * part, part), part)], weights,
                                       preferred_element_type=jnp.float32)

    def rotated(b, h):
        piece = acc[b * BLOCK:(b + 1) * BLOCK, h * HD:(h + 1) * HD]
        return (piece * cos_t[b] + pltpu.roll(piece, HD // 2, 1) * sin_t[b]).astype(jnp.bfloat16)

    for n in range(4):
        run(1 + n)
        project(gk, kbuf, edges[n], edges[n + 1], slice(QW, QKV))
    run(5)
    for b in range(2):
        slot = REACH + c if b == 0 else c
        kvw[b, slot, :, 0:HD] = rotated(b, HQ)
        kvw[b, slot, :, HD:2 * HD] = acc[b * BLOCK:(b + 1) * BLOCK, QW + HD:QKV].astype(jnp.bfloat16)

    def kv_copy(src, dst, sent, got, device):
        return pltpu.make_async_remote_copy(
            src_ref=src, dst_ref=dst, send_sem=sent, recv_sem=got, device_id=device, device_id_type=MESH)

    early_own, late_own = kvw.at[0, REACH + c], kvw.at[1, c]

    def kv_up(m):
        return kv_copy(early_own, kvw.at[0, REACH - 2 * m + c], kv_s, kv_r.at[0, m], me.on(k + m, c))

    def kv_over(m):
        return kv_copy(early_own, kvw.at[1, 2 * m + 1 - c], kv_s, kv_r.at[1, m],
                       me.on(2 * CHIPS - 1 - k - m, 1 - c))

    def kv_down(m):
        return kv_copy(late_own, kvw.at[1, 2 * m + c], kv_s, kv_r.at[1, m], me.on(k - m, c))

    def kv_side(b, m, core):
        ref = kvw.at[0, REACH - 2 * m + core] if b == 0 else kvw.at[1, 2 * m + core]
        return kv_copy(ref, ref, kvs_s, kvs_r.at[b, m], me.sibling())

    for m in range(4, 0, -1):
        pl.when(k + m < CHIPS)(lambda m=m: kv_up(m).start())
        pl.when(k + m >= CHIPS)(lambda m=m: kv_over(m).start())
        pl.when(k >= m)(lambda m=m: kv_down(m).start())
    for b in range(2):
        kv_side(b, 0, c).start()

    for n in range(3):
        run(6 + n)
        project(gq, qbuf, edges[n], edges[n + 1], slice(0, QW))
    run(9)

    for m in range(1, 5):
        def early_in(m=m):
            kv_copy(early_own, kvw.at[0, REACH - 2 * m + c], kv_s, kv_r.at[0, m], me.sibling()).wait_recv()
            kv_side(0, m, c).start()

        pl.when(k >= m)(early_in)
        kv_copy(late_own, kvw.at[1, 2 * m + c], kv_s, kv_r.at[1, m], me.sibling()).wait_recv()
        kv_side(1, m, c).start()

    run(10)
    project(gq, qbuf, edges[3], edges[4], slice(0, QW))
    run(11)
    for b in range(2):
        for h in range(HQ):
            qrot[b, h] = rotated(b, h)
    run(12)

    def attend(b, first):
        window = kvw.at[b, pl.ds(c, REACH + 1)]
        span = (REACH + 1) * BLOCK
        keys = window[:, :, 0:HD].reshape(span, HD)
        values = window[:, :, HD:2 * HD].reshape(span, HD)
        scale = math.log2(math.e) / math.sqrt(HD)
        scores = lax.dot_general(qrot[b, first:first + 2].reshape(2 * BLOCK, HD), keys, (((1,), (1,)), ((), ())),
                                 preferred_element_type=jnp.float32)
        scores = scores.reshape(2, BLOCK, span) * scale + bias[b][None]
        scores = scores.reshape(2 * BLOCK, span)
        peak = jnp.max(scores, axis=1, keepdims=True)
        terms = jnp.exp2(scores - peak)
        total = jnp.sum(terms, axis=1, keepdims=True)
        result = jnp.dot(terms.astype(jnp.bfloat16), values, preferred_element_type=jnp.float32)
        result = (result * (1.0 / total)).astype(jnp.bfloat16)
        for h in range(2):
            columns = slice((first + h) * HD, (first + h + 1) * HD)
            mixed[b * BLOCK:(b + 1) * BLOCK, columns] = result[h * BLOCK:(h + 1) * BLOCK]

    for m in range(0, 5):
        pl.when(k >= m)(lambda m=m: kv_side(0, m, 1 - c).wait_recv())
        kv_side(1, m, 1 - c).wait_recv()
    attend(0, 0)
    for n in range(1, 4):
        run(12 + n)
        attend(n // 2, 2 * (n % 2))


    def out_copy(t):
        zr = ((t + 1) // 2) * (2 * (t % 2) - 1)
        zz = (me.z + zr + NZ) % NZ
        columns = pl.ds(pl.multiple_of(zz * part, part), part)
        return pltpu.make_async_copy(outv.at[:, columns], out_hbm.at[:, columns], out_sem.at[t])

    def emit(t):
        zr = ((t + 1) // 2) * (2 * (t % 2) - 1)
        zz = (me.z + zr + NZ) % NZ
        both(lambda: gw.sib_recv(1, zr), lambda: gw.sib_recv(0, zr))
        for pair in range(NY * NX // 2):
            y, x = pair // 2, (pair % 2) * 2
            weights = jnp.concatenate([wbuf[zz, y, x], wbuf[zz, y, x + 1]], axis=1)
            result = jnp.dot(mixed[...], weights, preferred_element_type=jnp.float32)
            start = pl.multiple_of(zz * part + pair * 2 * BLOCK, 2 * BLOCK)
            outv[:, pl.ds(start, 2 * BLOCK)] = result.astype(jnp.bfloat16)
        out_copy(t).start()

    for n in range(3):
        run(16 + n)
        pl.loop(edges[n + 1] if n else 0, edges[n + 2])(emit)

    def finish(core):
        gk.drain(core)
        gq.drain(core)
        gw.drain(core)

    both(lambda: finish(0), lambda: finish(1))
    for m in range(1, 5):
        kv_copy(early_own, early_own, kv_s, kv_r.at[0, m], me.sibling()).wait_send()
        pl.when(k >= m)(lambda m=m: kv_down(m).wait_send())
    for m in range(0, 5):
        pl.when(k >= m)(lambda m=m: kv_side(0, m, c).wait_send())
        kv_side(1, m, c).wait_send()

    @pl.loop(0, NZ)
    def _(t):
        out_copy(t).wait()


def on_device(hidden_in, segment_ids, w_query, w_key, w_value, w_out):
    seg = segment_ids.reshape(4 * CHIPS, BLOCK)
    rows = hidden_in.shape[0]
    anywhere = pl.BlockSpec(memory_space=pl.ANY)
    dma = pltpu.SemaphoreType.DMA
    bf16, f32 = jnp.bfloat16, jnp.float32
    return pl.pallas_call(
        kernel,
        out_shape=jax.ShapeDtypeStruct((rows, D), bf16),
        in_specs=[anywhere] * 3,
        out_specs=anywhere,
        scratch_shapes=[
            pltpu.VMEM((rows, D), bf16),
            pltpu.VMEM((4 * CHIPS, BLOCK), jnp.int32),
            pltpu.VMEM((NZ, NY, NX, 2, SHARD, 2 * HD), bf16),
            pltpu.VMEM((NZ, NY, NX, 2, SHARD, QW), bf16),
            pltpu.VMEM((NZ, NY, NX, QW, BLOCK), bf16),
            pltpu.VMEM((SHARD, QW), bf16),
            pltpu.VMEM((SHARD, QW), bf16),
            pltpu.VMEM((rows, QKV), f32),
            pltpu.VMEM((2, BLOCK, HD), f32),
            pltpu.VMEM((2, BLOCK, HD), f32),
            pltpu.VMEM((2, BLOCK, (REACH + 1) * BLOCK), f32),
            pltpu.VMEM((2, HQ, BLOCK, HD), bf16),
            pltpu.VMEM((2, REACH + 2, BLOCK, 2 * HD), bf16),
            pltpu.VMEM((rows, QW), bf16),
            pltpu.VMEM((rows, D), bf16),
            dma((5,)), dma((NZ,)), dma, dma,
            dma, dma((40,)), dma((NZ,)),
            dma, dma((40,)), dma((NZ,)),
            dma, dma((40,)), dma((NZ,)),
            dma, dma((2, 5)), dma, dma((2, 5)),
        ],
        compiler_params=pltpu.CompilerParams(
            collective_id=1, has_side_effects=True, vmem_limit_bytes=48 * 2**20),
        name="layer",
    )(hidden_in, seg, jnp.concatenate([w_key, w_value, w_query, w_out.T], axis=1))


def solution(mesh):
    in_specs = (
        P(("dp", "ctx"), None),
        P("dp"),
        P("ctx", None),
        P("ctx", None),
        P("ctx", None),
        P(None, "ctx"),
    )
    out_specs = P(("dp", "ctx"), None)
    return jax.shard_map(
        on_device, mesh=mesh, in_specs=in_specs, out_specs=out_specs, check_vma=False
    )
```
